128 devices in a mesh: gx: 8 (over y, core), gy: 8 (over z, x_lo), gz: 2 (over x_hi).
Axes of the slice: x: 4 (x_hi: 2, x_lo: 2; x = x_hi * 2 + x_lo), y: 4, z: 4, core: 2. Of those that a mesh axis runs over, the one named last changes fastest.
Arguments:
- residual: float32 [64, 256, 1024], P('gz', 'gx', 'gy'), may hold values from -6 to 6
- scale_field: float32 [64, 256, 1024], P('gz', 'gx', 'gy'), may hold values from 0.3 to 3.3
- kappa_sq: float32 [64, 256, 1024], P('gz', 'gx', 'gy'), may hold values from 0.0002 to 0.005
Outputs:
- preconditioned: float32 [64, 256, 1024], P('gz', 'gx', 'gy')
The draws below stay inside these ranges and needn't reach their ends.
All inputs are finite; a program needn't handle non-finite values.
Results may differ from the reference program's by a relative error of at most 0.00002.
Values sent between devices are 32-bit elements; how exact they have to be, the bound alone decides.
No kernel may reach another device: no remote copies, remote signals or barrier semaphores. Data moves between devices by JAX's collectives and lax.ppermute only.
A program may use at most 192 MiB of HBM per device.

```python
import math
import jax
import jax.numpy as jnp

SWEEPS = 12
NX = 256
NY = 1024
NZ = 64


def smooth_part(key):
    phases = jax.random.uniform(key, (4,), jnp.float32, 0.0, 2.0 * math.pi)
    depth_pos = jnp.arange(NZ, dtype=jnp.float32)[:, None, None] / NZ
    east_pos = jnp.arange(NX, dtype=jnp.float32)[None, :, None] / NX
    north_pos = jnp.arange(NY, dtype=jnp.float32)[None, None, :] / NY
    first = jnp.sin(2.0 * math.pi * east_pos + phases[0]) * jnp.cos(2.0 * math.pi * north_pos + phases[1])
    second = jnp.sin(2.0 * math.pi * (east_pos + 2.0 * north_pos) + phases[2]) * jnp.cos(math.pi * depth_pos + phases[3])
    return jnp.broadcast_to(0.5 * (first + second), (NZ, NX, NY))


def draw_residual(key, part):
    key = jax.random.fold_in(key, 11)
    rough_key, smooth_key = jax.random.split(key)
    rough = jnp.clip(jax.random.normal(rough_key, (NZ, NX, NY), jnp.float32), -4.0, 4.0)
    return (rough + smooth_part(smooth_key)).astype(jnp.float32)


def draw_scale_field(key, part):
    key = jax.random.fold_in(key, 23)
    rough_key, smooth_key = jax.random.split(key)
    rough = jnp.exp(jax.random.uniform(rough_key, (NZ, NX, NY), jnp.float32, math.log(0.6), math.log(1.6)))
    return (rough * jnp.exp(0.6 * smooth_part(smooth_key))).astype(jnp.float32)


def block_scale(key, dims, shards, low, largest):
    def one(dim, blocks):
        steps = jax.random.uniform(jax.random.fold_in(jax.random.fold_in(key, 6), dim), (blocks,), jnp.float32, low / len(shards), largest / len(shards))
        return jnp.repeat(jnp.exp(steps), dims[dim] // blocks).reshape((-1,) + (1,) * (len(dims) - dim - 1))

    factor_of = one(*shards[0])
    for cut in shards[1:]:
        factor_of = factor_of * one(*cut)
    return factor_of


def setup_inputs(seed: int = 0) -> dict:
    seeds = jax.random.split(jax.random.key(seed), 4)
    return {
        "residual": draw_residual(jax.random.fold_in(seeds[3], 71), 0),
        "scale_field": draw_scale_field(jax.random.fold_in(seeds[3], 71), 0),
        "kappa_sq": jnp.clip(jnp.exp(math.log(0.005) - 3.218876 * jax.random.uniform(seeds[2], (NZ, NX, NY), jnp.float32) ** block_scale(seeds[2], (NZ, NX, NY), ((0, 2), (1, 8), (2, 8)), -0.2, 0.2)), 0.0002, 0.005),
    }


OMEGA = 0.8
VERTICAL = 0.25


def level_weights(level):
    w_horiz = 0.25 ** level
    return VERTICAL * w_horiz, w_horiz


def laplace_terms(padded, w_vert, w_horiz):
    centre = padded[1:-1, 1:-1, 1:-1]
    total = w_vert * (2.0 * centre - padded[2:, 1:-1, 1:-1] - padded[:-2, 1:-1, 1:-1])
    total = total + w_horiz * (2.0 * centre - padded[1:-1, 2:, 1:-1] - padded[1:-1, :-2, 1:-1])
    return total + w_horiz * (2.0 * centre - padded[1:-1, 1:-1, 2:] - padded[1:-1, 1:-1, :-2])


def operate(iterate, scale, kappa, w_vert, w_horiz):
    return kappa * iterate + scale * laplace_terms(jnp.pad(scale * iterate, 1), w_vert, w_horiz)


def coarsen(field):
    depth, width, length = field.shape
    return jnp.mean(field.reshape(depth // 2, 2, width // 2, 2, length // 2, 2), axis=(1, 3, 5))


def refine(field):
    return jnp.repeat(jnp.repeat(jnp.repeat(field, 2, 0), 2, 1), 2, 2)


def vcycle(source, scale, kappa, level):
    w_vert, w_horiz = level_weights(level)
    diagonal = kappa + 2.0 * scale * scale * (w_vert + 2.0 * w_horiz)
    iterate = OMEGA * source / diagonal
    if level == 4:
        for step in range(SWEEPS - 1):
            iterate = iterate + OMEGA * (source - operate(iterate, scale, kappa, w_vert, w_horiz)) / diagonal
        return iterate
    iterate = iterate + OMEGA * (source - operate(iterate, scale, kappa, w_vert, w_horiz)) / diagonal
    error_term = source - operate(iterate, scale, kappa, w_vert, w_horiz)
    iterate = iterate + refine(vcycle(coarsen(error_term), coarsen(scale), coarsen(kappa), level + 1))
    for step in range(2):
        iterate = iterate + OMEGA * (source - operate(iterate, scale, kappa, w_vert, w_horiz)) / diagonal
    return iterate


def reference(residual, scale_field, kappa_sq):
    return vcycle(residual, scale_field, kappa_sq, 0)
```

```python
import jax
import jax.numpy as jnp
from jax import lax
from jax.experimental import pallas as pl
from jax.experimental.pallas import tpu as pltpu
from jax.sharding import PartitionSpec as P

F32 = jnp.float32
VM = pl.BlockSpec(memory_space=pltpu.VMEM)
HI = lax.Precision.HIGHEST
COARSE_SWEEPS = 11


def run(body, args, outs, scratch=(), limit=48 << 20):
    return pl.pallas_call(
        body,
        out_shape=[jax.ShapeDtypeStruct(o, F32) for o in outs],
        in_specs=[VM] * len(args),
        out_specs=[VM] * len(outs),
        scratch_shapes=[pltpu.VMEM(s, F32) for s in scratch],
        compiler_params=pltpu.CompilerParams(vmem_limit_bytes=limit),
    )(*args)


def weights(level):
    wh = 0.25**level
    return wh, 2.0 * (0.25 * wh + 2.0 * wh)


def iota(shape, dim):
    return lax.broadcasted_iota(jnp.int32, shape, dim)


def lanes(v, shift):
    return pltpu.roll(v, shift % v.shape[-1], v.ndim - 1)


def rows(v, shift):
    return pltpu.roll(v, shift % v.shape[-2], v.ndim - 2)


def beside(v):
    return (rows(v, 1) + rows(v, -1)) + (lanes(v, 1) + lanes(v, -1))


def around(above, v, below):
    return 0.25 * (above + below) + beside(v)


def coefficients(f, s, k, level):
    wh, full = weights(level)
    diagonal = k + full * (s * s)
    sw = s * (0.8 / jnp.where(diagonal > 0.0, diagonal, 1.0))
    return sw * f, (wh * s) * sw


def dot(a, b):
    return jnp.dot(a, b, precision=HI, preferred_element_type=F32)


def dot3(a, b):
    n, r, c = a.shape
    return dot(a.reshape(n * r, c), b).reshape(n, r, b.shape[1])


def select_matrix(shape, source_of, scale=1.0):
    i, o = iota(shape, 0), iota(shape, 1)
    return jnp.where(source_of(i, o), scale, 0.0).astype(F32)


def k_face_z(f, s, k, g, c, zmsg):
    iz = lax.axis_index("gz")

    def one(z, _):
        gz, cz = coefficients(f[z], s[z], k[z], 0)
        g[z] = gz
        c[z] = cz
        return 0

    lax.fori_loop(0, 32, one, 0, unroll=4)
    for d in range(3):
        z = jnp.where(iz == 0, 31 - d, d)
        zmsg[d] = g[z]
        if d < 2:
            zmsg[3 + d] = c[z]
            zmsg[5 + d] = s[z]


def k_coarse_coeff(s, k, sk1, ps, pk):
    def one(z, _):
        ps[z] = s[2 * z] + s[2 * z + 1]
        pk[z] = k[2 * z] + k[2 * z + 1]
        return 0

    lax.fori_loop(0, 16, one, 0, unroll=4)
    a = ps[:, pl.ds(0, 16, 2), :] + ps[:, pl.ds(1, 16, 2), :]
    b = pk[:, pl.ds(0, 16, 2), :] + pk[:, pl.ds(1, 16, 2), :]
    left = select_matrix((128, 128), lambda i, o: i // 2 == o, 0.125)
    right = select_matrix((128, 128), lambda i, o: i // 2 == o - 64, 0.125)
    sk1[...] = dot3(a, left) + dot3(b, right)


def halo_rows(zr, iz, field, z):
    first, depth = ((0, 3), (3, 2), (5, 2))[field]
    d = z - 35 if z > 34 else 2 - z
    if d >= depth:
        return jnp.zeros(zr.shape[1:], F32)
    return jnp.where(iz == (0 if z > 34 else 1), zr[first + d], 0.0)


def k_face_x(g, c, s, zr, to_right, to_left):
    iz = lax.axis_index("gz")
    sub = iota((8, 128), 0)

    def put(z, gz, cz, sz):
        a, b, d = gz[24:32], cz[24:32], sz[24:32]
        to_right[z] = jnp.where(sub >= 5, a, jnp.where(sub >= 3, rows(b, -3), rows(d, -5)))
        a, b, d = gz[0:8], cz[0:8], sz[0:8]
        to_left[z] = jnp.where(sub < 3, a, jnp.where(sub < 5, rows(b, 3), rows(d, 5)))

    def one(z, _):
        put(z + 3, g[z], c[z], s[z])
        return 0

    lax.fori_loop(0, 32, one, 0, unroll=4)
    for z in (0, 1, 2, 35, 36, 37):
        put(z, *[halo_rows(zr, iz, n, z) for n in range(3)])


def k_face_y(g, c, s, zr, from_left, from_right, gm, cm, sm, ymsg):
    ix, iz = lax.axis_index("gx"), lax.axis_index("gz")
    sub = iota((8, 128), 0)

    def sides(z):
        lf = jnp.where(ix > 0, from_left[z], 0.0)
        rt = jnp.where(ix < 7, from_right[z], 0.0)
        return (
            jnp.where(sub >= 4, lf, rt),
            jnp.where(sub >= 4, rows(lf, 3), rows(rt, -3)),
            jnp.where(sub >= 4, rows(lf, 5), rows(rt, -5)),
        )

    def put(z, values):
        for ref, own, side in zip((gm, cm, sm), values, sides(z)):
            ref[z] = jnp.concatenate([own, side], axis=0)

    def one(z, _):
        put(z + 3, (g[z], c[z], s[z]))
        return 0

    lax.fori_loop(0, 32, one, 0, unroll=4)
    for z in (0, 1, 2, 35, 36, 37):
        put(z, [halo_rows(zr, iz, n, z) for n in range(3)])
    for z in (38, 39):
        for ref in (gm, cm, sm):
            ref[z] = jnp.zeros((40, 128), F32)
    lane = iota((40, 128), 1)

    def pack(group, _):
        total = jnp.zeros((40, 128), F32)
        for j in range(8):
            z = group * 8 + j
            slot = lane - 16 * j
            total = jnp.where(slot >= 0, lanes(gm[z], 16 * j + 3), total)
            total = jnp.where(slot >= 6, lanes(cm[z], 16 * j + 8), total)
            total = jnp.where(slot >= 10, lanes(sm[z], 16 * j + 12), total)
        ymsg[group] = total
        return 0

    lax.fori_loop(0, 5, pack, 0)


def k_down0(f, gm, cm, sm, from_left, from_right, gs, cs, ss, q, f1, e):
    iy = lax.axis_index("gy")
    lane = iota((40, 128), 1) % 16
    left = (lane < 3) | ((lane >= 6) & (lane < 8)) | ((lane >= 10) & (lane < 12))

    def unpack(group, _):
        both = jnp.where(
            left,
            jnp.where(iy > 0, from_left[group], 0.0),
            jnp.where(iy < 7, from_right[group], 0.0),
        )
        for j in range(8):
            z = group * 8 + j
            gs[z] = lanes(both, -16 * j - 3)
            cs[z] = lanes(both, -16 * j - 8)
            ss[z] = lanes(both, -16 * j - 12)
        return 0

    lax.fori_loop(0, 5, unpack, 0)

    def wide(a, b, z):
        return jnp.concatenate([a[z], b[z]], axis=1)

    def relax(z, _):
        v = wide(gm, gs, z)
        n = around(wide(gm, gs, z - 1), v, wide(gm, gs, z + 1))
        q[z] = 0.4 * v + wide(cm, cs, z) * n
        return 0

    lax.fori_loop(1, 37, relax, 0, unroll=2)

    def residual(z):
        n = around(q[z - 1], q[z], q[z + 1])[:32, :128]
        return 0.04 * f[z - 3] + sm[z, :32, :] * n

    def pair(z, _):
        e[z] = residual(2 * z + 3) + residual(2 * z + 4)
        return 0

    lax.fori_loop(0, 16, pair, 0)
    a = e[:, pl.ds(0, 16, 2), :] + e[:, pl.ds(1, 16, 2), :]
    lo = select_matrix((128, 128), lambda i, o: i // 2 == o, 0.125)
    hi = select_matrix((128, 128), lambda i, o: i // 2 == o - 64, 0.125)
    f1[...] = dot3(a[:8], lo) + dot3(a[8:], hi)


def k_spread1(own, xl, xr, s1, k1, f1, to_right, to_left):
    ix, iz = lax.axis_index("gx"), lax.axis_index("gz")
    sub = iota((8, 128), 0)
    lane = iota((40, 128), 1)

    def join(mid, lf, rt):
        lf = jnp.where(ix > 0, lf, 0.0)
        rt = jnp.where(ix < 7, rt, 0.0)
        return jnp.concatenate(
            [mid, rt[0:8], jnp.where(sub < 4, rt[8:16], lf[0:8]), lf[8:16]], axis=0
        )

    for half in range(2):
        base = jnp.where(iz == half, 0, 24)

        def one(z, _, half=half, base=base):
            sk = join(own[base + z], xl[base + z], xr[base + z])
            s1[half * 16 + z] = sk
            k1[half * 16 + z] = lanes(sk, 64)
            return 0

        lax.fori_loop(0, 16, one, 0, unroll=2)

        def two(z, _, half=half, base=base):
            ff = join(own[base + 16 + z], xl[base + 16 + z], xr[base + 16 + z])
            f1[half * 16 + z] = ff
            f1[half * 16 + 8 + z] = lanes(ff, 64)
            return 0

        lax.fori_loop(0, 8, two, 0, unroll=2)

    def pack(group, _):
        for n, ref in enumerate((s1, k1, f1)):
            a = jnp.zeros((40, 128), F32)
            b = jnp.zeros((40, 128), F32)
            for j in range(8):
                v = ref[group * 8 + j]
                a = jnp.where(lane >= 16 * j, lanes(v, 16 * j - 52), a)
                b = jnp.where(lane >= 16 * j, lanes(v, 16 * j), b)
            to_right[4 * n + group] = a
            to_left[4 * n + group] = b
        return 0

    lax.fori_loop(0, 4, pack, 0)


def k_down12(s1, k1, f1, fl, fr, g, c, s, q, g2, c2, s2, q2, chunk, f, e, fs, fk, x2, e2):
    iy = lax.axis_index("gy")
    lane = iota((40, 128), 1)
    for ref in (g, q):
        ref[0] = jnp.zeros((40, 128), F32)
        ref[33] = jnp.zeros((40, 128), F32)

    def unpack(group, _):
        lf = [jnp.where(iy > 0, fl[4 * n + group], 0.0) for n in range(3)]
        rt = [jnp.where(iy < 7, fr[4 * n + group], 0.0) for n in range(3)]
        for j in range(8):
            z = group * 8 + j
            sv, kv, fv = [
                jnp.where(
                    lane < 64,
                    ref[z],
                    jnp.where(lane < 96, lanes(rt[n], 64 - 16 * j), lanes(lf[n], 116 - 16 * j)),
                )
                for n, ref in enumerate((s1, k1, f1))
            ]
            gv, cv = coefficients(fv, sv, kv, 1)
            g[z + 1] = gv
            c[z + 1] = cv
            s[z + 1] = sv
            f[z] = fv
            fk[z] = kv
        return 0

    lax.fori_loop(0, 4, unpack, 0)

    def relax(z, _):
        q[z] = 0.4 * g[z] + c[z] * around(g[z - 1], g[z], g[z + 1])
        return 0

    lax.fori_loop(1, 33, relax, 0, unroll=2)
    wh, _ = weights(1)

    def residual(z):
        return 0.04 * f[z - 1] + (wh * s[z]) * around(q[z - 1], q[z], q[z + 1])

    def pair(z, _):
        e[z] = residual(2 * z + 1) + residual(2 * z + 2)
        fs[z] = s[2 * z + 1] + s[2 * z + 2]
        e[z + 16] = fk[2 * z] + fk[2 * z + 1]
        return 0

    lax.fori_loop(0, 16, pair, 0, unroll=2)
    down = select_matrix(
        (128, 128),
        lambda i, o: ((i // 2 == o) & (o < 38)) | ((i // 2 == o - 64) & (o >= 122)),
        0.125,
    )

    def coarse(ref, first):
        x2[:, 14:18, :] = jnp.zeros((16, 4, 128), F32)
        at = pl.ds(first, 16)
        x2[:, 0:14, :] = ref[at, pl.ds(0, 14, 2), :] + ref[at, pl.ds(1, 14, 2), :]
        x2[:, 18:24, :] = ref[at, pl.ds(28, 6, 2), :] + ref[at, pl.ds(29, 6, 2), :]
        return dot3(x2[...], down)

    fv = coarse(e, 0)
    sv = coarse(fs, 0)
    kv = coarse(e, 16)
    gv, cv = coefficients(fv, sv, kv, 2)
    zero = jnp.zeros((1, 24, 128), F32)

    def tall(v):
        return jnp.concatenate([zero, v, zero], axis=0)

    def spread(v):
        w = tall(v)
        return around(w[:16], v, w[2:])

    qv = 0.4 * gv + cv * spread(gv)
    wh, _ = weights(2)
    ev = 0.04 * fv + (wh * sv) * spread(qv)
    g2[...] = gv
    c2[...] = cv
    s2[...] = sv
    q2[...] = qv
    half = select_matrix((128, 128), lambda i, o: (i // 2 == o) & (o < 16), 0.125)
    parts = []
    for v in (ev, sv, kv):
        v = v.reshape(8, 2, 24, 128)
        e2[...] = v[:, 0, :8, :] + v[:, 1, :8, :]
        pairs = e2[:, pl.ds(0, 4, 2), :] + e2[:, pl.ds(1, 4, 2), :]
        total = jnp.zeros((4, 128), F32)
        for j in range(8):
            piece = dot(pairs[j], half)
            total = total + (lanes(piece, 16 * j) if j else piece)
        parts.append(total)
    parts.append(jnp.zeros((4, 128), F32))
    block = pltpu.roll(jnp.concatenate(parts, axis=0), 16 * iy, 1)

    def copy(n, _):
        chunk[n] = block
        return 0

    lax.fori_loop(0, 64, copy, 0, unroll=8)


def k_up(
    gathered, g2, c2, s2, q2, g1, c1, s1, q1, gm, cm, sm, gs, cs, ss, q0,
    out, t3, x4, p3, p2, p1, va, vb, p0, wa, wb, y0,
):
    ix, iy, iz = lax.axis_index("gx"), lax.axis_index("gy"), lax.axis_index("gz")
    lane = iota((8, 128), 1) // 16
    sub = iota((8, 128), 0)
    for j in range(8):
        for t in range(2):
            tiles = []
            for x in range(8):
                v = gathered[x * 8, 8 * t : 8 * t + 8, :]
                for y in range(1, 8):
                    v = jnp.where(lane == (j + y) % 8, gathered[x * 8 + y, 8 * t : 8 * t + 8, :], v)
                tiles.append(lanes(v, -16 * j) if j else v)
            for x in range(4):
                a, b = tiles[2 * x], tiles[2 * x + 1]
                t3[2 * t, j, 8 * x : 8 * x + 8, :] = jnp.where(sub < 4, a, rows(b, 4))
                if t == 0:
                    t3[1, j, 8 * x : 8 * x + 8, :] = jnp.where(sub < 4, rows(a, 4), b)
    f3, s3, k3 = t3[0], t3[1], t3[2]

    def spread_in(shape, last):
        n, r, _ = shape
        row, col = iota(shape, 1), iota(shape, 2)
        zero = jnp.zeros((1,) + shape[1:], F32)

        def apply(v):
            w = jnp.concatenate([zero, v, zero], axis=0)
            x = jnp.where(row > 0, rows(v, 1), 0.0) + jnp.where(row < r - 1, rows(v, -1), 0.0)
            y = jnp.where(col > 0, lanes(v, 1), 0.0) + jnp.where(col < last, lanes(v, -1), 0.0)
            return 0.25 * (w[:n] + w[2:]) + x + y

        return apply

    near3 = spread_in((8, 32, 128), 127)
    g3, c3 = coefficients(f3, s3, k3, 3)
    q3 = 0.4 * g3 + c3 * near3(g3)
    e3 = 0.04 * f3 + (weights(3)[0] * s3) * near3(q3)
    half = select_matrix((128, 128), lambda i, o: i // 2 == o, 0.125)
    fields = []
    for v in (e3, s3, k3):
        w = v.reshape(4, 2, 32, 128)
        x4[...] = w[:, 0] + w[:, 1]
        fields.append(dot3(x4[:, pl.ds(0, 16, 2), :] + x4[:, pl.ds(1, 16, 2), :], half))
    f4, s4, k4 = fields
    near4 = spread_in((4, 16, 128), 63)
    g4, c4 = coefficients(f4, s4, k4, 4)
    v4 = g4
    for _ in range(COARSE_SWEEPS):
        v4 = (0.2 * v4 + g4) + c4 * near4(v4)
    u4 = jnp.where(s4 > 0.0, v4 / jnp.where(s4 > 0.0, s4, 1.0), 0.0)
    u4 = dot3(u4, select_matrix((128, 128), lambda i, o: i == o // 2))
    p3[:, pl.ds(0, 16, 2), :] = u4
    p3[:, pl.ds(1, 16, 2), :] = u4
    w = p3[...]
    w = jnp.broadcast_to(w[:, None], (4, 2, 32, 128)).reshape(8, 32, 128)
    v3 = (q3 + 0.8 * g3) + s3 * w
    for _ in range(2):
        v3 = (0.2 * v3 + g3) + c3 * near3(v3)
    u3 = v3 / s3
    pick = select_matrix(
        (128, 128),
        lambda i, o: i == (jnp.where(o < 64, o // 2, 127 - (127 - o) // 2) + 16 * iy) % 128,
    )
    u3 = pltpu.roll(dot3(u3, pick), (32 - 4 * ix) % 32, 1)
    p2[:, 14:18, :] = jnp.zeros((8, 4, 128), F32)
    for n in range(2):
        p2[:, pl.ds(n, 7, 2), :] = u3[:, 0:7, :]
        p2[:, pl.ds(18 + n, 3, 2), :] = u3[:, 29:32, :]
    w = p2[...]
    w = jnp.broadcast_to(w[:, None], (8, 2, 24, 128)).reshape(16, 24, 128)
    gv, cv, sv = g2[...], c2[...], s2[...]
    zero = jnp.zeros((1, 24, 128), F32)
    v = (q2[...] + 0.8 * gv) + sv * w
    for _ in range(2):
        w = jnp.concatenate([zero, v, zero], axis=0)
        v = (0.2 * v + gv) + cv * around(w[:16], v, w[2:])
    u2 = jnp.where(sv > 0.0, v / jnp.where(sv > 0.0, sv, 1.0), 0.0)
    u2 = dot3(
        u2,
        select_matrix(
            (128, 128),
            lambda i, o: i == jnp.where(o < 96, o // 2, 127 - (127 - o) // 2),
        ),
    )
    for n in range(2):
        p1[:, pl.ds(n, 14, 2), :] = u2[:, 0:14, :]
        p1[:, pl.ds(28 + n, 6, 2), :] = u2[:, 18:24, :]
    for ref in (va, vb):
        ref[0] = jnp.zeros((40, 128), F32)
        ref[33] = jnp.zeros((40, 128), F32)

    def start1(z, _):
        va[z] = (q1[z] + 0.8 * g1[z]) + s1[z] * p1[(z - 1) // 2]
        return 0

    lax.fori_loop(1, 33, start1, 0, unroll=2)

    def sweep1(z, _):
        vb[z] = (0.2 * va[z] + g1[z]) + c1[z] * around(va[z - 1], va[z], va[z + 1])
        return 0

    lax.fori_loop(1, 33, sweep1, 0, unroll=2)

    def last1(z, _):
        v = (0.2 * vb[z] + g1[z]) + c1[z] * around(vb[z - 1], vb[z], vb[z + 1])
        sv = s1[z]
        va[z] = jnp.where(sv > 0.0, v / jnp.where(sv > 0.0, sv, 1.0), 0.0)
        return 0

    lax.fori_loop(1, 33, last1, 0, unroll=2)
    pick = select_matrix(
        (128, 256),
        lambda i, o: i == jnp.where(o < 192, o // 2, 127 - (255 - o) // 2),
    )
    y0[...] = dot3(va[pl.ds(16 * iz, 18)], pick)

    def twice(t, _):
        v = y0[t]
        for h in range(2):
            for n in range(2):
                p0[h, t, pl.ds(n, 18, 2), :] = v[0:18, 128 * h : 128 * h + 128]
                p0[h, t, pl.ds(36 + n, 2, 2), :] = v[38:40, 128 * h : 128 * h + 128]
        return 0

    lax.fori_loop(0, 18, twice, 0)

    def wide(a, b, z):
        return jnp.concatenate([a[z], b[z]], axis=1)

    def start0(z, _):
        wa[z] = (q0[z] + 0.8 * wide(gm, gs, z)) + wide(sm, ss, z) * wide(p0.at[0], p0.at[1], (z - 1) // 2)
        return 0

    lax.fori_loop(1, 37, start0, 0, unroll=2)

    def sweep0(z, _):
        n = around(wa[z - 1], wa[z], wa[z + 1])
        wb[z] = (0.2 * wa[z] + wide(gm, gs, z)) + wide(cm, cs, z) * n
        return 0

    lax.fori_loop(2, 36, sweep0, 0, unroll=2)

    def last0(z, _):
        n = around(wb[z - 1], wb[z], wb[z + 1])[:32, :128]
        v = (0.2 * wb[z, :32, :128] + gm[z, :32, :]) + cm[z, :32, :] * n
        out[z - 3] = v / sm[z, :32, :]
        return 0

    lax.fori_loop(3, 35, last0, 0, unroll=2)


def ring(v, axis, step):
    n = lax.axis_size(axis)
    return lax.ppermute(v, axis, [(i, (i + step) % n) for i in range(n)])


def shards(f, s, k):
    g, c, zmsg = run(k_face_z, (f, s, k), [(32, 32, 128), (32, 32, 128), (7, 32, 128)])
    zr = ring(zmsg, "gz", 1)
    (sk1,) = run(k_coarse_coeff, (s, k), [(16, 16, 128)], [(16, 32, 128)] * 2)
    to_right, to_left = run(k_face_x, (g, c, s, zr), [(38, 8, 128)] * 2)
    from_left, from_right = ring(to_right, "gx", 1), ring(to_left, "gx", -1)
    gm, cm, sm, ymsg = run(
        k_face_y, (g, c, s, zr, from_left, from_right), [(40, 40, 128)] * 3 + [(5, 40, 128)]
    )
    from_left, from_right = ring(ymsg, "gy", 1), ring(ymsg, "gy", -1)
    gs, cs, ss, q0, f1 = run(
        k_down0,
        (f, gm, cm, sm, from_left, from_right),
        [(40, 40, 128)] * 3 + [(38, 40, 256), (8, 16, 128)],
        [(16, 32, 128)],
    )
    own = jnp.concatenate([sk1, f1], axis=0)
    own = jnp.concatenate([own, ring(own, "gz", 1)], axis=0)
    xl, xr = ring(own, "gx", 1), ring(own, "gx", -1)
    s1, k1, f1, to_right, to_left = run(
        k_spread1, (own, xl, xr), [(32, 40, 128)] * 3 + [(12, 40, 128)] * 2
    )
    from_left, from_right = ring(to_right, "gy", 1), ring(to_left, "gy", -1)
    g1, c1, s1, q1, g2, c2, s2, q2, chunk = run(
        k_down12,
        (s1, k1, f1, from_left, from_right),
        [(34, 40, 128)] * 4 + [(16, 24, 128)] * 4 + [(64, 16, 128)],
        [(32, 40, 128), (32, 40, 128), (16, 40, 128), (32, 40, 128), (16, 24, 128), (8, 8, 128)],
    )
    gathered = lax.all_to_all(chunk, ("gx", "gy"), 0, 0, tiled=True)
    (out,) = run(
        k_up,
        (gathered, g2, c2, s2, q2, g1, c1, s1, q1, gm, cm, sm, gs, cs, ss, q0),
        [(32, 32, 128)],
        [
            (3, 8, 32, 128),
            (4, 32, 128),
            (4, 32, 128),
            (8, 24, 128),
            (16, 40, 128),
            (34, 40, 128),
            (34, 40, 128),
            (2, 18, 40, 128),
            (38, 40, 256),
            (38, 40, 256),
            (18, 40, 256),
        ],
    )
    return out


def solution(mesh):
    return jax.shard_map(
        shards,
        mesh=mesh,
        in_specs=(P("gz", "gx", "gy"),) * 3,
        out_specs=P("gz", "gx", "gy"),
        check_vma=False,
    )
```

```python
import math

import jax
import jax.numpy as jnp
from jax import lax
from jax.experimental import pallas as pl
from jax.experimental.pallas import tpu as pltpu
from jax.sharding import PartitionSpec as P

F32 = jnp.float32
VM = pl.BlockSpec(memory_space=pltpu.VMEM)
ANY = pl.BlockSpec(memory_space=pl.ANY)
HI = lax.Precision.HIGHEST
COARSE_SWEEPS = 11


def run(body, args, outs, scratch=(), spec=VM, sems=()):
    words = sum(math.prod(s) for s in (*outs, *scratch))
    words += sum(a.size for a in args) if spec is VM else 0
    return pl.pallas_call(
        body,
        out_shape=[jax.ShapeDtypeStruct(o, F32) for o in outs],
        in_specs=[spec] * len(args),
        out_specs=[VM] * len(outs),
        scratch_shapes=[pltpu.VMEM(s, F32) for s in scratch]
        + [pltpu.SemaphoreType.DMA(n) for n in sems],
        compiler_params=pltpu.CompilerParams(vmem_limit_bytes=6 * words + (6 << 20)),
    )(*args)


def weights(level):
    wh = 0.25**level
    return wh, 2.0 * (0.25 * wh + 2.0 * wh)


def iota(shape, dim):
    return lax.broadcasted_iota(jnp.int32, shape, dim)


def lanes(v, shift):
    return pltpu.roll(v, shift % v.shape[-1], v.ndim - 1)


def rows(v, shift):
    return pltpu.roll(v, shift % v.shape[-2], v.ndim - 2)


def beside(v):
    return (rows(v, 1) + rows(v, -1)) + (lanes(v, 1) + lanes(v, -1))


def around(above, v, below):
    return 0.25 * (above + below) + beside(v)


def factors(s, k, level):
    wh, full = weights(level)
    diagonal = k + full * (s * s)
    sw = s * (0.8 / jnp.where(diagonal > 0.0, diagonal, 1.0))
    return sw, (wh * s) * sw


def unscale(v, s):
    inside = s > 0.0
    return jnp.where(inside, v / jnp.where(inside, s, 1.0), 0.0)


def dot(a, b):
    return jnp.dot(a, b, precision=HI, preferred_element_type=F32)


def dot3(a, b):
    n, r, c = a.shape
    return dot(a.reshape(n * r, c), b).reshape(n, r, b.shape[1])


def select_matrix(shape, source_of, scale=1.0):
    i, o = iota(shape, 0), iota(shape, 1)
    return jnp.where(source_of(i, o), scale, 0.0).astype(F32)


def k_face_z(f, s, k, zmsg, buf, sem):
    iz = lax.axis_index("gz")
    first = jnp.where(iz == 0, 29, 0)
    copies = [
        pltpu.make_async_copy(ref.at[pl.ds(first, 3)], buf.at[n], sem.at[n])
        for n, ref in enumerate((f, s, k))
    ]
    for copy in copies:
        copy.start()
    for copy in copies:
        copy.wait()
    for d in range(3):
        z = jnp.where(iz == 0, 2 - d, d)
        sv = buf[1, z]
        sw, c = factors(sv, buf[2, z], 0)
        zmsg[d] = sw * buf[0, z]
        if d < 2:
            zmsg[3 + d] = c
            zmsg[5 + d] = sv


def k_load(f, s, k, fv, sv, kv, g, c, sem):
    copies = [
        [
            pltpu.make_async_copy(
                ref.at[pl.ds(8 * b, 8)], dst.at[pl.ds(8 * b, 8)], sem.at[3 * b + n]
            )
            for n, (ref, dst) in enumerate(((f, fv), (s, sv), (k, kv)))
        ]
        for b in range(4)
    ]
    for block in copies:
        for copy in block:
            copy.start()
    for b in range(4):
        for copy in copies[b]:
            copy.wait()

        def one(z, _):
            sw, cz = factors(sv[z], kv[z], 0)
            g[z] = sw * fv[z]
            c[z] = cz
            return 0

        lax.fori_loop(8 * b, 8 * b + 8, one, 0, unroll=4)


def k_coarse_coeff(s, k, sk1, ps, pk):
    def one(z, _):
        ps[z] = s[2 * z] + s[2 * z + 1]
        pk[z] = k[2 * z] + k[2 * z + 1]
        return 0

    lax.fori_loop(0, 16, one, 0, unroll=4)
    a = ps[:, pl.ds(0, 16, 2), :] + ps[:, pl.ds(1, 16, 2), :]
    b = pk[:, pl.ds(0, 16, 2), :] + pk[:, pl.ds(1, 16, 2), :]
    left = select_matrix((128, 128), lambda i, o: i // 2 == o, 0.125)
    right = select_matrix((128, 128), lambda i, o: i // 2 == o - 64, 0.125)
    sk1[...] = dot3(a, left) + dot3(b, right)


def halo_rows(zr, iz, field, z):
    first, depth = ((0, 3), (3, 2), (5, 2))[field]
    d = z - 35 if z > 34 else 2 - z
    if d >= depth:
        return jnp.zeros(zr.shape[1:], F32)
    return jnp.where(iz == (0 if z > 34 else 1), zr[first + d], 0.0)


def k_face_x(g, c, s, zr, to_right, to_left):
    iz = lax.axis_index("gz")
    sub = iota((8, 128), 0)

    def put(z, gz, cz, sz):
        a, b, d = gz[24:32], cz[24:32], sz[24:32]
        to_right[z] = jnp.where(sub >= 5, a, jnp.where(sub >= 3, rows(b, -3), rows(d, -5)))
        a, b, d = gz[0:8], cz[0:8], sz[0:8]
        to_left[z] = jnp.where(sub < 3, a, jnp.where(sub < 5, rows(b, 3), rows(d, 5)))

    def one(z, _):
        put(z + 3, g[z], c[z], s[z])
        return 0

    lax.fori_loop(0, 32, one, 0, unroll=4)
    for z in (0, 1, 2, 35, 36, 37):
        put(z, *[halo_rows(zr, iz, n, z) for n in range(3)])


def k_face_y(g, c, s, zr, from_left, from_right, gm, cm, sm, ymsg):
    ix, iz = lax.axis_index("gx"), lax.axis_index("gz")
    sub = iota((8, 128), 0)

    def sides(z):
        lf = jnp.where(ix > 0, from_left[z], 0.0)
        rt = jnp.where(ix < 7, from_right[z], 0.0)
        return (
            jnp.where(sub >= 4, lf, rt),
            jnp.where(sub >= 4, rows(lf, 3), rows(rt, -3)),
            jnp.where(sub >= 4, rows(lf, 5), rows(rt, -5)),
        )

    def put(z, values):
        for ref, own, side in zip((gm, cm, sm), values, sides(z)):
            ref[z] = jnp.concatenate([own, side], axis=0)

    def one(z, _):
        put(z + 3, (g[z], c[z], s[z]))
        return 0

    lax.fori_loop(0, 32, one, 0, unroll=4)
    for z in (0, 1, 2, 35, 36, 37):
        put(z, [halo_rows(zr, iz, n, z) for n in range(3)])
    for z in (38, 39):
        for ref in (gm, cm, sm):
            ref[z] = jnp.zeros((40, 128), F32)
    lane = iota((40, 128), 1)

    def pack(group, _):
        total = jnp.zeros((40, 128), F32)
        for j in range(8):
            z = group * 8 + j
            slot = lane - 16 * j
            total = jnp.where(slot >= 0, lanes(gm[z], 16 * j + 3), total)
            total = jnp.where(slot >= 6, lanes(cm[z], 16 * j + 8), total)
            total = jnp.where(slot >= 10, lanes(sm[z], 16 * j + 12), total)
        ymsg[group] = total
        return 0

    lax.fori_loop(0, 5, pack, 0)


def near_edges(v):
    lane = iota(v.shape, 2)
    zero = jnp.zeros((1,) + v.shape[1:], F32)
    up, down = lanes(v, 16), lanes(v, -16)
    above = jnp.where(lane < 16, jnp.concatenate([zero, up[:-1]], axis=0), up)
    below = jnp.where(lane >= 112, jnp.concatenate([down[1:], zero], axis=0), down)
    return around(above, v, below)


def joint(v):
    return jnp.where(iota(v.shape, 2) % 16 == 4, lanes(v, -6), v)


def near_main(ref, edge, z):
    v = ref[z]
    lane = iota(v.shape, 1)
    e = pltpu.roll(edge[z // 8], (124 - 16 * (z % 8)) % 128, 1)
    across = jnp.where(lane == 0, e, lanes(v, 1)) + jnp.where(lane == 127, e, lanes(v, -1))
    return 0.25 * (ref[z - 1] + ref[z + 1]) + ((rows(v, 1) + rows(v, -1)) + across)


def k_down0(f, gm, cm, sm, own, from_left, from_right, gw, cw, sw, q, qw, f1, e, eg, eq):
    iy = lax.axis_index("gy")
    lane = iota((5, 40, 128), 2) % 16
    mid = own[...]
    lf = jnp.where(iy > 0, from_left[...], 0.0)
    rt = jnp.where(iy < 7, from_right[...], 0.0)

    def window(split, to_right, to_left):
        a = jnp.where(lane < split, mid, rt)
        b = jnp.where(lane < split, lf, mid)
        a = lanes(a, to_right) if to_right else a
        return jnp.where(lane < 8, a, lanes(b, to_left))

    g = window(3, 0, 8)
    c = window(8, -5, 3)
    gw[...] = g
    cw[...] = c
    sw[...] = window(12, -9, -1)
    w = 0.4 * g + c * near_edges(g)
    qw[...] = w
    eg[...] = joint(g)
    eq[...] = joint(w)
    q[0] = jnp.zeros((40, 128), F32)
    q[37] = jnp.zeros((40, 128), F32)

    def relax(z, _):
        q[z] = 0.4 * gm[z] + cm[z] * near_main(gm, eg, z)
        return 0

    lax.fori_loop(1, 37, relax, 0, unroll=2)

    def residual(z):
        return 0.04 * f[z - 3] + sm[z, :32, :] * near_main(q, eq, z)[:32]

    def pair(z, _):
        e[z] = residual(2 * z + 3) + residual(2 * z + 4)
        return 0

    lax.fori_loop(0, 16, pair, 0)
    a = e[:, pl.ds(0, 16, 2), :] + e[:, pl.ds(1, 16, 2), :]
    lo = select_matrix((128, 128), lambda i, o: i // 2 == o, 0.125)
    hi = select_matrix((128, 128), lambda i, o: i // 2 == o - 64, 0.125)
    f1[...] = dot3(a[:8], lo) + dot3(a[8:], hi)


def k_spread(own, xl, xr, full, to_right, to_left):
    ix, iz = lax.axis_index("gx"), lax.axis_index("gz")
    sub = iota((8, 128), 0)
    lane = iota((40, 128), 1) % 64
    n = own.shape[0] // 2

    def one(z, _):
        for half in range(2):
            src = jnp.where(iz == half, 0, n) + z
            lf = jnp.where(ix > 0, xl[src], 0.0)
            rt = jnp.where(ix < 7, xr[src], 0.0)
            full[half * n + z] = jnp.concatenate(
                [own[src], rt[0:8], jnp.where(sub < 4, rt[8:16], lf[0:8]), lf[8:16]], axis=0
            )
        return 0

    lax.fori_loop(0, n, one, 0, unroll=2)

    def pack(group, _):
        a = lanes(full[group * 4], -52)
        b = full[group * 4]
        for j in range(1, 4):
            v = full[group * 4 + j]
            a = jnp.where(lane >= 16 * j, lanes(v, 16 * j - 52), a)
            b = jnp.where(lane >= 16 * j, lanes(v, 16 * j), b)
        to_right[group] = a
        to_left[group] = b
        return 0

    lax.fori_loop(0, n // 2, pack, 0)


def both(mid, lf, rt, j):
    lane = iota((40, 128), 1)
    rt, lf = lanes(rt, 64 - 16 * j), lanes(lf, 116 - 16 * j)
    first = jnp.where(lane < 64, mid, jnp.where(lane < 96, rt, lf))
    second = jnp.where(lane >= 64, mid, jnp.where(lane < 32, rt, lf))
    return first, lanes(second, 64)


def halve_x(ref, n, x2):
    x2[:, 14:18, :] = jnp.zeros((n, 4, 128), F32)
    x2[:, 0:14, :] = ref[:, pl.ds(0, 14, 2), :] + ref[:, pl.ds(1, 14, 2), :]
    x2[:, 18:24, :] = ref[:, pl.ds(28, 6, 2), :] + ref[:, pl.ds(29, 6, 2), :]
    return x2[...]


def down_matrix():
    return select_matrix(
        (128, 128),
        lambda i, o: ((i // 2 == o) & (o < 38)) | ((i // 2 == o - 64) & (o >= 122)),
        0.125,
    )


def level3_rows(v, e2):
    half = select_matrix((128, 128), lambda i, o: (i // 2 == o) & (o < 16), 0.125)
    v = v.reshape(8, 2, 24, 128)
    e2[...] = v[:, 0, :8, :] + v[:, 1, :8, :]
    pairs = e2[:, pl.ds(0, 4, 2), :] + e2[:, pl.ds(1, 4, 2), :]
    total = dot(pairs[0], half)
    for j in range(1, 8):
        total = total + lanes(dot(pairs[j], half), 16 * j)
    return total


def k_coeff(full, fl, fr, s1, c1, w1, s2, c2, w2, sk3, ps, pk, x2, e2):
    iy = lax.axis_index("gy")

    def unpack(group, _):
        lf = jnp.where(iy > 0, fl[group], 0.0)
        rt = jnp.where(iy < 7, fr[group], 0.0)
        for j in range(0, 4, 2):
            pair = []
            for i in range(2):
                z = group * 4 + j + i
                s, k = both(full[z], lf, rt, j + i)
                s1[z] = s
                w1[z], c1[z] = factors(s, k, 1)
                pair.append((s, k))
            ps[group * 2 + j // 2] = pair[0][0] + pair[1][0]
            pk[group * 2 + j // 2] = pair[0][1] + pair[1][1]
        return 0

    lax.fori_loop(0, 8, unpack, 0)
    down = down_matrix()
    s = dot3(halve_x(ps, 16, x2), down)
    k = dot3(halve_x(pk, 16, x2), down)
    s2[...] = s
    w2[...], c2[...] = factors(s, k, 2)
    sk3[...] = jnp.concatenate([level3_rows(s, e2), level3_rows(k, e2)], axis=0)


def k_down12(
    full, fl, fr, s1, c1, w1, s2, c2, w2, sk3, g, q, g2, q2, chunk, f, e, x2, e2
):
    iy = lax.axis_index("gy")
    for ref in (g, q):
        ref[0] = jnp.zeros((40, 128), F32)
        ref[33] = jnp.zeros((40, 128), F32)

    def unpack(group, _):
        lf = jnp.where(iy > 0, fl[group], 0.0)
        rt = jnp.where(iy < 7, fr[group], 0.0)
        for j in range(4):
            n = group * 4 + j
            z = n + 8 * (group // 2)
            a, b = both(full[n], lf, rt, j)
            f[z] = a
            f[z + 8] = b
            g[z + 1] = w1[z] * a
            g[z + 9] = w1[z + 8] * b
        return 0

    lax.fori_loop(0, 4, unpack, 0)

    def relax(z, _):
        q[z] = 0.4 * g[z] + c1[z - 1] * around(g[z - 1], g[z], g[z + 1])
        return 0

    lax.fori_loop(1, 33, relax, 0, unroll=2)
    wh, _ = weights(1)

    def residual(z):
        return 0.04 * f[z - 1] + (wh * s1[z - 1]) * around(q[z - 1], q[z], q[z + 1])

    def pair(z, _):
        e[z] = residual(2 * z + 1) + residual(2 * z + 2)
        return 0

    lax.fori_loop(0, 16, pair, 0)
    fv = dot3(halve_x(e, 16, x2), down_matrix())
    gv = w2[...] * fv
    zero = jnp.zeros((1, 24, 128), F32)

    def spread(v):
        w = jnp.concatenate([zero, v, zero], axis=0)
        return around(w[:16], v, w[2:])

    qv = 0.4 * gv + c2[...] * spread(gv)
    wh, _ = weights(2)
    ev = 0.04 * fv + (wh * s2[...]) * spread(qv)
    g2[...] = gv
    q2[...] = qv
    block = jnp.concatenate([level3_rows(ev, e2), sk3[...], jnp.zeros((4, 128), F32)], axis=0)
    block = pltpu.roll(block, 16 * iy, 1)

    def copy(n, _):
        chunk[n] = block
        return 0

    lax.fori_loop(0, 64, copy, 0, unroll=8)


def spread_in(shape, last):
    n, r, _ = shape
    row, col = iota(shape, 1), iota(shape, 2)
    zero = jnp.zeros((1,) + shape[1:], F32)

    def apply(v):
        w = jnp.concatenate([zero, v, zero], axis=0)
        x = jnp.where(row > 0, rows(v, 1), 0.0) + jnp.where(row < r - 1, rows(v, -1), 0.0)
        y = jnp.where(col > 0, lanes(v, 1), 0.0) + jnp.where(col < last, lanes(v, -1), 0.0)
        return 0.25 * (w[:n] + w[2:]) + x + y

    return apply


def k_whole(gathered, u, t3, x4, p3):
    ix, iy = lax.axis_index("gx"), lax.axis_index("gy")
    lane = iota((8, 128), 1) // 16
    sub = iota((8, 128), 0)
    for j in range(8):
        for t in range(2):
            tiles = []
            for x in range(8):
                v = gathered[x * 8, 8 * t : 8 * t + 8, :]
                for y in range(1, 8):
                    v = jnp.where(lane == (j + y) % 8, gathered[x * 8 + y, 8 * t : 8 * t + 8, :], v)
                tiles.append(lanes(v, -16 * j) if j else v)
            for x in range(4):
                a, b = tiles[2 * x], tiles[2 * x + 1]
                t3[2 * t, j, 8 * x : 8 * x + 8, :] = jnp.where(sub < 4, a, rows(b, 4))
                if t == 0:
                    t3[1, j, 8 * x : 8 * x + 8, :] = jnp.where(sub < 4, rows(a, 4), b)
    f3, s3, k3 = t3[0], t3[1], t3[2]
    near3 = spread_in((8, 32, 128), 127)
    w3, c3 = factors(s3, k3, 3)
    g3 = w3 * f3
    q3 = 0.4 * g3 + c3 * near3(g3)
    e3 = 0.04 * f3 + (weights(3)[0] * s3) * near3(q3)
    half = select_matrix((128, 128), lambda i, o: i // 2 == o, 0.125)
    fields = []
    for v in (e3, s3, k3):
        w = v.reshape(4, 2, 32, 128)
        x4[...] = w[:, 0] + w[:, 1]
        fields.append(dot3(x4[:, pl.ds(0, 16, 2), :] + x4[:, pl.ds(1, 16, 2), :], half))
    f4, s4, k4 = fields
    near4 = spread_in((4, 16, 128), 63)
    w4, c4 = factors(s4, k4, 4)
    g4 = w4 * f4
    v4 = g4
    for _ in range(COARSE_SWEEPS):
        v4 = (0.2 * v4 + g4) + c4 * near4(v4)
    u4 = dot3(unscale(v4, s4), select_matrix((128, 128), lambda i, o: i == o // 2))
    p3[:, pl.ds(0, 16, 2), :] = u4
    p3[:, pl.ds(1, 16, 2), :] = u4
    w = p3[...]
    w = jnp.broadcast_to(w[:, None], (4, 2, 32, 128)).reshape(8, 32, 128)
    v3 = (q3 + 0.8 * g3) + s3 * w
    for _ in range(2):
        v3 = (0.2 * v3 + g3) + c3 * near3(v3)
    pick = select_matrix(
        (128, 128),
        lambda i, o: i == (jnp.where(o < 64, o // 2, 127 - (127 - o) // 2) + 16 * iy) % 128,
    )
    u[...] = pltpu.roll(dot3(v3 / s3, pick), (32 - 4 * ix) % 32, 1)


def k_up2(u3, g2, c2, s2, q2, u, p2):
    p2[:, 14:18, :] = jnp.zeros((8, 4, 128), F32)
    for n in range(2):
        p2[:, pl.ds(n, 7, 2), :] = u3[:, 0:7, :]
        p2[:, pl.ds(18 + n, 3, 2), :] = u3[:, 29:32, :]
    w = p2[...]
    w = jnp.broadcast_to(w[:, None], (8, 2, 24, 128)).reshape(16, 24, 128)
    gv, cv, sv = g2[...], c2[...], s2[...]
    zero = jnp.zeros((1, 24, 128), F32)
    v = (q2[...] + 0.8 * gv) + sv * w
    for _ in range(2):
        w = jnp.concatenate([zero, v, zero], axis=0)
        v = (0.2 * v + gv) + cv * around(w[:16], v, w[2:])
    pick = select_matrix(
        (128, 128),
        lambda i, o: i == jnp.where(o < 96, o // 2, 127 - (127 - o) // 2),
    )
    u[...] = dot3(unscale(v, sv), pick)


def k_up1(u2, g1, c1, s1, q1, u, p1, va, vb):
    for n in range(2):
        p1[:, pl.ds(n, 14, 2), :] = u2[:, 0:14, :]
        p1[:, pl.ds(28 + n, 6, 2), :] = u2[:, 18:24, :]
    for ref in (va, vb, u):
        ref[0] = jnp.zeros((40, 128), F32)
        ref[33] = jnp.zeros((40, 128), F32)

    def start(z, _):
        va[z] = (q1[z] + 0.8 * g1[z]) + s1[z - 1] * p1[(z - 1) // 2]
        return 0

    lax.fori_loop(1, 33, start, 0, unroll=2)

    def sweep(z, _):
        vb[z] = (0.2 * va[z] + g1[z]) + c1[z - 1] * around(va[z - 1], va[z], va[z + 1])
        return 0

    lax.fori_loop(1, 33, sweep, 0, unroll=2)

    def last(z, _):
        v = (0.2 * vb[z] + g1[z]) + c1[z - 1] * around(vb[z - 1], vb[z], vb[z + 1])
        u[z] = unscale(v, s1[z - 1])
        return 0

    lax.fori_loop(1, 33, last, 0, unroll=2)


def k_up0(u1, gm, cm, sm, q, gw, cw, sw, qw, out, y0, pm, pw, wa, wb, ea, eb):
    iz = lax.axis_index("gz")

    def source(i, o):
        y = jnp.where(o % 16 < 8, 125 + o % 16, o % 16 - 11)
        return i == jnp.where(o < 128, o // 2, ((y + 256) // 2) % 128)

    y0[...] = dot3(u1[pl.ds(16 * iz, 18)], select_matrix((128, 256), source))

    def twice(t, _):
        v = y0[t]
        for h, ref in enumerate((pm, pw)):
            w = v[:, 128 * h : 128 * h + 128]
            for n in range(2):
                ref[t, pl.ds(n, 18, 2), :] = w[0:18]
                ref[t, pl.ds(36 + n, 2, 2), :] = w[38:40]
        return 0

    lax.fori_loop(0, 18, twice, 0)
    slot = iota((40, 128), 1) // 16
    parts = []
    for group in range(5):
        total = None
        for j in range(8):
            part = pw[min(max((8 * group + j - 1) // 2, 0), 17)]
            total = part if total is None else jnp.where(slot >= j, part, total)
        parts.append(total[None])
    g, c = gw[...], cw[...]
    v = (qw[...] + 0.8 * g) + sw[...] * jnp.concatenate(parts, axis=0)
    ea[...] = joint(v)
    eb[...] = joint((0.2 * v + g) + c * near_edges(v))

    def start(z, _):
        wa[z] = (q[z] + 0.8 * gm[z]) + sm[z] * pm[(z - 1) // 2]
        return 0

    lax.fori_loop(1, 37, start, 0, unroll=2)

    def sweep(z, _):
        wb[z] = (0.2 * wa[z] + gm[z]) + cm[z] * near_main(wa, ea, z)
        return 0

    lax.fori_loop(2, 36, sweep, 0, unroll=2)

    def last(z, _):
        n = near_main(wb, eb, z)[:32]
        v = (0.2 * wb[z, :32, :] + gm[z, :32, :]) + cm[z, :32, :] * n
        out[z - 3] = v / sm[z, :32, :]
        return 0

    lax.fori_loop(3, 35, last, 0, unroll=2)


def ring(v, axis, step):
    n = lax.axis_size(axis)
    return lax.ppermute(v, axis, [(i, (i + step) % n) for i in range(n)])


def pair(to_right, to_left, axis):
    return ring(to_right, axis, 1), ring(to_left, axis, -1)


def spread(own):
    own = jnp.concatenate([own, ring(own, "gz", 1)], axis=0)
    n = own.shape[0]
    full, to_right, to_left = run(
        k_spread, (own, *pair(own, own, "gx")), [(n, 40, 128)] + [(n // 4, 40, 128)] * 2
    )
    return (full, *pair(to_right, to_left, "gy"))


def shards(f, s, k):
    (zmsg,) = run(k_face_z, (f, s, k), [(7, 32, 128)], [(3, 3, 32, 128)], ANY, [(3,)])
    zr = ring(zmsg, "gz", 1)
    f, s, k, g, c = run(k_load, (f, s, k), [(32, 32, 128)] * 5, (), ANY, [(12,)])
    (sk1,) = run(k_coarse_coeff, (s, k), [(16, 16, 128)], [(16, 32, 128)] * 2)
    xs = pair(*run(k_face_x, (g, c, s, zr), [(38, 8, 128)] * 2), "gx")
    gm, cm, sm, ymsg = run(k_face_y, (g, c, s, zr, *xs), [(40, 40, 128)] * 3 + [(5, 40, 128)])
    ys = pair(ymsg, ymsg, "gy")
    small = [(5, 40, 128)]
    gw, cw, sw, q0, qw, f1 = run(
        k_down0,
        (f, gm, cm, sm, ymsg, *ys),
        small * 3 + [(38, 40, 128)] + small + [(8, 16, 128)],
        [(16, 32, 128)] + small * 2,
    )
    s1, c1, w1, s2, c2, w2, sk3 = run(
        k_coeff,
        spread(sk1),
        [(32, 40, 128)] * 3 + [(16, 24, 128)] * 3 + [(8, 128)],
        [(16, 40, 128)] * 2 + [(16, 24, 128), (8, 8, 128)],
    )
    g1, q1, g2, q2, chunk = run(
        k_down12,
        (*spread(f1), s1, c1, w1, s2, c2, w2, sk3),
        [(34, 40, 128)] * 2 + [(16, 24, 128)] * 2 + [(64, 16, 128)],
        [(32, 40, 128), (16, 40, 128), (16, 24, 128), (8, 8, 128)],
    )
    gathered = lax.all_to_all(chunk, ("gx", "gy"), 0, 0, tiled=True)
    (u3,) = run(
        k_whole, (gathered,), [(8, 32, 128)], [(3, 8, 32, 128), (4, 32, 128), (4, 32, 128)]
    )
    (u2,) = run(k_up2, (u3, g2, c2, s2, q2), [(16, 24, 128)], [(8, 24, 128)])
    (u1,) = run(
        k_up1, (u2, g1, c1, s1, q1), [(34, 40, 128)], [(16, 40, 128)] + [(34, 40, 128)] * 2
    )
    (out,) = run(
        k_up0,
        (u1, gm, cm, sm, q0, gw, cw, sw, qw),
        [(32, 32, 128)],
        [(18, 40, 256)] + [(18, 40, 128)] * 2 + [(38, 40, 128)] * 2 + small * 2,
    )
    return out


def solution(mesh):
    return jax.shard_map(
        shards,
        mesh=mesh,
        in_specs=(P("gz", "gx", "gy"),) * 3,
        out_specs=P("gz", "gx", "gy"),
        check_vma=False,
    )
```

```python
import math

import jax
import jax.numpy as jnp
from jax import lax
from jax.experimental import pallas as pl
from jax.experimental.pallas import tpu as pltpu
from jax.sharding import PartitionSpec as P

F32 = jnp.float32
VM = pl.BlockSpec(memory_space=pltpu.VMEM)
HBM = pl.BlockSpec(memory_space=pltpu.HBM)
BF16 = jnp.bfloat16
COARSE_SWEEPS = 11
A0, B0, U0 = 12, 8, 3
A1, U1 = 8, 2


def run(body, args, outs, scratch=(), spec=VM, sems=()):
    words = sum(math.prod(s) for s in (*outs, *scratch))
    words += sum(a.size for a in args) if spec is VM else 0
    return pl.pallas_call(
        body,
        out_shape=[jax.ShapeDtypeStruct(o, F32) for o in outs],
        in_specs=[spec] * len(args),
        out_specs=[VM] * len(outs),
        scratch_shapes=[pltpu.VMEM(s, F32) for s in scratch]
        + [pltpu.SemaphoreType.DMA(n) for n in sems],
        compiler_params=pltpu.CompilerParams(vmem_limit_bytes=6 * words + (6 << 20)),
    )(*args)


def weights(level):
    wh = 0.25**level
    return wh, 2.0 * (0.25 * wh + 2.0 * wh)


def iota(shape, dim):
    return lax.broadcasted_iota(jnp.int32, shape, dim)


def lanes(v, shift):
    return pltpu.roll(v, shift % v.shape[-1], v.ndim - 1)


def rows(v, shift):
    return pltpu.roll(v, shift % v.shape[-2], v.ndim - 2)


def beside(v):
    return (rows(v, 1) + rows(v, -1)) + (lanes(v, 1) + lanes(v, -1))


def around(above, v, below):
    return 0.25 * (above + below) + beside(v)


def factors(s, k, level):
    wh, full = weights(level)
    diagonal = k + full * (s * s)
    sw = s * (0.8 / jnp.where(diagonal > 0.0, diagonal, 1.0))
    return sw, (wh * s) * sw


def unscale(v, s):
    inside = s > 0.0
    return jnp.where(inside, v / jnp.where(inside, s, 1.0), 0.0)


def dot(a, b):
    b = b.astype(BF16)
    high = a.astype(BF16)
    rest = a - high.astype(F32)
    middle = rest.astype(BF16)
    low = (rest - middle.astype(F32)).astype(BF16)
    terms = [jnp.dot(t, b, preferred_element_type=F32) for t in (high, middle, low)]
    return terms[0] + (terms[1] + terms[2])


def dot3(a, b):
    n, r, c = a.shape
    return dot(a.reshape(n * r, c), b).reshape(n, r, b.shape[1])


def blocks(first, count, size, body, unroll=1):
    def one(b, _):
        z = first + size * b
        body(z, pl.ds(z, size))
        return 0

    lax.fori_loop(0, count // size, one, 0, unroll=unroll)


def pair_sum(v):
    v = v.reshape(v.shape[0] // 2, 2, *v.shape[1:])
    return v[:, 0] + v[:, 1]


def select_matrix(shape, source_of, scale=1.0):
    i, o = iota(shape, 0), iota(shape, 1)
    return jnp.where(source_of(i, o), scale, 0.0).astype(F32)


def k_face_z(f, s, k, zmsg, buf, sem):
    iz = lax.axis_index("gz")
    first = jnp.where(iz == 0, 29, 0)
    copies = [
        pltpu.make_async_copy(ref.at[pl.ds(first, 3)], buf.at[n], sem.at[n])
        for n, ref in enumerate((f, s, k))
    ]
    for copy in copies:
        copy.start()
    for copy in copies:
        copy.wait()
    for d in range(3):
        z = jnp.where(iz == 0, 2 - d, d)
        sv = buf[1, z]
        sw, c = factors(sv, buf[2, z], 0)
        zmsg[d] = sw * buf[0, z]
        if d < 2:
            zmsg[3 + d] = c
            zmsg[5 + d] = sv


def k_load(f, s, k, fv, sv, kv, g, c, sem):
    copies = [
        [
            pltpu.make_async_copy(
                ref.at[pl.ds(8 * b, 8)], dst.at[pl.ds(8 * b, 8)], sem.at[3 * b + n]
            )
            for n, (ref, dst) in enumerate(((f, fv), (s, sv), (k, kv)))
        ]
        for b in range(4)
    ]
    for block in copies:
        for copy in block:
            copy.start()
    for b in range(4):
        for copy in copies[b]:
            copy.wait()

        def one(z, _):
            sw, cz = factors(sv[z], kv[z], 0)
            g[z] = sw * fv[z]
            c[z] = cz
            return 0

        lax.fori_loop(8 * b, 8 * b + 8, one, 0, unroll=4)


def k_coarse_coeff(s, k, sk1, ps, pk):
    def one(z, _):
        ps[z] = s[2 * z] + s[2 * z + 1]
        pk[z] = k[2 * z] + k[2 * z + 1]
        return 0

    lax.fori_loop(0, 16, one, 0, unroll=4)
    a = ps[:, pl.ds(0, 16, 2), :] + ps[:, pl.ds(1, 16, 2), :]
    b = pk[:, pl.ds(0, 16, 2), :] + pk[:, pl.ds(1, 16, 2), :]
    left = select_matrix((128, 128), lambda i, o: i // 2 == o, 0.125)
    right = select_matrix((128, 128), lambda i, o: i // 2 == o - 64, 0.125)
    sk1[...] = dot3(a, left) + dot3(b, right)


def halo_rows(zr, iz, field, z):
    first, depth = ((0, 3), (3, 2), (5, 2))[field]
    d = z - 35 if z > 34 else 2 - z
    if d >= depth:
        return jnp.zeros(zr.shape[1:], F32)
    return jnp.where(iz == (0 if z > 34 else 1), zr[first + d], 0.0)


def k_face_x(g, c, s, zr, to_right, to_left):
    iz = lax.axis_index("gz")
    sub = iota((8, 128), 0)

    def put(z, gz, cz, sz):
        a, b, d = gz[24:32], cz[24:32], sz[24:32]
        to_right[z] = jnp.where(sub >= 5, a, jnp.where(sub >= 3, rows(b, -3), rows(d, -5)))
        a, b, d = gz[0:8], cz[0:8], sz[0:8]
        to_left[z] = jnp.where(sub < 3, a, jnp.where(sub < 5, rows(b, 3), rows(d, 5)))

    def one(z, _):
        put(z + 3, g[z], c[z], s[z])
        return 0

    lax.fori_loop(0, 32, one, 0, unroll=4)
    for z in (0, 1, 2, 35, 36, 37):
        put(z, *[halo_rows(zr, iz, n, z) for n in range(3)])


def k_face_y(g, c, s, zr, from_left, from_right, gm, cm, sm, ymsg):
    ix, iz = lax.axis_index("gx"), lax.axis_index("gz")
    sub = iota((8, 128), 0)

    def sides(z):
        lf = jnp.where(ix > 0, from_left[z], 0.0)
        rt = jnp.where(ix < 7, from_right[z], 0.0)
        return (
            jnp.where(sub >= 4, lf, rt),
            jnp.where(sub >= 4, rows(lf, 3), rows(rt, -3)),
            jnp.where(sub >= 4, rows(lf, 5), rows(rt, -5)),
        )

    def put(z, values):
        for ref, own, side in zip((gm, cm, sm), values, sides(z)):
            ref[z] = jnp.concatenate([own, side], axis=0)

    def one(z, _):
        put(z + 3, (g[z], c[z], s[z]))
        return 0

    lax.fori_loop(0, 32, one, 0, unroll=4)
    for z in (0, 1, 2, 35, 36, 37):
        put(z, [halo_rows(zr, iz, n, z) for n in range(3)])
    for z in (38, 39):
        for ref in (gm, cm, sm):
            ref[z] = jnp.zeros((40, 128), F32)
    lane = iota((40, 128), 1)

    def pack(group, _):
        total = jnp.zeros((40, 128), F32)
        for j in range(8):
            z = group * 8 + j
            slot = lane - 16 * j
            total = jnp.where(slot >= 0, lanes(gm[z], 16 * j + 3), total)
            total = jnp.where(slot >= 6, lanes(cm[z], 16 * j + 8), total)
            total = jnp.where(slot >= 10, lanes(sm[z], 16 * j + 12), total)
        ymsg[group] = total
        return 0

    lax.fori_loop(0, 5, pack, 0)


def near_edges(v):
    lane = iota(v.shape, 2)
    zero = jnp.zeros((1,) + v.shape[1:], F32)
    up, down = lanes(v, 16), lanes(v, -16)
    above = jnp.where(lane < 16, jnp.concatenate([zero, up[:-1]], axis=0), up)
    below = jnp.where(lane >= 112, jnp.concatenate([down[1:], zero], axis=0), down)
    return around(above, v, below)


def joint(v):
    return jnp.where(iota(v.shape, 2) % 16 == 4, lanes(v, -6), v)


def near_main(ref, edge, z, n):
    v = ref[pl.ds(z, n)]
    lane = iota(v.shape, 2)
    e = jnp.stack(
        [
            pltpu.roll(edge[(z + i) // 8], (124 - 16 * ((z + i) % 8)) % 128, 1)
            for i in range(n)
        ]
    )
    across = jnp.where(lane == 0, e, lanes(v, 1)) + jnp.where(lane == 127, e, lanes(v, -1))
    above, below = ref[pl.ds(z - 1, n)], ref[pl.ds(z + 1, n)]
    return 0.25 * (above + below) + ((rows(v, 1) + rows(v, -1)) + across)


def near(ref, z, n):
    return around(ref[pl.ds(z - 1, n)], ref[pl.ds(z, n)], ref[pl.ds(z + 1, n)])


def k_down0(f, gm, cm, sm, own, from_left, from_right, gw, cw, sw, q, qw, f1, e, eg, eq):
    iy = lax.axis_index("gy")
    lane = iota((5, 40, 128), 2) % 16
    mid = own[...]
    lf = jnp.where(iy > 0, from_left[...], 0.0)
    rt = jnp.where(iy < 7, from_right[...], 0.0)

    def window(split, to_right, to_left):
        a = jnp.where(lane < split, mid, rt)
        b = jnp.where(lane < split, lf, mid)
        a = lanes(a, to_right) if to_right else a
        return jnp.where(lane < 8, a, lanes(b, to_left))

    g = window(3, 0, 8)
    c = window(8, -5, 3)
    gw[...] = g
    cw[...] = c
    sw[...] = window(12, -9, -1)
    w = 0.4 * g + c * near_edges(g)
    qw[...] = w
    eg[...] = joint(g)
    eq[...] = joint(w)
    q[0] = jnp.zeros((40, 128), F32)
    q[37] = jnp.zeros((40, 128), F32)

    def relax(z, at):
        q[at] = 0.4 * gm[at] + cm[at] * near_main(gm, eg, z, A0)

    blocks(1, 36, A0, relax, U0)

    def residual(z, at):
        v = 0.04 * f[pl.ds(z - 3, B0)] + sm[at, :32, :] * near_main(q, eq, z, B0)[:, :32]
        e[pl.ds((z - 3) // 2, B0 // 2)] = pair_sum(v)

    blocks(3, 32, B0, residual, U0)
    a = e[:, pl.ds(0, 16, 2), :] + e[:, pl.ds(1, 16, 2), :]
    lo = select_matrix((128, 128), lambda i, o: i // 2 == o, 0.125)
    hi = select_matrix((128, 128), lambda i, o: i // 2 == o - 64, 0.125)
    f1[...] = dot3(a[:8], lo) + dot3(a[8:], hi)


def k_spread(own, xl, xr, full, to_right, to_left):
    ix, iz = lax.axis_index("gx"), lax.axis_index("gz")
    sub = iota((8, 128), 0)
    lane = iota((40, 128), 1) % 64
    n = own.shape[0] // 2

    def one(z, _):
        for half in range(2):
            src = jnp.where(iz == half, 0, n) + z
            lf = jnp.where(ix > 0, xl[src], 0.0)
            rt = jnp.where(ix < 7, xr[src], 0.0)
            full[half * n + z] = jnp.concatenate(
                [own[src], rt[0:8], jnp.where(sub < 4, rt[8:16], lf[0:8]), lf[8:16]], axis=0
            )
        return 0

    lax.fori_loop(0, n, one, 0, unroll=2)

    def pack(group, _):
        a = lanes(full[group * 4], -52)
        b = full[group * 4]
        for j in range(1, 4):
            v = full[group * 4 + j]
            a = jnp.where(lane >= 16 * j, lanes(v, 16 * j - 52), a)
            b = jnp.where(lane >= 16 * j, lanes(v, 16 * j), b)
        to_right[group] = a
        to_left[group] = b
        return 0

    lax.fori_loop(0, n // 2, pack, 0)


def both(mid, lf, rt, j):
    lane = iota((40, 128), 1)
    rt, lf = lanes(rt, 64 - 16 * j), lanes(lf, 116 - 16 * j)
    first = jnp.where(lane < 64, mid, jnp.where(lane < 96, rt, lf))
    second = jnp.where(lane >= 64, mid, jnp.where(lane < 32, rt, lf))
    return first, lanes(second, 64)


def halve_x(ref, n, x2):
    x2[:, 14:18, :] = jnp.zeros((n, 4, 128), F32)
    x2[:, 0:14, :] = ref[:, pl.ds(0, 14, 2), :] + ref[:, pl.ds(1, 14, 2), :]
    x2[:, 18:24, :] = ref[:, pl.ds(28, 6, 2), :] + ref[:, pl.ds(29, 6, 2), :]
    return x2[...]


def down_matrix():
    return select_matrix(
        (128, 128),
        lambda i, o: ((i // 2 == o) & (o < 38)) | ((i // 2 == o - 64) & (o >= 122)),
        0.125,
    )


def level3_rows(v, e2):
    half = select_matrix((128, 128), lambda i, o: (i // 2 == o) & (o < 16), 0.125)
    v = v.reshape(8, 2, 24, 128)
    e2[...] = v[:, 0, :8, :] + v[:, 1, :8, :]
    pairs = e2[:, pl.ds(0, 4, 2), :] + e2[:, pl.ds(1, 4, 2), :]
    total = dot(pairs[0], half)
    for j in range(1, 8):
        total = total + lanes(dot(pairs[j], half), 16 * j)
    return total


def k_coeff(full, fl, fr, s1, c1, w1, s2, c2, w2, sk3, ps, pk, x2, e2):
    iy = lax.axis_index("gy")

    def unpack(group, _):
        lf = jnp.where(iy > 0, fl[group], 0.0)
        rt = jnp.where(iy < 7, fr[group], 0.0)
        sk = [both(full[group * 4 + j], lf, rt, j) for j in range(4)]
        fs = [factors(s, k, 1) for s, k in sk]
        for j in range(4):
            z = group * 4 + j
            s1[z] = sk[j][0]
            w1[z], c1[z] = fs[j]
        for j in range(2):
            ps[group * 2 + j] = sk[2 * j][0] + sk[2 * j + 1][0]
            pk[group * 2 + j] = sk[2 * j][1] + sk[2 * j + 1][1]
        return 0

    lax.fori_loop(0, 8, unpack, 0, unroll=2)
    down = down_matrix()
    s = dot3(halve_x(ps, 16, x2), down)
    k = dot3(halve_x(pk, 16, x2), down)
    s2[...] = s
    w2[...], c2[...] = factors(s, k, 2)
    sk3[...] = jnp.concatenate([level3_rows(s, e2), level3_rows(k, e2)], axis=0)


def k_down12(
    full, fl, fr, s1, c1, w1, s2, c2, w2, sk3, g, q, g2, q2, chunk, f, e, x2, e2
):
    iy = lax.axis_index("gy")
    for ref in (g, q):
        ref[0] = jnp.zeros((40, 128), F32)
        ref[33] = jnp.zeros((40, 128), F32)

    def unpack(group, _):
        lf = jnp.where(iy > 0, fl[group], 0.0)
        rt = jnp.where(iy < 7, fr[group], 0.0)
        parts = [both(full[group * 4 + j], lf, rt, j) for j in range(4)]
        first = group * 4 + 8 * (group // 2)
        for i in range(2):
            v = jnp.stack([p[i] for p in parts])
            w = w1[pl.ds(first + 8 * i, 4)] * v
            f[pl.ds(first + 8 * i, 4)] = v
            g[pl.ds(first + 8 * i + 1, 4)] = w
        return 0

    lax.fori_loop(0, 4, unpack, 0, unroll=2)

    def relax(z, at):
        q[at] = 0.4 * g[at] + c1[pl.ds(z - 1, A1)] * near(g, z, A1)

    blocks(1, 32, A1, relax, U1)
    wh, _ = weights(1)

    def residual(z, at):
        own = pl.ds(z - 1, A1)
        v = 0.04 * f[own] + (wh * s1[own]) * near(q, z, A1)
        e[pl.ds((z - 1) // 2, A1 // 2)] = pair_sum(v)

    blocks(1, 32, A1, residual, U1)
    fv = dot3(halve_x(e, 16, x2), down_matrix())
    gv = w2[...] * fv
    zero = jnp.zeros((1, 24, 128), F32)

    def spread(v):
        w = jnp.concatenate([zero, v, zero], axis=0)
        return around(w[:16], v, w[2:])

    qv = 0.4 * gv + c2[...] * spread(gv)
    wh, _ = weights(2)
    ev = 0.04 * fv + (wh * s2[...]) * spread(qv)
    g2[...] = gv
    q2[...] = qv
    block = jnp.concatenate([level3_rows(ev, e2), sk3[...], jnp.zeros((4, 128), F32)], axis=0)
    block = pltpu.roll(block, 16 * iy, 1)

    def copy(n, _):
        chunk[n] = block
        return 0

    lax.fori_loop(0, 64, copy, 0, unroll=8)


def spread_in(shape, last):
    n, r, _ = shape
    row, col = iota(shape, 1), iota(shape, 2)
    zero = jnp.zeros((1,) + shape[1:], F32)

    def apply(v):
        w = jnp.concatenate([zero, v, zero], axis=0)
        x = jnp.where(row > 0, rows(v, 1), 0.0) + jnp.where(row < r - 1, rows(v, -1), 0.0)
        y = jnp.where(col > 0, lanes(v, 1), 0.0) + jnp.where(col < last, lanes(v, -1), 0.0)
        return 0.25 * (w[:n] + w[2:]) + x + y

    return apply


def k_whole(gathered, u, t3, x4, p3):
    ix, iy = lax.axis_index("gx"), lax.axis_index("gy")
    lane = iota((8, 128), 1) // 16
    sub = iota((8, 128), 0)
    for j in range(8):
        for t in range(2):
            tiles = []
            for x in range(8):
                v = gathered[x * 8, 8 * t : 8 * t + 8, :]
                for y in range(1, 8):
                    v = jnp.where(lane == (j + y) % 8, gathered[x * 8 + y, 8 * t : 8 * t + 8, :], v)
                tiles.append(lanes(v, -16 * j) if j else v)
            for x in range(4):
                a, b = tiles[2 * x], tiles[2 * x + 1]
                t3[2 * t, j, 8 * x : 8 * x + 8, :] = jnp.where(sub < 4, a, rows(b, 4))
                if t == 0:
                    t3[1, j, 8 * x : 8 * x + 8, :] = jnp.where(sub < 4, rows(a, 4), b)
    f3, s3, k3 = t3[0], t3[1], t3[2]
    near3 = spread_in((8, 32, 128), 127)
    w3, c3 = factors(s3, k3, 3)
    g3 = w3 * f3
    q3 = 0.4 * g3 + c3 * near3(g3)
    e3 = 0.04 * f3 + (weights(3)[0] * s3) * near3(q3)
    half = select_matrix((128, 128), lambda i, o: i // 2 == o, 0.125)
    fields = []
    for v in (e3, s3, k3):
        w = v.reshape(4, 2, 32, 128)
        x4[...] = w[:, 0] + w[:, 1]
        fields.append(dot3(x4[:, pl.ds(0, 16, 2), :] + x4[:, pl.ds(1, 16, 2), :], half))
    f4, s4, k4 = fields
    near4 = spread_in((4, 16, 128), 63)
    w4, c4 = factors(s4, k4, 4)
    g4 = w4 * f4
    v4 = g4
    for _ in range(COARSE_SWEEPS):
        v4 = (0.2 * v4 + g4) + c4 * near4(v4)
    u4 = dot3(unscale(v4, s4), select_matrix((128, 128), lambda i, o: i == o // 2))
    p3[:, pl.ds(0, 16, 2), :] = u4
    p3[:, pl.ds(1, 16, 2), :] = u4
    w = p3[...]
    w = jnp.broadcast_to(w[:, None], (4, 2, 32, 128)).reshape(8, 32, 128)
    v3 = (q3 + 0.8 * g3) + s3 * w
    for _ in range(2):
        v3 = (0.2 * v3 + g3) + c3 * near3(v3)
    pick = select_matrix(
        (128, 128),
        lambda i, o: i == (jnp.where(o < 64, o // 2, 127 - (127 - o) // 2) + 16 * iy) % 128,
    )
    u[...] = pltpu.roll(dot3(v3 / s3, pick), (32 - 4 * ix) % 32, 1)


def k_up2(u3, g2, c2, s2, q2, u, p2):
    p2[:, 14:18, :] = jnp.zeros((8, 4, 128), F32)
    for n in range(2):
        p2[:, pl.ds(n, 7, 2), :] = u3[:, 0:7, :]
        p2[:, pl.ds(18 + n, 3, 2), :] = u3[:, 29:32, :]
    w = p2[...]
    w = jnp.broadcast_to(w[:, None], (8, 2, 24, 128)).reshape(16, 24, 128)
    gv, cv, sv = g2[...], c2[...], s2[...]
    zero = jnp.zeros((1, 24, 128), F32)
    v = (q2[...] + 0.8 * gv) + sv * w
    for _ in range(2):
        w = jnp.concatenate([zero, v, zero], axis=0)
        v = (0.2 * v + gv) + cv * around(w[:16], v, w[2:])
    pick = select_matrix(
        (128, 128),
        lambda i, o: i == jnp.where(o < 96, o // 2, 127 - (127 - o) // 2),
    )
    u[...] = dot3(unscale(v, sv), pick)


def k_up1(u2, g1, c1, s1, q1, u, p1, va, vb):
    for n in range(2):
        p1[:, pl.ds(n, 14, 2), :] = u2[:, 0:14, :]
        p1[:, pl.ds(28 + n, 6, 2), :] = u2[:, 18:24, :]
    for ref in (va, vb, u):
        ref[0] = jnp.zeros((40, 128), F32)
        ref[33] = jnp.zeros((40, 128), F32)

    def start(z, at):
        t = p1[pl.ds((z - 1) // 2, A1 // 2)]
        t = jnp.broadcast_to(t[:, None], (A1 // 2, 2, 40, 128)).reshape(A1, 40, 128)
        va[at] = (q1[at] + 0.8 * g1[at]) + s1[pl.ds(z - 1, A1)] * t

    blocks(1, 32, A1, start, U1)

    def sweep(z, at):
        vb[at] = (0.2 * va[at] + g1[at]) + c1[pl.ds(z - 1, A1)] * near(va, z, A1)

    blocks(1, 32, A1, sweep, U1)

    def last(z, at):
        own = pl.ds(z - 1, A1)
        v = (0.2 * vb[at] + g1[at]) + c1[own] * near(vb, z, A1)
        u[at] = unscale(v, s1[own])

    blocks(1, 32, A1, last, U1)


def k_up0(u1, gm, cm, sm, q, gw, cw, sw, qw, out, pm, pw, wa, wb, ea, eb):
    iz = lax.axis_index("gz")

    def source(i, o):
        y = jnp.where(o % 16 < 8, 125 + o % 16, o % 16 - 11)
        return i == jnp.where(o < 128, o // 2, ((y + 256) // 2) % 128)

    u = u1[pl.ds(16 * iz, 18)]
    sub = iota((18, 8, 128), 1)
    u = jnp.concatenate([u[:, :16], jnp.where(sub < 4, u[:, 16:24], u[:, 32:40])], axis=1)
    u = dot3(u, select_matrix((128, 256), source))
    for h, ref in enumerate((pm, pw)):
        w = u[:, :, 128 * h : 128 * h + 128]
        for n in range(2):
            ref[:, pl.ds(n, 18, 2), :] = w[:, 0:18]
            ref[:, pl.ds(36 + n, 2, 2), :] = w[:, 22:24]
    slot = iota((40, 128), 1) // 16
    parts = []
    for group in range(5):
        total = None
        for j in range(8):
            part = pw[min(max((8 * group + j - 1) // 2, 0), 17)]
            total = part if total is None else jnp.where(slot >= j, part, total)
        parts.append(total[None])
    g, c = gw[...], cw[...]
    v = (qw[...] + 0.8 * g) + sw[...] * jnp.concatenate(parts, axis=0)
    ea[...] = joint(v)
    eb[...] = joint((0.2 * v + g) + c * near_edges(v))

    def start(z, at):
        t = jnp.stack([pm[(z + i - 1) // 2] for i in range(A0)])
        wa[at] = (q[at] + 0.8 * gm[at]) + sm[at] * t

    blocks(1, 36, A0, start, U0)
    wa[0] = jnp.zeros((40, 128), F32)
    wa[37] = jnp.zeros((40, 128), F32)

    def sweep(z, at):
        wb[at] = (0.2 * wa[at] + gm[at]) + cm[at] * near_main(wa, ea, z, A0)

    blocks(1, 36, A0, sweep, U0)

    def last(z, at):
        n = near_main(wb, eb, z, B0)[:, :32]
        v = (0.2 * wb[at, :32, :] + gm[at, :32, :]) + cm[at, :32, :] * n
        out[pl.ds(z - 3, B0)] = v / sm[at, :32, :]

    blocks(3, 32, B0, last, U0)


def ring(v, axis, step):
    n = lax.axis_size(axis)
    return lax.ppermute(v, axis, [(i, (i + step) % n) for i in range(n)])


def pair(to_right, to_left, axis):
    return ring(to_right, axis, 1), ring(to_left, axis, -1)


def spread(own):
    own = jnp.concatenate([own, ring(own, "gz", 1)], axis=0)
    n = own.shape[0]
    full, to_right, to_left = run(
        k_spread, (own, *pair(own, own, "gx")), [(n, 40, 128)] + [(n // 4, 40, 128)] * 2
    )
    return (full, *pair(to_right, to_left, "gy"))


def shards(f, s, k):
    (zmsg,) = run(k_face_z, (f, s, k), [(7, 32, 128)], [(3, 3, 32, 128)], HBM, [(3,)])
    zr = ring(zmsg, "gz", 1)
    f, s, k, g, c = run(k_load, (f, s, k), [(32, 32, 128)] * 5, (), HBM, [(12,)])
    (sk1,) = run(k_coarse_coeff, (s, k), [(16, 16, 128)], [(16, 32, 128)] * 2)
    xs = pair(*run(k_face_x, (g, c, s, zr), [(38, 8, 128)] * 2), "gx")
    gm, cm, sm, ymsg = run(k_face_y, (g, c, s, zr, *xs), [(40, 40, 128)] * 3 + [(5, 40, 128)])
    ys = pair(ymsg, ymsg, "gy")
    small = [(5, 40, 128)]
    gw, cw, sw, q0, qw, f1 = run(
        k_down0,
        (f, gm, cm, sm, ymsg, *ys),
        small * 3 + [(38, 40, 128)] + small + [(8, 16, 128)],
        [(16, 32, 128)] + small * 2,
    )
    s1, c1, w1, s2, c2, w2, sk3 = run(
        k_coeff,
        spread(sk1),
        [(32, 40, 128)] * 3 + [(16, 24, 128)] * 3 + [(8, 128)],
        [(16, 40, 128)] * 2 + [(16, 24, 128), (8, 8, 128)],
    )
    g1, q1, g2, q2, chunk = run(
        k_down12,
        (*spread(f1), s1, c1, w1, s2, c2, w2, sk3),
        [(34, 40, 128)] * 2 + [(16, 24, 128)] * 2 + [(64, 16, 128)],
        [(32, 40, 128), (16, 40, 128), (16, 24, 128), (8, 8, 128)],
    )
    gathered = lax.all_to_all(chunk, ("gx", "gy"), 0, 0, tiled=True)
    (u3,) = run(
        k_whole, (gathered,), [(8, 32, 128)], [(3, 8, 32, 128), (4, 32, 128), (4, 32, 128)]
    )
    (u2,) = run(k_up2, (u3, g2, c2, s2, q2), [(16, 24, 128)], [(8, 24, 128)])
    (u1,) = run(
        k_up1, (u2, g1, c1, s1, q1), [(34, 40, 128)], [(16, 40, 128)] + [(34, 40, 128)] * 2
    )
    (out,) = run(
        k_up0,
        (u1, gm, cm, sm, q0, gw, cw, sw, qw),
        [(32, 32, 128)],
        [(18, 40, 128)] * 2 + [(38, 40, 128)] * 2 + small * 2,
    )
    return out


def solution(mesh):
    return jax.shard_map(
        shards,
        mesh=mesh,
        in_specs=(P("gz", "gx", "gy"),) * 3,
        out_specs=P("gz", "gx", "gy"),
        check_vma=False,
    )
```

```python
import math

import jax
import jax.numpy as jnp
from jax import lax
from jax.experimental import pallas as pl
from jax.experimental.pallas import tpu as pltpu
from jax.sharding import PartitionSpec as P

F32 = jnp.float32
VM = pl.BlockSpec(memory_space=pltpu.VMEM)
BF16 = jnp.bfloat16
COARSE_SWEEPS = 11
MICROSECONDS = dict(
    k_load=4.0,
    k_face_x=0.2,
    k_pack_own=1.0,
    k_face_y=0.6,
    k_assemble=1.0,
    k_spread=1.0,
    k_down0=2.0,
    k_coeff=2.0,
    k_down12=3.0,
    k_whole=2.0,
    k_up2=0.5,
    k_up1=1.5,
    k_up0=2.5,
)
A0, B0, U0 = 12, 8, 3
A1, U1 = 8, 2


def run(body, args, outs, scratch=()):
    words = sum(math.prod(s) for s in (*outs, *scratch)) + sum(a.size for a in args)
    return pl.pallas_call(
        body,
        out_shape=[jax.ShapeDtypeStruct(o, F32) for o in outs],
        in_specs=[VM] * len(args),
        out_specs=[VM] * len(outs),
        scratch_shapes=[pltpu.VMEM(s, F32) for s in scratch],
        compiler_params=pltpu.CompilerParams(vmem_limit_bytes=6 * words + (6 << 20)),
        cost_estimate=pl.CostEstimate(
            flops=0, transcendentals=0, bytes_accessed=int(3.5e6 * MICROSECONDS[body.__name__])
        ),
    )(*args)


def weights(level):
    wh = 0.25**level
    return wh, 2.0 * (0.25 * wh + 2.0 * wh)


def iota(shape, dim):
    return lax.broadcasted_iota(jnp.int32, shape, dim)


def lanes(v, shift):
    return pltpu.roll(v, shift % v.shape[-1], v.ndim - 1)


def rows(v, shift):
    return pltpu.roll(v, shift % v.shape[-2], v.ndim - 2)


def beside(v):
    return (rows(v, 1) + rows(v, -1)) + (lanes(v, 1) + lanes(v, -1))


def around(above, v, below):
    return 0.25 * (above + below) + beside(v)


def factors(s, k, level):
    wh, full = weights(level)
    diagonal = k + full * (s * s)
    sw = s * (0.8 / jnp.where(diagonal > 0.0, diagonal, 1.0))
    return sw, (wh * s) * sw


def unscale(v, s):
    inside = s > 0.0
    return jnp.where(inside, v / jnp.where(inside, s, 1.0), 0.0)


def dot(a, b):
    b = b.astype(BF16)
    high = a.astype(BF16)
    rest = a - high.astype(F32)
    middle = rest.astype(BF16)
    low = (rest - middle.astype(F32)).astype(BF16)
    terms = [jnp.dot(t, b, preferred_element_type=F32) for t in (high, middle, low)]
    return terms[0] + (terms[1] + terms[2])


def dot3(a, b):
    n, r, c = a.shape
    return dot(a.reshape(n * r, c), b).reshape(n, r, b.shape[1])


def blocks(first, count, size, body, unroll=1):
    def one(b, _):
        z = first + size * b
        body(z, pl.ds(z, size))
        return 0

    lax.fori_loop(0, count // size, one, 0, unroll=unroll)


def pair_sum(v):
    v = v.reshape(v.shape[0] // 2, 2, *v.shape[1:])
    return v[:, 0] + v[:, 1]


def select_matrix(shape, source_of, scale=1.0):
    i, o = iota(shape, 0), iota(shape, 1)
    return jnp.where(source_of(i, o), scale, 0.0).astype(F32)


def face_z(f, s, k):
    upper = lax.axis_index("gz") == 0
    first = jnp.where(upper, 29, 0)
    f, s, k = [lax.dynamic_slice_in_dim(v, first, 3, 0) for v in (f, s, k)]
    sw, c = factors(s, k, 0)
    near = [jnp.where(upper, v[1:], v[:2]) for v in (c, s)]
    return jnp.concatenate([sw * f, *near], axis=0)


def k_load(f, s, k, g, c, sk1, ps, pk):
    def one(z, at):
        sv, kv = s[at], k[at]
        sw, cv = factors(sv, kv, 0)
        g[at] = sw * f[at]
        c[at] = cv
        ps[pl.ds(z // 2, 2)] = pair_sum(sv)
        pk[pl.ds(z // 2, 2)] = pair_sum(kv)

    blocks(0, 32, 4, one, 2)
    a = ps[:, pl.ds(0, 16, 2), :] + ps[:, pl.ds(1, 16, 2), :]
    b = pk[:, pl.ds(0, 16, 2), :] + pk[:, pl.ds(1, 16, 2), :]
    left = select_matrix((128, 128), lambda i, o: i // 2 == o, 0.125)
    right = select_matrix((128, 128), lambda i, o: i // 2 == o - 64, 0.125)
    sk1[...] = dot3(a, left) + dot3(b, right)


def halo_rows(zr, iz, field, z):
    first, depth = ((0, 3), (3, 2), (5, 2))[field]
    d = z - 35 if z > 34 else 2 - z
    if d >= depth:
        return jnp.zeros(zr.shape[1:], F32)
    row = first + (d if z > 34 else depth - 1 - d)
    return jnp.where(iz == (0 if z > 34 else 1), zr[row], 0.0)


def k_face_x(g, c, s, zr, to_right, to_left):
    iz = lax.axis_index("gz")
    sub = iota((8, 128), 0)

    def put(z, gz, cz, sz):
        a, b, d = gz[24:32], cz[24:32], sz[24:32]
        to_right[z] = jnp.where(sub >= 5, a, jnp.where(sub >= 3, rows(b, -3), rows(d, -5)))
        a, b, d = gz[0:8], cz[0:8], sz[0:8]
        to_left[z] = jnp.where(sub < 3, a, jnp.where(sub < 5, rows(b, 3), rows(d, 5)))

    def one(z, _):
        put(z + 3, g[z], c[z], s[z])
        return 0

    lax.fori_loop(0, 32, one, 0, unroll=4)
    for z in (0, 1, 2, 35, 36, 37):
        put(z, *[halo_rows(zr, iz, n, z) for n in range(3)])


def k_pack_own(g, c, s, own):
    own[...] = jnp.zeros((5, 40, 128), F32)
    slot = iota((32, 128), 1)

    def pack(first, group, js):
        total = jnp.zeros((32, 128), F32)
        for j in js:
            z = first + j - js[0]
            total = jnp.where(slot >= 16 * j, lanes(g[z], 16 * j + 3), total)
            total = jnp.where(slot >= 16 * j + 6, lanes(c[z], 16 * j + 8), total)
            total = jnp.where(slot >= 16 * j + 10, lanes(s[z], 16 * j + 12), total)
        own[group, :32, :] = total

    pack(0, 0, range(3, 8))
    for group in range(1, 4):
        pack(8 * group - 3, group, range(8))
    pack(29, 4, range(3))


def side_rows(from_left, from_right, ix, z):
    sub = iota((8, 128), 0)
    lf = jnp.where(ix > 0, from_left[z], 0.0)
    rt = jnp.where(ix < 7, from_right[z], 0.0)
    return (
        jnp.where(sub >= 4, lf, rt),
        jnp.where(sub >= 4, rows(lf, 3), rows(rt, -3)),
        jnp.where(sub >= 4, rows(lf, 5), rows(rt, -5)),
    )


def slotted(total, slot, fields, j):
    for n, (lane, shift) in enumerate(((0, 3), (6, 8), (10, 12))):
        total = jnp.where(slot >= 16 * j + lane, lanes(fields[n], 16 * j + shift), total)
    return total


def k_face_y(own, zr, from_left, from_right, ymsg):
    ix, iz = lax.axis_index("gx"), lax.axis_index("gz")
    slot = iota((8, 128), 1)
    wide = iota((32, 128), 1)
    for group in range(5):
        side = jnp.zeros((8, 128), F32)
        for j in range(8 if group < 4 else 6):
            side = slotted(side, slot, side_rows(from_left, from_right, ix, group * 8 + j), j)
        mid = own[group, :32, :]
        if group == 0:
            edge = jnp.zeros((32, 128), F32)
            for j in range(3):
                edge = slotted(edge, wide, [halo_rows(zr, iz, n, j) for n in range(3)], j)
            mid = jnp.where(wide < 48, edge, mid)
        if group == 4:
            for j in range(3, 6):
                mid = slotted(mid, wide, [halo_rows(zr, iz, n, 32 + j) for n in range(3)], j)
        ymsg[group] = jnp.concatenate([mid, side], axis=0)


def k_assemble(g, c, s, zr, from_left, from_right, gm, cm, sm):
    ix, iz = lax.axis_index("gx"), lax.axis_index("gz")

    def put(z, values):
        for ref, mid, side in zip(
            (gm, cm, sm), values, side_rows(from_left, from_right, ix, z)
        ):
            ref[z] = jnp.concatenate([mid, side], axis=0)

    def one(z, _):
        put(z + 3, (g[z], c[z], s[z]))
        return 0

    lax.fori_loop(0, 32, one, 0, unroll=4)
    for z in (0, 1, 2, 35, 36, 37):
        put(z, [halo_rows(zr, iz, n, z) for n in range(3)])


def near_edges(v):
    lane = iota(v.shape, 2)
    zero = jnp.zeros((1,) + v.shape[1:], F32)
    up, down = lanes(v, 16), lanes(v, -16)
    above = jnp.where(lane < 16, jnp.concatenate([zero, up[:-1]], axis=0), up)
    below = jnp.where(lane >= 112, jnp.concatenate([down[1:], zero], axis=0), down)
    return around(above, v, below)


def joint(v):
    return jnp.where(iota(v.shape, 2) % 16 == 4, lanes(v, -6), v)


def near_main(ref, edge, z, n):
    v = ref[pl.ds(z, n)]
    lane = iota(v.shape, 2)
    e = jnp.stack(
        [
            pltpu.roll(edge[(z + i) // 8], (124 - 16 * ((z + i) % 8)) % 128, 1)
            for i in range(n)
        ]
    )
    across = jnp.where(lane == 0, e, lanes(v, 1)) + jnp.where(lane == 127, e, lanes(v, -1))
    above, below = ref[pl.ds(z - 1, n)], ref[pl.ds(z + 1, n)]
    return 0.25 * (above + below) + ((rows(v, 1) + rows(v, -1)) + across)


def near(ref, z, n):
    return around(ref[pl.ds(z - 1, n)], ref[pl.ds(z, n)], ref[pl.ds(z + 1, n)])


def k_down0(f, gm, cm, sm, own, from_left, from_right, gw, cw, sw, q, qw, f1, e, eg, eq):
    iy = lax.axis_index("gy")
    lane = iota((5, 40, 128), 2) % 16
    mid = own[...]
    lf = jnp.where(iy > 0, from_left[...], 0.0)
    rt = jnp.where(iy < 7, from_right[...], 0.0)

    def window(split, to_right, to_left):
        a = jnp.where(lane < split, mid, rt)
        b = jnp.where(lane < split, lf, mid)
        a = lanes(a, to_right) if to_right else a
        return jnp.where(lane < 8, a, lanes(b, to_left))

    g = window(3, 0, 8)
    c = window(8, -5, 3)
    gw[...] = g
    cw[...] = c
    sw[...] = window(12, -9, -1)
    w = 0.4 * g + c * near_edges(g)
    qw[...] = w
    eg[...] = joint(g)
    eq[...] = joint(w)
    q[0] = jnp.zeros((40, 128), F32)
    q[37] = jnp.zeros((40, 128), F32)

    def relax(z, at):
        q[at] = 0.4 * gm[at] + cm[at] * near_main(gm, eg, z, A0)

    blocks(1, 36, A0, relax, U0)

    def residual(z, at):
        v = 0.04 * f[pl.ds(z - 3, B0)] + sm[at, :32, :] * near_main(q, eq, z, B0)[:, :32]
        e[pl.ds((z - 3) // 2, B0 // 2)] = pair_sum(v)

    blocks(3, 32, B0, residual, U0)
    a = e[:, pl.ds(0, 16, 2), :] + e[:, pl.ds(1, 16, 2), :]
    lo = select_matrix((128, 128), lambda i, o: i // 2 == o, 0.125)
    hi = select_matrix((128, 128), lambda i, o: i // 2 == o - 64, 0.125)
    f1[...] = dot3(a[:8], lo) + dot3(a[8:], hi)


def k_spread(own, xl, xr, full, to_right, to_left):
    ix, iz = lax.axis_index("gx"), lax.axis_index("gz")
    sub = iota((8, 128), 0)
    lane = iota((40, 128), 1) % 64
    n = own.shape[0] // 2

    def one(z, _):
        for half in range(2):
            src = jnp.where(iz == half, 0, n) + z
            lf = jnp.where(ix > 0, xl[src], 0.0)
            rt = jnp.where(ix < 7, xr[src], 0.0)
            full[half * n + z] = jnp.concatenate(
                [own[src], rt[0:8], jnp.where(sub < 4, rt[8:16], lf[0:8]), lf[8:16]], axis=0
            )
        return 0

    lax.fori_loop(0, n, one, 0, unroll=2)

    def pack(group, _):
        a = lanes(full[group * 4], -52)
        b = full[group * 4]
        for j in range(1, 4):
            v = full[group * 4 + j]
            a = jnp.where(lane >= 16 * j, lanes(v, 16 * j - 52), a)
            b = jnp.where(lane >= 16 * j, lanes(v, 16 * j), b)
        to_right[group] = a
        to_left[group] = b
        return 0

    lax.fori_loop(0, n // 2, pack, 0)


def both(mid, lf, rt, j):
    lane = iota((40, 128), 1)
    rt, lf = lanes(rt, 64 - 16 * j), lanes(lf, 116 - 16 * j)
    first = jnp.where(lane < 64, mid, jnp.where(lane < 96, rt, lf))
    second = jnp.where(lane >= 64, mid, jnp.where(lane < 32, rt, lf))
    return first, lanes(second, 64)


def halve_x(ref, n, x2):
    x2[:, 14:18, :] = jnp.zeros((n, 4, 128), F32)
    x2[:, 0:14, :] = ref[:, pl.ds(0, 14, 2), :] + ref[:, pl.ds(1, 14, 2), :]
    x2[:, 18:24, :] = ref[:, pl.ds(28, 6, 2), :] + ref[:, pl.ds(29, 6, 2), :]
    return x2[...]


def down_matrix():
    return select_matrix(
        (128, 128),
        lambda i, o: ((i // 2 == o) & (o < 38)) | ((i // 2 == o - 64) & (o >= 122)),
        0.125,
    )


def level3_rows(v, e2):
    half = select_matrix((128, 128), lambda i, o: (i // 2 == o) & (o < 16), 0.125)
    v = v.reshape(8, 2, 24, 128)
    e2[...] = v[:, 0, :8, :] + v[:, 1, :8, :]
    pairs = e2[:, pl.ds(0, 4, 2), :] + e2[:, pl.ds(1, 4, 2), :]
    total = dot(pairs[0], half)
    for j in range(1, 8):
        total = total + lanes(dot(pairs[j], half), 16 * j)
    return total


def k_coeff(full, fl, fr, s1, c1, w1, s2, c2, w2, sk3, ps, pk, x2, e2):
    iy = lax.axis_index("gy")

    def unpack(group, _):
        lf = jnp.where(iy > 0, fl[group], 0.0)
        rt = jnp.where(iy < 7, fr[group], 0.0)
        sk = [both(full[group * 4 + j], lf, rt, j) for j in range(4)]
        fs = [factors(s, k, 1) for s, k in sk]
        for j in range(4):
            z = group * 4 + j
            s1[z] = sk[j][0]
            w1[z], c1[z] = fs[j]
        for j in range(2):
            ps[group * 2 + j] = sk[2 * j][0] + sk[2 * j + 1][0]
            pk[group * 2 + j] = sk[2 * j][1] + sk[2 * j + 1][1]
        return 0

    lax.fori_loop(0, 8, unpack, 0, unroll=2)
    down = down_matrix()
    s = dot3(halve_x(ps, 16, x2), down)
    k = dot3(halve_x(pk, 16, x2), down)
    s2[...] = s
    w2[...], c2[...] = factors(s, k, 2)
    sk3[...] = jnp.concatenate([level3_rows(s, e2), level3_rows(k, e2)], axis=0)


def k_down12(
    full, fl, fr, s1, c1, w1, s2, c2, w2, sk3, g, q, g2, q2, chunk, f, e, x2, e2
):
    iy = lax.axis_index("gy")
    for ref in (g, q):
        ref[0] = jnp.zeros((40, 128), F32)
        ref[33] = jnp.zeros((40, 128), F32)

    def unpack(group, _):
        lf = jnp.where(iy > 0, fl[group], 0.0)
        rt = jnp.where(iy < 7, fr[group], 0.0)
        parts = [both(full[group * 4 + j], lf, rt, j) for j in range(4)]
        first = group * 4 + 8 * (group // 2)
        for i in range(2):
            v = jnp.stack([p[i] for p in parts])
            w = w1[pl.ds(first + 8 * i, 4)] * v
            f[pl.ds(first + 8 * i, 4)] = v
            g[pl.ds(first + 8 * i + 1, 4)] = w
        return 0

    lax.fori_loop(0, 4, unpack, 0, unroll=2)

    def relax(z, at):
        q[at] = 0.4 * g[at] + c1[pl.ds(z - 1, A1)] * near(g, z, A1)

    blocks(1, 32, A1, relax, U1)
    wh, _ = weights(1)

    def residual(z, at):
        own = pl.ds(z - 1, A1)
        v = 0.04 * f[own] + (wh * s1[own]) * near(q, z, A1)
        e[pl.ds((z - 1) // 2, A1 // 2)] = pair_sum(v)

    blocks(1, 32, A1, residual, U1)
    fv = dot3(halve_x(e, 16, x2), down_matrix())
    gv = w2[...] * fv
    zero = jnp.zeros((1, 24, 128), F32)

    def spread(v):
        w = jnp.concatenate([zero, v, zero], axis=0)
        return around(w[:16], v, w[2:])

    qv = 0.4 * gv + c2[...] * spread(gv)
    wh, _ = weights(2)
    ev = 0.04 * fv + (wh * s2[...]) * spread(qv)
    g2[...] = gv
    q2[...] = qv
    block = jnp.concatenate([level3_rows(ev, e2), sk3[...], jnp.zeros((4, 128), F32)], axis=0)
    block = pltpu.roll(block, 16 * iy, 1)

    def copy(n, _):
        chunk[n] = block
        return 0

    lax.fori_loop(0, 64, copy, 0, unroll=8)


def spread_in(shape, last):
    n, r, _ = shape
    row, col = iota(shape, 1), iota(shape, 2)
    zero = jnp.zeros((1,) + shape[1:], F32)

    def apply(v):
        w = jnp.concatenate([zero, v, zero], axis=0)
        x = jnp.where(row > 0, rows(v, 1), 0.0) + jnp.where(row < r - 1, rows(v, -1), 0.0)
        y = jnp.where(col > 0, lanes(v, 1), 0.0) + jnp.where(col < last, lanes(v, -1), 0.0)
        return 0.25 * (w[:n] + w[2:]) + x + y

    return apply


def k_whole(gathered, u, t3, x4, p3):
    ix, iy = lax.axis_index("gx"), lax.axis_index("gy")
    lane = iota((8, 128), 1) // 16
    sub = iota((8, 128), 0)
    for j in range(8):
        for t in range(2):
            tiles = []
            for x in range(8):
                v = gathered[x * 8, 8 * t : 8 * t + 8, :]
                for y in range(1, 8):
                    v = jnp.where(lane == (j + y) % 8, gathered[x * 8 + y, 8 * t : 8 * t + 8, :], v)
                tiles.append(lanes(v, -16 * j) if j else v)
            for x in range(4):
                a, b = tiles[2 * x], tiles[2 * x + 1]
                t3[2 * t, j, 8 * x : 8 * x + 8, :] = jnp.where(sub < 4, a, rows(b, 4))
                if t == 0:
                    t3[1, j, 8 * x : 8 * x + 8, :] = jnp.where(sub < 4, rows(a, 4), b)
    f3, s3, k3 = t3[0], t3[1], t3[2]
    near3 = spread_in((8, 32, 128), 127)
    w3, c3 = factors(s3, k3, 3)
    g3 = w3 * f3
    q3 = 0.4 * g3 + c3 * near3(g3)
    e3 = 0.04 * f3 + (weights(3)[0] * s3) * near3(q3)
    half = select_matrix((128, 128), lambda i, o: i // 2 == o, 0.125)
    fields = []
    for v in (e3, s3, k3):
        w = v.reshape(4, 2, 32, 128)
        x4[...] = w[:, 0] + w[:, 1]
        fields.append(dot3(x4[:, pl.ds(0, 16, 2), :] + x4[:, pl.ds(1, 16, 2), :], half))
    f4, s4, k4 = fields
    near4 = spread_in((4, 16, 128), 63)
    w4, c4 = factors(s4, k4, 4)
    g4 = w4 * f4
    v4 = g4
    for _ in range(COARSE_SWEEPS):
        v4 = (0.2 * v4 + g4) + c4 * near4(v4)
    u4 = dot3(unscale(v4, s4), select_matrix((128, 128), lambda i, o: i == o // 2))
    p3[:, pl.ds(0, 16, 2), :] = u4
    p3[:, pl.ds(1, 16, 2), :] = u4
    w = p3[...]
    w = jnp.broadcast_to(w[:, None], (4, 2, 32, 128)).reshape(8, 32, 128)
    v3 = (q3 + 0.8 * g3) + s3 * w
    for _ in range(2):
        v3 = (0.2 * v3 + g3) + c3 * near3(v3)
    pick = select_matrix(
        (128, 128),
        lambda i, o: i == (jnp.where(o < 64, o // 2, 127 - (127 - o) // 2) + 16 * iy) % 128,
    )
    u[...] = pltpu.roll(dot3(v3 / s3, pick), (32 - 4 * ix) % 32, 1)


def k_up2(u3, g2, c2, s2, q2, u, p2):
    p2[:, 14:18, :] = jnp.zeros((8, 4, 128), F32)
    for n in range(2):
        p2[:, pl.ds(n, 7, 2), :] = u3[:, 0:7, :]
        p2[:, pl.ds(18 + n, 3, 2), :] = u3[:, 29:32, :]
    w = p2[...]
    w = jnp.broadcast_to(w[:, None], (8, 2, 24, 128)).reshape(16, 24, 128)
    gv, cv, sv = g2[...], c2[...], s2[...]
    zero = jnp.zeros((1, 24, 128), F32)
    v = (q2[...] + 0.8 * gv) + sv * w
    for _ in range(2):
        w = jnp.concatenate([zero, v, zero], axis=0)
        v = (0.2 * v + gv) + cv * around(w[:16], v, w[2:])
    pick = select_matrix(
        (128, 128),
        lambda i, o: i == jnp.where(o < 96, o // 2, 127 - (127 - o) // 2),
    )
    u[...] = dot3(unscale(v, sv), pick)


def k_up1(u2, g1, c1, s1, q1, u, p1, va, vb):
    for n in range(2):
        p1[:, pl.ds(n, 14, 2), :] = u2[:, 0:14, :]
        p1[:, pl.ds(28 + n, 6, 2), :] = u2[:, 18:24, :]
    for ref in (va, vb, u):
        ref[0] = jnp.zeros((40, 128), F32)
        ref[33] = jnp.zeros((40, 128), F32)

    def start(z, at):
        t = p1[pl.ds((z - 1) // 2, A1 // 2)]
        t = jnp.broadcast_to(t[:, None], (A1 // 2, 2, 40, 128)).reshape(A1, 40, 128)
        va[at] = (q1[at] + 0.8 * g1[at]) + s1[pl.ds(z - 1, A1)] * t

    blocks(1, 32, A1, start, U1)

    def sweep(z, at):
        vb[at] = (0.2 * va[at] + g1[at]) + c1[pl.ds(z - 1, A1)] * near(va, z, A1)

    blocks(1, 32, A1, sweep, U1)

    def last(z, at):
        own = pl.ds(z - 1, A1)
        v = (0.2 * vb[at] + g1[at]) + c1[own] * near(vb, z, A1)
        u[at] = unscale(v, s1[own])

    blocks(1, 32, A1, last, U1)


def k_up0(u1, gm, cm, sm, q, gw, cw, sw, qw, out, pm, pw, wa, wb, ea, eb):
    iz = lax.axis_index("gz")

    def source(i, o):
        y = jnp.where(o % 16 < 8, 125 + o % 16, o % 16 - 11)
        return i == jnp.where(o < 128, o // 2, ((y + 256) // 2) % 128)

    u = u1[pl.ds(16 * iz, 18)]
    sub = iota((18, 8, 128), 1)
    u = jnp.concatenate([u[:, :16], jnp.where(sub < 4, u[:, 16:24], u[:, 32:40])], axis=1)
    u = dot3(u, select_matrix((128, 256), source))
    for h, ref in enumerate((pm, pw)):
        w = u[:, :, 128 * h : 128 * h + 128]
        for n in range(2):
            ref[:, pl.ds(n, 18, 2), :] = w[:, 0:18]
            ref[:, pl.ds(36 + n, 2, 2), :] = w[:, 22:24]
    slot = iota((40, 128), 1) // 16
    parts = []
    for group in range(5):
        total = None
        for j in range(8):
            part = pw[min(max((8 * group + j - 1) // 2, 0), 17)]
            total = part if total is None else jnp.where(slot >= j, part, total)
        parts.append(total[None])
    g, c = gw[...], cw[...]
    v = (qw[...] + 0.8 * g) + sw[...] * jnp.concatenate(parts, axis=0)
    ea[...] = joint(v)
    eb[...] = joint((0.2 * v + g) + c * near_edges(v))

    def start(z, at):
        t = jnp.stack([pm[(z + i - 1) // 2] for i in range(A0)])
        wa[at] = (q[at] + 0.8 * gm[at]) + sm[at] * t

    blocks(1, 36, A0, start, U0)
    wa[0] = jnp.zeros((40, 128), F32)
    wa[37] = jnp.zeros((40, 128), F32)

    def sweep(z, at):
        wb[at] = (0.2 * wa[at] + gm[at]) + cm[at] * near_main(wa, ea, z, A0)

    blocks(1, 36, A0, sweep, U0)

    def last(z, at):
        n = near_main(wb, eb, z, B0)[:, :32]
        v = (0.2 * wb[at, :32, :] + gm[at, :32, :]) + cm[at, :32, :] * n
        out[pl.ds(z - 3, B0)] = v / sm[at, :32, :]

    blocks(3, 32, B0, last, U0)


def ring(v, axis, step):
    n = lax.axis_size(axis)
    return lax.ppermute(v, axis, [(i, (i + step) % n) for i in range(n)])


def pair(to_right, to_left, axis):
    return ring(to_right, axis, 1), ring(to_left, axis, -1)


def after(values, *others):
    return lax.optimization_barrier((values, others))[0]


def shards(f, s, k):
    zr = ring(face_z(f, s, k), "gz", 1)
    g, c, sk1 = run(
        k_load, (f, s, k), [(32, 32, 128)] * 2 + [(16, 16, 128)], [(16, 32, 128)] * 2
    )
    sk1 = after(sk1, zr)
    sk_all = jnp.concatenate([sk1, ring(sk1, "gz", 1)], axis=0)
    xs = pair(*run(k_face_x, (g, c, s, zr), [(38, 8, 128)] * 2), "gx")
    (edges,) = run(k_pack_own, (g, c, s), [(5, 40, 128)])
    sk_x = pair(sk_all, sk_all, "gx")
    (ymsg,) = run(k_face_y, (edges, zr, *xs), [(5, 40, 128)])
    ys = pair(ymsg, ymsg, "gy")
    gm, cm, sm = run(k_assemble, (g, c, s, zr, *xs), [(38, 40, 128)] * 3)
    sk_full, *sk_y = run(k_spread, (sk_all, *sk_x), [(32, 40, 128)] + [(8, 40, 128)] * 2)
    sk_y = pair(*sk_y, "gy")
    small = [(5, 40, 128)]
    gw, cw, sw, q0, qw, f1 = run(
        k_down0,
        (f, gm, cm, sm, ymsg, *ys),
        small * 3 + [(38, 40, 128)] + small + [(8, 16, 128)],
        [(16, 32, 128)] + small * 2,
    )
    f1 = after(jnp.concatenate([f1, ring(f1, "gz", 1)], axis=0), sk_full)
    s1, c1, w1, s2, c2, w2, sk3 = run(
        k_coeff,
        (sk_full, *sk_y),
        [(32, 40, 128)] * 3 + [(16, 24, 128)] * 3 + [(8, 128)],
        [(16, 40, 128)] * 2 + [(16, 24, 128), (8, 8, 128)],
    )
    f1_full, *f1_y = run(
        k_spread, (f1, *pair(f1, f1, "gx")), [(16, 40, 128)] + [(4, 40, 128)] * 2
    )
    g1, q1, g2, q2, chunk = run(
        k_down12,
        (f1_full, *pair(*f1_y, "gy"), s1, c1, w1, s2, c2, w2, sk3),
        [(34, 40, 128)] * 2 + [(16, 24, 128)] * 2 + [(64, 16, 128)],
        [(32, 40, 128), (16, 40, 128), (16, 24, 128), (8, 8, 128)],
    )
    gathered = lax.all_to_all(chunk, ("gx", "gy"), 0, 0, tiled=True)
    (u3,) = run(
        k_whole, (gathered,), [(8, 32, 128)], [(3, 8, 32, 128), (4, 32, 128), (4, 32, 128)]
    )
    (u2,) = run(k_up2, (u3, g2, c2, s2, q2), [(16, 24, 128)], [(8, 24, 128)])
    (u1,) = run(
        k_up1, (u2, g1, c1, s1, q1), [(34, 40, 128)], [(16, 40, 128)] + [(34, 40, 128)] * 2
    )
    (out,) = run(
        k_up0,
        (u1, gm, cm, sm, q0, gw, cw, sw, qw),
        [(32, 32, 128)],
        [(18, 40, 128)] * 2 + [(38, 40, 128)] * 2 + small * 2,
    )
    return out


def solution(mesh):
    return jax.shard_map(
        shards,
        mesh=mesh,
        in_specs=(P("gz", "gx", "gy"),) * 3,
        out_specs=P("gz", "gx", "gy"),
        check_vma=False,
    )
```

```python
import math

import jax
import jax.numpy as jnp
from jax import lax
from jax.experimental import pallas as pl
from jax.experimental.pallas import tpu as pltpu
from jax.sharding import PartitionSpec as P

F32 = jnp.float32
VM = pl.BlockSpec(memory_space=pltpu.VMEM)
BF16 = jnp.bfloat16
COARSE_SWEEPS = 11
MICROSECONDS = dict(
    k_load=4.0,
    k_face_x=0.2,
    k_pack_own=1.0,
    k_face_y=0.6,
    k_assemble=1.0,
    k_spread=1.0,
    k_down0=2.0,
    k_coeff=2.0,
    k_down12=3.0,
    k_whole=2.0,
    k_up2=0.5,
    k_up1=1.5,
    k_up0=2.5,
)
A0, B0, U0 = 12, 8, 3
A1, U1 = 8, 2


def run(body, args, outs, scratch=()):
    words = sum(math.prod(s) for s in (*outs, *scratch)) + sum(a.size for a in args)
    return pl.pallas_call(
        body,
        out_shape=[jax.ShapeDtypeStruct(o, F32) for o in outs],
        in_specs=[VM] * len(args),
        out_specs=[VM] * len(outs),
        scratch_shapes=[pltpu.VMEM(s, F32) for s in scratch],
        compiler_params=pltpu.CompilerParams(vmem_limit_bytes=6 * words + (6 << 20)),
        cost_estimate=pl.CostEstimate(
            flops=0, transcendentals=0, bytes_accessed=int(3.5e6 * MICROSECONDS[body.__name__])
        ),
    )(*args)


def weights(level):
    wh = 0.25**level
    return wh, 2.0 * (0.25 * wh + 2.0 * wh)


def iota(shape, dim):
    return lax.broadcasted_iota(jnp.int32, shape, dim)


def lanes(v, shift):
    return pltpu.roll(v, shift % v.shape[-1], v.ndim - 1)


def rows(v, shift):
    return pltpu.roll(v, shift % v.shape[-2], v.ndim - 2)


def beside(v):
    return (rows(v, 1) + rows(v, -1)) + (lanes(v, 1) + lanes(v, -1))


def around(above, v, below):
    return 0.25 * (above + below) + beside(v)


def factors(s, k, level):
    wh, full = weights(level)
    diagonal = k + full * (s * s)
    sw = s * (0.8 / jnp.where(diagonal > 0.0, diagonal, 1.0))
    return sw, (wh * s) * sw


def unscale(v, s):
    inside = s > 0.0
    return jnp.where(inside, v / jnp.where(inside, s, 1.0), 0.0)


def dot(a, b):
    b = b.astype(BF16)
    high = a.astype(BF16)
    rest = a - high.astype(F32)
    middle = rest.astype(BF16)
    low = (rest - middle.astype(F32)).astype(BF16)
    terms = [jnp.dot(t, b, preferred_element_type=F32) for t in (high, middle, low)]
    return terms[0] + (terms[1] + terms[2])


def dot3(a, b):
    n, r, c = a.shape
    return dot(a.reshape(n * r, c), b).reshape(n, r, b.shape[1])


def blocks(first, count, size, body, unroll=1):
    def one(b, _):
        z = first + size * b
        body(z, pl.ds(z, size))
        return 0

    lax.fori_loop(0, count // size, one, 0, unroll=unroll)


def pair_sum(v):
    v = v.reshape(v.shape[0] // 2, 2, *v.shape[1:])
    return v[:, 0] + v[:, 1]


def select_matrix(shape, source_of, scale=1.0):
    i, o = iota(shape, 0), iota(shape, 1)
    return jnp.where(source_of(i, o), scale, 0.0).astype(F32)


def face_z(f, s, k):
    upper = lax.axis_index("gz") == 0
    first = jnp.where(upper, 29, 0)
    f, s, k = [lax.dynamic_slice_in_dim(v, first, 3, 0) for v in (f, s, k)]
    sw, c = factors(s, k, 0)
    near = [jnp.where(upper, v[1:], v[:2]) for v in (c, s)]
    return jnp.concatenate([sw * f, *near], axis=0)


def k_load(f, s, k, g, c, sk1, ps, pk):
    def one(z, at):
        sv, kv = s[at], k[at]
        sw, cv = factors(sv, kv, 0)
        g[at] = sw * f[at]
        c[at] = cv
        ps[pl.ds(z // 2, 2)] = pair_sum(sv)
        pk[pl.ds(z // 2, 2)] = pair_sum(kv)

    blocks(0, 32, 4, one, 2)
    a = ps[:, pl.ds(0, 16, 2), :] + ps[:, pl.ds(1, 16, 2), :]
    b = pk[:, pl.ds(0, 16, 2), :] + pk[:, pl.ds(1, 16, 2), :]
    left = select_matrix((128, 128), lambda i, o: i // 2 == o, 0.125)
    right = select_matrix((128, 128), lambda i, o: i // 2 == o - 64, 0.125)
    sk1[...] = dot3(a, left) + dot3(b, right)


def halo_rows(zr, iz, field, z):
    first, depth = ((0, 3), (3, 2), (5, 2))[field]
    d = z - 35 if z > 34 else 2 - z
    if d >= depth:
        return jnp.zeros(zr.shape[1:], F32)
    row = first + (d if z > 34 else depth - 1 - d)
    return jnp.where(iz == (0 if z > 34 else 1), zr[row], 0.0)


def k_face_x(g, c, s, zr, to_right, to_left):
    iz = lax.axis_index("gz")
    sub = iota((8, 128), 0)

    def put(z, gz, cz, sz):
        a, b, d = gz[24:32], cz[24:32], sz[24:32]
        to_right[z] = jnp.where(sub >= 5, a, jnp.where(sub >= 3, rows(b, -3), rows(d, -5)))
        a, b, d = gz[0:8], cz[0:8], sz[0:8]
        to_left[z] = jnp.where(sub < 3, a, jnp.where(sub < 5, rows(b, 3), rows(d, 5)))

    def one(z, _):
        put(z + 3, g[z], c[z], s[z])
        return 0

    lax.fori_loop(0, 32, one, 0, unroll=4)
    for z in (0, 1, 2, 35, 36, 37):
        put(z, *[halo_rows(zr, iz, n, z) for n in range(3)])


def k_pack_own(g, c, s, own):
    own[...] = jnp.zeros((5, 40, 128), F32)
    slot = iota((32, 128), 1)

    def pack(first, group, js):
        total = jnp.zeros((32, 128), F32)
        for j in js:
            z = first + j - js[0]
            total = jnp.where(slot >= 16 * j, lanes(g[z], 16 * j + 3), total)
            total = jnp.where(slot >= 16 * j + 6, lanes(c[z], 16 * j + 8), total)
            total = jnp.where(slot >= 16 * j + 10, lanes(s[z], 16 * j + 12), total)
        own[group, :32, :] = total

    pack(0, 0, range(3, 8))
    for group in range(1, 4):
        pack(8 * group - 3, group, range(8))
    pack(29, 4, range(3))


def side_rows(from_left, from_right, ix, z):
    sub = iota((8, 128), 0)
    lf = jnp.where(ix > 0, from_left[z], 0.0)
    rt = jnp.where(ix < 7, from_right[z], 0.0)
    return (
        jnp.where(sub >= 4, lf, rt),
        jnp.where(sub >= 4, rows(lf, 3), rows(rt, -3)),
        jnp.where(sub >= 4, rows(lf, 5), rows(rt, -5)),
    )


def slotted(total, slot, fields, j):
    for n, (lane, shift) in enumerate(((0, 3), (6, 8), (10, 12))):
        total = jnp.where(slot >= 16 * j + lane, lanes(fields[n], 16 * j + shift), total)
    return total


def k_face_y(own, zr, from_left, from_right, ymsg):
    ix, iz = lax.axis_index("gx"), lax.axis_index("gz")
    slot = iota((8, 128), 1)
    wide = iota((32, 128), 1)
    for group in range(5):
        side = jnp.zeros((8, 128), F32)
        for j in range(8 if group < 4 else 6):
            side = slotted(side, slot, side_rows(from_left, from_right, ix, group * 8 + j), j)
        mid = own[group, :32, :]
        if group == 0:
            edge = jnp.zeros((32, 128), F32)
            for j in range(3):
                edge = slotted(edge, wide, [halo_rows(zr, iz, n, j) for n in range(3)], j)
            mid = jnp.where(wide < 48, edge, mid)
        if group == 4:
            for j in range(3, 6):
                mid = slotted(mid, wide, [halo_rows(zr, iz, n, 32 + j) for n in range(3)], j)
        ymsg[group] = jnp.concatenate([mid, side], axis=0)


def k_assemble(g, c, s, zr, from_left, from_right, gm, cm, sm):
    ix, iz = lax.axis_index("gx"), lax.axis_index("gz")

    def put(z, values):
        for ref, mid, side in zip(
            (gm, cm, sm), values, side_rows(from_left, from_right, ix, z)
        ):
            ref[z] = jnp.concatenate([mid, side], axis=0)

    def one(z, _):
        put(z + 3, (g[z], c[z], s[z]))
        return 0

    lax.fori_loop(0, 32, one, 0, unroll=4)
    for z in (0, 1, 2, 35, 36, 37):
        put(z, [halo_rows(zr, iz, n, z) for n in range(3)])


def near_edges(v):
    lane = iota(v.shape, 2)
    zero = jnp.zeros((1,) + v.shape[1:], F32)
    up, down = lanes(v, 16), lanes(v, -16)
    above = jnp.where(lane < 16, jnp.concatenate([zero, up[:-1]], axis=0), up)
    below = jnp.where(lane >= 112, jnp.concatenate([down[1:], zero], axis=0), down)
    return around(above, v, below)


def joint(v):
    return jnp.where(iota(v.shape, 2) % 16 == 4, lanes(v, -6), v)


def near_main(ref, edge, z, n):
    v = ref[pl.ds(z, n)]
    lane = iota(v.shape, 2)
    e = jnp.stack(
        [
            pltpu.roll(edge[(z + i) // 8], (124 - 16 * ((z + i) % 8)) % 128, 1)
            for i in range(n)
        ]
    )
    across = jnp.where(lane == 0, e, lanes(v, 1)) + jnp.where(lane == 127, e, lanes(v, -1))
    above, below = ref[pl.ds(z - 1, n)], ref[pl.ds(z + 1, n)]
    return 0.25 * (above + below) + ((rows(v, 1) + rows(v, -1)) + across)


def near(ref, z, n):
    return around(ref[pl.ds(z - 1, n)], ref[pl.ds(z, n)], ref[pl.ds(z + 1, n)])


def k_down0(f, gm, cm, sm, own, from_left, from_right, gw, cw, sw, q, qw, f1, e, eg, eq):
    iy = lax.axis_index("gy")
    lane = iota((5, 40, 128), 2) % 16
    mid = own[...]
    lf = jnp.where(iy > 0, from_left[...], 0.0)
    rt = jnp.where(iy < 7, from_right[...], 0.0)

    def window(split, to_right, to_left):
        a = jnp.where(lane < split, mid, rt)
        b = jnp.where(lane < split, lf, mid)
        a = lanes(a, to_right) if to_right else a
        return jnp.where(lane < 8, a, lanes(b, to_left))

    g = window(3, 0, 8)
    c = window(8, -5, 3)
    gw[...] = g
    cw[...] = c
    sw[...] = window(12, -9, -1)
    w = 0.4 * g + c * near_edges(g)
    qw[...] = w
    eg[...] = joint(g)
    eq[...] = joint(w)
    q[0] = jnp.zeros((40, 128), F32)
    q[37] = jnp.zeros((40, 128), F32)

    def relax(z, at):
        q[at] = 0.4 * gm[at] + cm[at] * near_main(gm, eg, z, A0)

    blocks(1, 36, A0, relax, U0)

    def residual(z, at):
        v = 0.04 * f[pl.ds(z - 3, B0)] + sm[at, :32, :] * near_main(q, eq, z, B0)[:, :32]
        e[pl.ds((z - 3) // 2, B0 // 2)] = pair_sum(v)

    blocks(3, 32, B0, residual, U0)
    a = e[:, pl.ds(0, 16, 2), :] + e[:, pl.ds(1, 16, 2), :]
    lo = select_matrix((128, 128), lambda i, o: i // 2 == o, 0.125)
    hi = select_matrix((128, 128), lambda i, o: i // 2 == o - 64, 0.125)
    f1[...] = dot3(a[:8], lo) + dot3(a[8:], hi)


def k_spread(own, xl, xr, full, to_right, to_left):
    ix, iz = lax.axis_index("gx"), lax.axis_index("gz")
    sub = iota((4, 8, 128), 1)
    lane = iota((40, 128), 1) % 64
    n = own.shape[0] // 2

    def one(z, at):
        src = pl.ds(z + jnp.where(z < n, 0, -n) + jnp.where((iz == 0) == (z < n), 0, n), 4)
        lf = jnp.where(ix > 0, xl[src], 0.0)
        rt = jnp.where(ix < 7, xr[src], 0.0)
        v = jnp.concatenate(
            [own[src], rt[:, 0:8], jnp.where(sub < 4, rt[:, 8:16], lf[:, 0:8]), lf[:, 8:16]],
            axis=1,
        )
        full[at] = v
        a = lanes(v[0], -52)
        b = v[0]
        for j in range(1, 4):
            a = jnp.where(lane >= 16 * j, lanes(v[j], 16 * j - 52), a)
            b = jnp.where(lane >= 16 * j, lanes(v[j], 16 * j), b)
        to_right[z // 4] = a
        to_left[z // 4] = b

    blocks(0, 2 * n, 4, one, 2)


def both(mid, lf, rt, j):
    lane = iota((40, 128), 1)
    rt, lf = lanes(rt, 64 - 16 * j), lanes(lf, 116 - 16 * j)
    first = jnp.where(lane < 64, mid, jnp.where(lane < 96, rt, lf))
    second = jnp.where(lane >= 64, mid, jnp.where(lane < 32, rt, lf))
    return first, lanes(second, 64)


def halve_x(ref, n, x2):
    x2[:, 14:18, :] = jnp.zeros((n, 4, 128), F32)
    x2[:, 0:14, :] = ref[:, pl.ds(0, 14, 2), :] + ref[:, pl.ds(1, 14, 2), :]
    x2[:, 18:24, :] = ref[:, pl.ds(28, 6, 2), :] + ref[:, pl.ds(29, 6, 2), :]
    return x2[...]


def down_matrix():
    return select_matrix(
        (128, 128),
        lambda i, o: ((i // 2 == o) & (o < 38)) | ((i // 2 == o - 64) & (o >= 122)),
        0.125,
    )


def level3_rows(v, e2):
    half = select_matrix((128, 128), lambda i, o: (i // 2 == o) & (o < 16), 0.125)
    v = v.reshape(8, 2, 24, 128)
    e2[...] = v[:, 0, :8, :] + v[:, 1, :8, :]
    pairs = e2[:, pl.ds(0, 4, 2), :] + e2[:, pl.ds(1, 4, 2), :]
    total = dot(pairs[0], half)
    for j in range(1, 8):
        total = total + lanes(dot(pairs[j], half), 16 * j)
    return total


def k_coeff(full, fl, fr, s1, c1, w1, s2, c2, w2, sk3, ps, pk, x2, e2):
    iy = lax.axis_index("gy")

    def unpack(group, _):
        lf = jnp.where(iy > 0, fl[group], 0.0)
        rt = jnp.where(iy < 7, fr[group], 0.0)
        sk = [both(full[group * 4 + j], lf, rt, j) for j in range(4)]
        fs = [factors(s, k, 1) for s, k in sk]
        for j in range(4):
            z = group * 4 + j
            s1[z] = sk[j][0]
            w1[z], c1[z] = fs[j]
        for j in range(2):
            ps[group * 2 + j] = sk[2 * j][0] + sk[2 * j + 1][0]
            pk[group * 2 + j] = sk[2 * j][1] + sk[2 * j + 1][1]
        return 0

    lax.fori_loop(0, 8, unpack, 0, unroll=2)
    down = down_matrix()
    s = dot3(halve_x(ps, 16, x2), down)
    k = dot3(halve_x(pk, 16, x2), down)
    s2[...] = s
    w2[...], c2[...] = factors(s, k, 2)
    sk3[...] = jnp.concatenate([level3_rows(s, e2), level3_rows(k, e2)], axis=0)


def k_down12(
    full, fl, fr, s1, c1, w1, s2, c2, w2, sk3, g, q, g2, q2, chunk, f, e, x2, e2
):
    iy = lax.axis_index("gy")
    for ref in (g, q):
        ref[0] = jnp.zeros((40, 128), F32)
        ref[33] = jnp.zeros((40, 128), F32)

    def unpack(group, _):
        lf = jnp.where(iy > 0, fl[group], 0.0)
        rt = jnp.where(iy < 7, fr[group], 0.0)
        parts = [both(full[group * 4 + j], lf, rt, j) for j in range(4)]
        first = group * 4 + 8 * (group // 2)
        for i in range(2):
            v = jnp.stack([p[i] for p in parts])
            w = w1[pl.ds(first + 8 * i, 4)] * v
            f[pl.ds(first + 8 * i, 4)] = v
            g[pl.ds(first + 8 * i + 1, 4)] = w
        return 0

    lax.fori_loop(0, 4, unpack, 0, unroll=2)

    def relax(z, at):
        q[at] = 0.4 * g[at] + c1[pl.ds(z - 1, A1)] * near(g, z, A1)

    blocks(1, 32, A1, relax, U1)
    wh, _ = weights(1)

    def residual(z, at):
        own = pl.ds(z - 1, A1)
        v = 0.04 * f[own] + (wh * s1[own]) * near(q, z, A1)
        e[pl.ds((z - 1) // 2, A1 // 2)] = pair_sum(v)

    blocks(1, 32, A1, residual, U1)
    fv = dot3(halve_x(e, 16, x2), down_matrix())
    gv = w2[...] * fv
    zero = jnp.zeros((1, 24, 128), F32)

    def spread(v):
        w = jnp.concatenate([zero, v, zero], axis=0)
        return around(w[:16], v, w[2:])

    qv = 0.4 * gv + c2[...] * spread(gv)
    wh, _ = weights(2)
    ev = 0.04 * fv + (wh * s2[...]) * spread(qv)
    g2[...] = gv
    q2[...] = qv
    block = jnp.concatenate([level3_rows(ev, e2), sk3[...], jnp.zeros((4, 128), F32)], axis=0)
    block = pltpu.roll(block, 16 * iy, 1)

    def copy(n, _):
        chunk[n] = block
        return 0

    lax.fori_loop(0, 64, copy, 0, unroll=8)


def spread_in(shape, last):
    n, r, _ = shape
    row, col = iota(shape, 1), iota(shape, 2)
    zero = jnp.zeros((1,) + shape[1:], F32)

    def apply(v):
        w = jnp.concatenate([zero, v, zero], axis=0)
        x = jnp.where(row > 0, rows(v, 1), 0.0) + jnp.where(row < r - 1, rows(v, -1), 0.0)
        y = jnp.where(col > 0, lanes(v, 1), 0.0) + jnp.where(col < last, lanes(v, -1), 0.0)
        return 0.25 * (w[:n] + w[2:]) + x + y

    return apply


def k_whole(gathered, u, t3, x4, p3):
    ix, iy = lax.axis_index("gx"), lax.axis_index("gy")
    lane = iota((8, 128), 1) // 16
    sub = iota((8, 128), 0)
    for j in range(8):
        for t in range(2):
            tiles = []
            for x in range(8):
                v = gathered[x * 8, 8 * t : 8 * t + 8, :]
                for y in range(1, 8):
                    v = jnp.where(lane == (j + y) % 8, gathered[x * 8 + y, 8 * t : 8 * t + 8, :], v)
                tiles.append(lanes(v, -16 * j) if j else v)
            for x in range(4):
                a, b = tiles[2 * x], tiles[2 * x + 1]
                t3[2 * t, j, 8 * x : 8 * x + 8, :] = jnp.where(sub < 4, a, rows(b, 4))
                if t == 0:
                    t3[1, j, 8 * x : 8 * x + 8, :] = jnp.where(sub < 4, rows(a, 4), b)
    f3, s3, k3 = t3[0], t3[1], t3[2]
    near3 = spread_in((8, 32, 128), 127)
    w3, c3 = factors(s3, k3, 3)
    g3 = w3 * f3
    q3 = 0.4 * g3 + c3 * near3(g3)
    e3 = 0.04 * f3 + (weights(3)[0] * s3) * near3(q3)
    half = select_matrix((128, 128), lambda i, o: i // 2 == o, 0.125)
    fields = []
    for v in (e3, s3, k3):
        w = v.reshape(4, 2, 32, 128)
        x4[...] = w[:, 0] + w[:, 1]
        fields.append(dot3(x4[:, pl.ds(0, 16, 2), :] + x4[:, pl.ds(1, 16, 2), :], half))
    f4, s4, k4 = fields
    near4 = spread_in((4, 16, 128), 63)
    w4, c4 = factors(s4, k4, 4)
    g4 = w4 * f4
    v4 = g4
    for _ in range(COARSE_SWEEPS):
        v4 = (0.2 * v4 + g4) + c4 * near4(v4)
    u4 = dot3(unscale(v4, s4), select_matrix((128, 128), lambda i, o: i == o // 2))
    p3[:, pl.ds(0, 16, 2), :] = u4
    p3[:, pl.ds(1, 16, 2), :] = u4
    w = p3[...]
    w = jnp.broadcast_to(w[:, None], (4, 2, 32, 128)).reshape(8, 32, 128)
    v3 = (q3 + 0.8 * g3) + s3 * w
    for _ in range(2):
        v3 = (0.2 * v3 + g3) + c3 * near3(v3)
    pick = select_matrix(
        (128, 128),
        lambda i, o: i == (jnp.where(o < 64, o // 2, 127 - (127 - o) // 2) + 16 * iy) % 128,
    )
    u[...] = pltpu.roll(dot3(v3 / s3, pick), (32 - 4 * ix) % 32, 1)


def k_up2(u3, g2, c2, s2, q2, u, p2):
    p2[:, 14:18, :] = jnp.zeros((8, 4, 128), F32)
    for n in range(2):
        p2[:, pl.ds(n, 7, 2), :] = u3[:, 0:7, :]
        p2[:, pl.ds(18 + n, 3, 2), :] = u3[:, 29:32, :]
    w = p2[...]
    w = jnp.broadcast_to(w[:, None], (8, 2, 24, 128)).reshape(16, 24, 128)
    gv, cv, sv = g2[...], c2[...], s2[...]
    zero = jnp.zeros((1, 24, 128), F32)
    v = (q2[...] + 0.8 * gv) + sv * w
    for _ in range(2):
        w = jnp.concatenate([zero, v, zero], axis=0)
        v = (0.2 * v + gv) + cv * around(w[:16], v, w[2:])
    pick = select_matrix(
        (128, 128),
        lambda i, o: i == jnp.where(o < 96, o // 2, 127 - (127 - o) // 2),
    )
    u[...] = dot3(unscale(v, sv), pick)


def k_up1(u2, g1, c1, s1, q1, u, p1, va, vb):
    for n in range(2):
        p1[:, pl.ds(n, 14, 2), :] = u2[:, 0:14, :]
        p1[:, pl.ds(28 + n, 6, 2), :] = u2[:, 18:24, :]
    for ref in (va, vb, u):
        ref[0] = jnp.zeros((40, 128), F32)
        ref[33] = jnp.zeros((40, 128), F32)

    def start(z, at):
        t = p1[pl.ds((z - 1) // 2, A1 // 2)]
        t = jnp.broadcast_to(t[:, None], (A1 // 2, 2, 40, 128)).reshape(A1, 40, 128)
        va[at] = (q1[at] + 0.8 * g1[at]) + s1[pl.ds(z - 1, A1)] * t

    blocks(1, 32, A1, start, U1)

    def sweep(z, at):
        vb[at] = (0.2 * va[at] + g1[at]) + c1[pl.ds(z - 1, A1)] * near(va, z, A1)

    blocks(1, 32, A1, sweep, U1)

    def last(z, at):
        own = pl.ds(z - 1, A1)
        v = (0.2 * vb[at] + g1[at]) + c1[own] * near(vb, z, A1)
        u[at] = unscale(v, s1[own])

    blocks(1, 32, A1, last, U1)


def k_up0(u1, gm, cm, sm, q, gw, cw, sw, qw, out, pm, pw, wa, wb, ea, eb):
    iz = lax.axis_index("gz")

    def source(i, o):
        y = jnp.where(o % 16 < 8, 125 + o % 16, o % 16 - 11)
        return i == jnp.where(o < 128, o // 2, ((y + 256) // 2) % 128)

    u = u1[pl.ds(16 * iz, 18)]
    sub = iota((18, 8, 128), 1)
    u = jnp.concatenate([u[:, :16], jnp.where(sub < 4, u[:, 16:24], u[:, 32:40])], axis=1)
    u = dot3(u, select_matrix((128, 256), source))
    for h, ref in enumerate((pm, pw)):
        w = u[:, :, 128 * h : 128 * h + 128]
        for n in range(2):
            ref[:, pl.ds(n, 18, 2), :] = w[:, 0:18]
            ref[:, pl.ds(36 + n, 2, 2), :] = w[:, 22:24]
    slot = iota((40, 128), 1) // 16
    parts = []
    for group in range(5):
        total = None
        for j in range(8):
            part = pw[min(max((8 * group + j - 1) // 2, 0), 17)]
            total = part if total is None else jnp.where(slot >= j, part, total)
        parts.append(total[None])
    g, c = gw[...], cw[...]
    v = (qw[...] + 0.8 * g) + sw[...] * jnp.concatenate(parts, axis=0)
    ea[...] = joint(v)
    eb[...] = joint((0.2 * v + g) + c * near_edges(v))

    def start(z, at):
        t = jnp.stack([pm[(z + i - 1) // 2] for i in range(A0)])
        wa[at] = (q[at] + 0.8 * gm[at]) + sm[at] * t

    blocks(1, 36, A0, start, U0)
    wa[0] = jnp.zeros((40, 128), F32)
    wa[37] = jnp.zeros((40, 128), F32)

    def sweep(z, at):
        wb[at] = (0.2 * wa[at] + gm[at]) + cm[at] * near_main(wa, ea, z, A0)

    blocks(1, 36, A0, sweep, U0)

    def last(z, at):
        n = near_main(wb, eb, z, B0)[:, :32]
        v = (0.2 * wb[at, :32, :] + gm[at, :32, :]) + cm[at, :32, :] * n
        out[pl.ds(z - 3, B0)] = v / sm[at, :32, :]

    blocks(3, 32, B0, last, U0)


def ring(v, axis, step):
    n = lax.axis_size(axis)
    return lax.ppermute(v, axis, [(i, (i + step) % n) for i in range(n)])


def pair(to_right, to_left, axis):
    return ring(to_right, axis, 1), ring(to_left, axis, -1)


def after(values, *others):
    return lax.optimization_barrier((values, others))[0]


def shards(f, s, k):
    zr = ring(face_z(f, s, k), "gz", 1)
    g, c, sk1 = run(
        k_load, (f, s, k), [(32, 32, 128)] * 2 + [(16, 16, 128)], [(16, 32, 128)] * 2
    )
    sk1 = after(sk1, zr)
    sk_all = jnp.concatenate([sk1, ring(sk1, "gz", 1)], axis=0)
    xs = pair(*run(k_face_x, (g, c, s, zr), [(38, 8, 128)] * 2), "gx")
    (edges,) = run(k_pack_own, (g, c, s), [(5, 40, 128)])
    sk_x = pair(sk_all, sk_all, "gx")
    (ymsg,) = run(k_face_y, (edges, zr, *xs), [(5, 40, 128)])
    ys = pair(ymsg, ymsg, "gy")
    gm, cm, sm = run(k_assemble, (g, c, s, zr, *xs), [(38, 40, 128)] * 3)
    sk_full, *sk_y = run(k_spread, (sk_all, *sk_x), [(32, 40, 128)] + [(8, 40, 128)] * 2)
    sk_y = pair(*sk_y, "gy")
    small = [(5, 40, 128)]
    gw, cw, sw, q0, qw, f1 = run(
        k_down0,
        (f, gm, cm, sm, ymsg, *ys),
        small * 3 + [(38, 40, 128)] + small + [(8, 16, 128)],
        [(16, 32, 128)] + small * 2,
    )
    f1 = jnp.concatenate([f1, ring(f1, "gz", 1)], axis=0)
    s1, c1, w1, s2, c2, w2, sk3 = run(
        k_coeff,
        (sk_full, *sk_y),
        [(32, 40, 128)] * 3 + [(16, 24, 128)] * 3 + [(8, 128)],
        [(16, 40, 128)] * 2 + [(16, 24, 128), (8, 8, 128)],
    )
    f1_x = after(pair(f1, f1, "gx"), sk3)
    f1_full, *f1_y = run(k_spread, (f1, *f1_x), [(16, 40, 128)] + [(4, 40, 128)] * 2)
    g1, q1, g2, q2, chunk = run(
        k_down12,
        (f1_full, *pair(*f1_y, "gy"), s1, c1, w1, s2, c2, w2, sk3),
        [(34, 40, 128)] * 2 + [(16, 24, 128)] * 2 + [(64, 16, 128)],
        [(32, 40, 128), (16, 40, 128), (16, 24, 128), (8, 8, 128)],
    )
    gathered = lax.all_to_all(chunk, ("gx", "gy"), 0, 0, tiled=True)
    (u3,) = run(
        k_whole, (gathered,), [(8, 32, 128)], [(3, 8, 32, 128), (4, 32, 128), (4, 32, 128)]
    )
    (u2,) = run(k_up2, (u3, g2, c2, s2, q2), [(16, 24, 128)], [(8, 24, 128)])
    (u1,) = run(
        k_up1, (u2, g1, c1, s1, q1), [(34, 40, 128)], [(16, 40, 128)] + [(34, 40, 128)] * 2
    )
    (out,) = run(
        k_up0,
        (u1, gm, cm, sm, q0, gw, cw, sw, qw),
        [(32, 32, 128)],
        [(18, 40, 128)] * 2 + [(38, 40, 128)] * 2 + small * 2,
    )
    return out


def solution(mesh):
    return jax.shard_map(
        shards,
        mesh=mesh,
        in_specs=(P("gz", "gx", "gy"),) * 3,
        out_specs=P("gz", "gx", "gy"),
        check_vma=False,
    )
```

```python
import math

import jax
import jax.numpy as jnp
from jax import lax
from jax.experimental import pallas as pl
from jax.experimental.pallas import tpu as pltpu
from jax.sharding import PartitionSpec as P

F32 = jnp.float32
VM = pl.BlockSpec(memory_space=pltpu.VMEM)
HBM = pl.BlockSpec(memory_space=pltpu.HBM)
BF16 = jnp.bfloat16
COARSE_SWEEPS = 11
MICROSECONDS = dict(
    k_face_z=0.2,
    k_load=4.0,
    k_face_x=0.2,
    k_pack_own=1.0,
    k_face_y=0.6,
    k_assemble=1.0,
    k_pack=0.3,
    k_down0=2.0,
    k_coeff=2.0,
    k_down12=3.0,
    k_whole=2.0,
    k_up2=0.5,
    k_up1=1.5,
    k_up0=2.5,
)
A0, B0, U0 = 12, 8, 3
A1, U1 = 8, 2


def run(body, args, outs, scratch=(), out_spec=VM, sems=()):
    words = sum(math.prod(s) for s in (*outs, *scratch)) + sum(a.size for a in args)
    return pl.pallas_call(
        body,
        out_shape=[jax.ShapeDtypeStruct(o, F32) for o in outs],
        in_specs=[VM] * len(args),
        out_specs=[out_spec] * len(outs),
        scratch_shapes=[pltpu.VMEM(s, F32) for s in scratch]
        + [pltpu.SemaphoreType.DMA(n) for n in sems],
        compiler_params=pltpu.CompilerParams(vmem_limit_bytes=6 * words + (6 << 20)),
        cost_estimate=pl.CostEstimate(
            flops=0, transcendentals=0, bytes_accessed=int(3.5e6 * MICROSECONDS[body.__name__])
        ),
    )(*args)


def weights(level):
    wh = 0.25**level
    return wh, 2.0 * (0.25 * wh + 2.0 * wh)


def iota(shape, dim):
    return lax.broadcasted_iota(jnp.int32, shape, dim)


def lanes(v, shift):
    return pltpu.roll(v, shift % v.shape[-1], v.ndim - 1)


def rows(v, shift):
    return pltpu.roll(v, shift % v.shape[-2], v.ndim - 2)


def beside(v):
    return (rows(v, 1) + rows(v, -1)) + (lanes(v, 1) + lanes(v, -1))


def around(above, v, below):
    return 0.25 * (above + below) + beside(v)


def factors(s, k, level):
    wh, full = weights(level)
    diagonal = k + full * (s * s)
    sw = s * (0.8 / jnp.where(diagonal > 0.0, diagonal, 1.0))
    return sw, (wh * s) * sw


def unscale(v, s):
    inside = s > 0.0
    return jnp.where(inside, v / jnp.where(inside, s, 1.0), 0.0)


def dot(a, b):
    b = b.astype(BF16)
    high = a.astype(BF16)
    rest = a - high.astype(F32)
    middle = rest.astype(BF16)
    low = (rest - middle.astype(F32)).astype(BF16)
    terms = [jnp.dot(t, b, preferred_element_type=F32) for t in (high, middle, low)]
    return terms[0] + (terms[1] + terms[2])


def dot3(a, b):
    n, r, c = a.shape
    return dot(a.reshape(n * r, c), b).reshape(n, r, b.shape[1])


def blocks(first, count, size, body, unroll=1):
    def one(b, _):
        z = first + size * b
        body(z, pl.ds(z, size))
        return 0

    lax.fori_loop(0, count // size, one, 0, unroll=unroll)


def pair_sum(v):
    v = v.reshape(v.shape[0] // 2, 2, *v.shape[1:])
    return v[:, 0] + v[:, 1]


def select_matrix(shape, source_of, scale=1.0):
    i, o = iota(shape, 0), iota(shape, 1)
    return jnp.where(source_of(i, o), scale, 0.0).astype(F32)


def k_face_z(near, zmsg):
    upper = lax.axis_index("gz") == 0
    s = near[3:6]
    sw, c = factors(s, near[6:9], 0)
    zmsg[0:3] = sw * near[0:3]
    zmsg[3:5] = jnp.where(upper, c[1:], c[:2])
    zmsg[5:7] = jnp.where(upper, s[1:], s[:2])


def k_load(f, s, k, g, c, sk1, ps, pk):
    def one(z, at):
        sv, kv = s[at], k[at]
        sw, cv = factors(sv, kv, 0)
        g[at] = sw * f[at]
        c[at] = cv
        ps[pl.ds(z // 2, 2)] = pair_sum(sv)
        pk[pl.ds(z // 2, 2)] = pair_sum(kv)

    blocks(0, 32, 4, one, 2)
    a = ps[:, pl.ds(0, 16, 2), :] + ps[:, pl.ds(1, 16, 2), :]
    b = pk[:, pl.ds(0, 16, 2), :] + pk[:, pl.ds(1, 16, 2), :]
    left = select_matrix((128, 128), lambda i, o: i // 2 == o, 0.125)
    right = select_matrix((128, 128), lambda i, o: i // 2 == o - 64, 0.125)
    sk1[...] = dot3(a, left) + dot3(b, right)


def halo_rows(zr, iz, field, z):
    first, depth = ((0, 3), (3, 2), (5, 2))[field]
    d = z - 35 if z > 34 else 2 - z
    if d >= depth:
        return jnp.zeros(zr.shape[1:], F32)
    row = first + (d if z > 34 else depth - 1 - d)
    return jnp.where(iz == (0 if z > 34 else 1), zr[row], 0.0)


def k_face_x(g, c, s, zr, to_right, to_left):
    iz = lax.axis_index("gz")
    sub = iota((8, 128), 0)

    def put(z, gz, cz, sz):
        a, b, d = gz[24:32], cz[24:32], sz[24:32]
        to_right[z] = jnp.where(sub >= 5, a, jnp.where(sub >= 3, rows(b, -3), rows(d, -5)))
        a, b, d = gz[0:8], cz[0:8], sz[0:8]
        to_left[z] = jnp.where(sub < 3, a, jnp.where(sub < 5, rows(b, 3), rows(d, 5)))

    def one(z, _):
        put(z + 3, g[z], c[z], s[z])
        return 0

    lax.fori_loop(0, 32, one, 0, unroll=4)
    for z in (0, 1, 2, 35, 36, 37):
        put(z, *[halo_rows(zr, iz, n, z) for n in range(3)])


def k_pack_own(g, c, s, own):
    own[...] = jnp.zeros((5, 40, 128), F32)
    slot = iota((32, 128), 1)

    def pack(first, group, js):
        total = jnp.zeros((32, 128), F32)
        for j in js:
            z = first + j - js[0]
            total = jnp.where(slot >= 16 * j, lanes(g[z], 16 * j + 3), total)
            total = jnp.where(slot >= 16 * j + 6, lanes(c[z], 16 * j + 8), total)
            total = jnp.where(slot >= 16 * j + 10, lanes(s[z], 16 * j + 12), total)
        own[group, :32, :] = total

    pack(0, 0, range(3, 8))
    for group in range(1, 4):
        pack(8 * group - 3, group, range(8))
    pack(29, 4, range(3))


def side_rows(from_left, from_right, ix, z):
    sub = iota((8, 128), 0)
    lf = jnp.where(ix > 0, from_left[z], 0.0)
    rt = jnp.where(ix < 7, from_right[z], 0.0)
    return (
        jnp.where(sub >= 4, lf, rt),
        jnp.where(sub >= 4, rows(lf, 3), rows(rt, -3)),
        jnp.where(sub >= 4, rows(lf, 5), rows(rt, -5)),
    )


def slotted(total, slot, fields, j):
    for n, (lane, shift) in enumerate(((0, 3), (6, 8), (10, 12))):
        total = jnp.where(slot >= 16 * j + lane, lanes(fields[n], 16 * j + shift), total)
    return total


def k_face_y(own, zr, from_left, from_right, ymsg):
    ix, iz = lax.axis_index("gx"), lax.axis_index("gz")
    slot = iota((8, 128), 1)
    wide = iota((32, 128), 1)
    for group in range(5):
        side = jnp.zeros((8, 128), F32)
        for j in range(8 if group < 4 else 6):
            side = slotted(side, slot, side_rows(from_left, from_right, ix, group * 8 + j), j)
        mid = own[group, :32, :]
        if group == 0:
            edge = jnp.zeros((32, 128), F32)
            for j in range(3):
                edge = slotted(edge, wide, [halo_rows(zr, iz, n, j) for n in range(3)], j)
            mid = jnp.where(wide < 48, edge, mid)
        if group == 4:
            for j in range(3, 6):
                mid = slotted(mid, wide, [halo_rows(zr, iz, n, 32 + j) for n in range(3)], j)
        ymsg[group] = jnp.concatenate([mid, side], axis=0)


def k_assemble(g, c, s, zr, from_left, from_right, gm, cm, sm):
    ix, iz = lax.axis_index("gx"), lax.axis_index("gz")

    def put(z, values):
        for ref, mid, side in zip(
            (gm, cm, sm), values, side_rows(from_left, from_right, ix, z)
        ):
            ref[z] = jnp.concatenate([mid, side], axis=0)

    def one(z, _):
        put(z + 3, (g[z], c[z], s[z]))
        return 0

    lax.fori_loop(0, 32, one, 0, unroll=4)
    for z in (0, 1, 2, 35, 36, 37):
        put(z, [halo_rows(zr, iz, n, z) for n in range(3)])


def near_edges(v):
    lane = iota(v.shape, 2)
    zero = jnp.zeros((1,) + v.shape[1:], F32)
    up, down = lanes(v, 16), lanes(v, -16)
    above = jnp.where(lane < 16, jnp.concatenate([zero, up[:-1]], axis=0), up)
    below = jnp.where(lane >= 112, jnp.concatenate([down[1:], zero], axis=0), down)
    return around(above, v, below)


def joint(v):
    return jnp.where(iota(v.shape, 2) % 16 == 4, lanes(v, -6), v)


def near_main(ref, edge, z, n):
    v = ref[pl.ds(z, n)]
    lane = iota(v.shape, 2)
    e = jnp.stack(
        [
            pltpu.roll(edge[(z + i) // 8], (124 - 16 * ((z + i) % 8)) % 128, 1)
            for i in range(n)
        ]
    )
    across = jnp.where(lane == 0, e, lanes(v, 1)) + jnp.where(lane == 127, e, lanes(v, -1))
    above, below = ref[pl.ds(z - 1, n)], ref[pl.ds(z + 1, n)]
    return 0.25 * (above + below) + ((rows(v, 1) + rows(v, -1)) + across)


def near(ref, z, n):
    return around(ref[pl.ds(z - 1, n)], ref[pl.ds(z, n)], ref[pl.ds(z + 1, n)])


def k_down0(f, gm, cm, sm, own, from_left, from_right, gw, cw, sw, q, qw, f1, e, eg, eq):
    iy = lax.axis_index("gy")
    lane = iota((5, 40, 128), 2) % 16
    mid = own[...]
    lf = jnp.where(iy > 0, from_left[...], 0.0)
    rt = jnp.where(iy < 7, from_right[...], 0.0)

    def window(split, to_right, to_left):
        a = jnp.where(lane < split, mid, rt)
        b = jnp.where(lane < split, lf, mid)
        a = lanes(a, to_right) if to_right else a
        return jnp.where(lane < 8, a, lanes(b, to_left))

    g = window(3, 0, 8)
    c = window(8, -5, 3)
    gw[...] = g
    cw[...] = c
    sw[...] = window(12, -9, -1)
    w = 0.4 * g + c * near_edges(g)
    qw[...] = w
    eg[...] = joint(g)
    eq[...] = joint(w)
    q[0] = jnp.zeros((40, 128), F32)
    q[37] = jnp.zeros((40, 128), F32)

    def relax(z, at):
        q[at] = 0.4 * gm[at] + cm[at] * near_main(gm, eg, z, A0)

    blocks(1, 36, A0, relax, U0)

    def residual(z, at):
        v = 0.04 * f[pl.ds(z - 3, B0)] + sm[at, :32, :] * near_main(q, eq, z, B0)[:, :32]
        e[pl.ds((z - 3) // 2, B0 // 2)] = pair_sum(v)

    blocks(3, 32, B0, residual, U0)
    a = e[:, pl.ds(0, 16, 2), :] + e[:, pl.ds(1, 16, 2), :]
    lo = select_matrix((128, 128), lambda i, o: i // 2 == o, 0.125)
    hi = select_matrix((128, 128), lambda i, o: i // 2 == o - 64, 0.125)
    f1[...] = dot3(a[:8], lo) + dot3(a[8:], hi)


def k_pack(own, full, to_right, to_left):
    iz = lax.axis_index("gz")
    lane = iota((16, 128), 1) % 64
    n = own.shape[0] // 2

    def one(z, at):
        first = z + jnp.where(z < n, 0, -n) + jnp.where((iz == 0) == (z < n), 0, n)
        v = own[pl.ds(first, 4)]
        full[at] = v
        a = lanes(v[0], -52)
        b = v[0]
        for j in range(1, 4):
            a = jnp.where(lane >= 16 * j, lanes(v[j], 16 * j - 52), a)
            b = jnp.where(lane >= 16 * j, lanes(v[j], 16 * j), b)
        to_right[z // 4] = a
        to_left[z // 4] = b

    blocks(0, 2 * n, 4, one, 2)


def joined(own, xl, xr, at, ix):
    lf = jnp.where(ix > 0, xl[at], 0.0)
    rt = jnp.where(ix < 7, xr[at], 0.0)
    sub = iota((rt.shape[0], 8, 128), 1)
    edge = jnp.where(sub < 4, rt[:, 8:16], lf[:, 0:8])
    return jnp.concatenate([own[at], rt[:, 0:8], edge, lf[:, 8:16]], axis=1)


def opened(own, xl, xr, z, n, ix, iy):
    mid = joined(own, xl, xr, pl.ds(z, 4), ix)
    lf = jnp.where(iy > 0, joined(own, xl, xr, pl.ds(n + z // 4, 1), ix)[0], 0.0)
    rt = jnp.where(iy < 7, joined(own, xl, xr, pl.ds(n + (n + z) // 4, 1), ix)[0], 0.0)
    lf = jnp.stack([lanes(lf, 116 - 16 * j) for j in range(4)])
    rt = jnp.stack([lanes(rt, 64 - 16 * j) for j in range(4)])
    lane = iota(mid.shape, 2)
    first = jnp.where(lane < 64, mid, jnp.where(lane < 96, rt, lf))
    second = jnp.where(lane >= 64, mid, jnp.where(lane < 32, rt, lf))
    return first, lanes(second, 64)


def halve_x(ref, n, x2):
    x2[:, 14:18, :] = jnp.zeros((n, 4, 128), F32)
    x2[:, 0:14, :] = ref[:, pl.ds(0, 14, 2), :] + ref[:, pl.ds(1, 14, 2), :]
    x2[:, 18:24, :] = ref[:, pl.ds(28, 6, 2), :] + ref[:, pl.ds(29, 6, 2), :]
    return x2[...]


def down_matrix():
    return select_matrix(
        (128, 128),
        lambda i, o: ((i // 2 == o) & (o < 38)) | ((i // 2 == o - 64) & (o >= 122)),
        0.125,
    )


def level3_rows(v, e2):
    half = select_matrix((128, 128), lambda i, o: (i // 2 == o) & (o < 16), 0.125)
    v = v.reshape(8, 2, 24, 128)
    e2[...] = v[:, 0, :8, :] + v[:, 1, :8, :]
    pairs = e2[:, pl.ds(0, 4, 2), :] + e2[:, pl.ds(1, 4, 2), :]
    total = dot(pairs[0], half)
    for j in range(1, 8):
        total = total + lanes(dot(pairs[j], half), 16 * j)
    return total


def k_coeff(own, xl, xr, s1, c1, w1, s2, c2, w2, sk3, ps, pk, x2, e2):
    ix, iy = lax.axis_index("gx"), lax.axis_index("gy")

    def one(z, at):
        s, k = opened(own, xl, xr, z, 32, ix, iy)
        s1[at] = s
        w1[at], c1[at] = factors(s, k, 1)
        ps[pl.ds(z // 2, 2)] = pair_sum(s)
        pk[pl.ds(z // 2, 2)] = pair_sum(k)

    blocks(0, 32, 4, one, 2)
    down = down_matrix()
    s = dot3(halve_x(ps, 16, x2), down)
    k = dot3(halve_x(pk, 16, x2), down)
    s2[...] = s
    w2[...], c2[...] = factors(s, k, 2)
    sk3[...] = jnp.concatenate([level3_rows(s, e2), level3_rows(k, e2)], axis=0)


def k_down12(own, xl, xr, s1, c1, w1, s2, c2, w2, sk3, g, q, g2, q2, chunk, f, e, x2, e2):
    ix, iy = lax.axis_index("gx"), lax.axis_index("gy")
    for ref in (g, q):
        ref[0] = jnp.zeros((40, 128), F32)
        ref[33] = jnp.zeros((40, 128), F32)

    def one(z, at):
        for i, v in enumerate(opened(own, xl, xr, z, 16, ix, iy)):
            first = z + 8 * (z // 8) + 8 * i
            f[pl.ds(first, 4)] = v
            g[pl.ds(first + 1, 4)] = w1[pl.ds(first, 4)] * v

    blocks(0, 16, 4, one, 2)

    def relax(z, at):
        q[at] = 0.4 * g[at] + c1[pl.ds(z - 1, A1)] * near(g, z, A1)

    blocks(1, 32, A1, relax, U1)
    wh, _ = weights(1)

    def residual(z, at):
        own = pl.ds(z - 1, A1)
        v = 0.04 * f[own] + (wh * s1[own]) * near(q, z, A1)
        e[pl.ds((z - 1) // 2, A1 // 2)] = pair_sum(v)

    blocks(1, 32, A1, residual, U1)
    fv = dot3(halve_x(e, 16, x2), down_matrix())
    gv = w2[...] * fv
    zero = jnp.zeros((1, 24, 128), F32)

    def spread(v):
        w = jnp.concatenate([zero, v, zero], axis=0)
        return around(w[:16], v, w[2:])

    qv = 0.4 * gv + c2[...] * spread(gv)
    wh, _ = weights(2)
    ev = 0.04 * fv + (wh * s2[...]) * spread(qv)
    g2[...] = gv
    q2[...] = qv
    parts = [level3_rows(ev, e2), sk3[:4], sk3[4:]]
    parts = [pltpu.roll(part, 16 * iy, 1) for part in parts]

    def copy(n, _):
        for i in range(3):
            chunk[3 * n + i] = parts[i]
        return 0

    lax.fori_loop(0, 64, copy, 0, unroll=8)


def spread_in(shape, last):
    n, r, _ = shape
    row, col = iota(shape, 1), iota(shape, 2)
    zero = jnp.zeros((1,) + shape[1:], F32)

    def apply(v):
        w = jnp.concatenate([zero, v, zero], axis=0)
        x = jnp.where(row > 0, rows(v, 1), 0.0) + jnp.where(row < r - 1, rows(v, -1), 0.0)
        y = jnp.where(col > 0, lanes(v, 1), 0.0) + jnp.where(col < last, lanes(v, -1), 0.0)
        return 0.25 * (w[:n] + w[2:]) + x + y

    return apply


def k_whole(gathered, u, t3, x4, p3):
    ix, iy = lax.axis_index("gx"), lax.axis_index("gy")
    lane = iota((4, 128), 1) // 16
    for j in range(8):
        for n in range(3):
            for x in range(8):
                v = gathered[x * 24 + n]
                for y in range(1, 8):
                    v = jnp.where(lane == (j + y) % 8, gathered[x * 24 + 3 * y + n], v)
                t3[n, j, 4 * x : 4 * x + 4, :] = lanes(v, -16 * j) if j else v
    f3, s3, k3 = t3[0], t3[1], t3[2]
    near3 = spread_in((8, 32, 128), 127)
    w3, c3 = factors(s3, k3, 3)
    g3 = w3 * f3
    q3 = 0.4 * g3 + c3 * near3(g3)
    e3 = 0.04 * f3 + (weights(3)[0] * s3) * near3(q3)
    half = select_matrix((128, 128), lambda i, o: i // 2 == o, 0.125)
    fields = []
    for v in (e3, s3, k3):
        w = v.reshape(4, 2, 32, 128)
        x4[...] = w[:, 0] + w[:, 1]
        fields.append(dot3(x4[:, pl.ds(0, 16, 2), :] + x4[:, pl.ds(1, 16, 2), :], half))
    f4, s4, k4 = fields
    near4 = spread_in((4, 16, 128), 63)
    w4, c4 = factors(s4, k4, 4)
    g4 = w4 * f4
    v4 = g4
    for _ in range(COARSE_SWEEPS):
        v4 = (0.2 * v4 + g4) + c4 * near4(v4)
    u4 = dot3(unscale(v4, s4), select_matrix((128, 128), lambda i, o: i == o // 2))
    p3[:, pl.ds(0, 16, 2), :] = u4
    p3[:, pl.ds(1, 16, 2), :] = u4
    w = p3[...]
    w = jnp.broadcast_to(w[:, None], (4, 2, 32, 128)).reshape(8, 32, 128)
    v3 = (q3 + 0.8 * g3) + s3 * w
    for _ in range(2):
        v3 = (0.2 * v3 + g3) + c3 * near3(v3)
    pick = select_matrix(
        (128, 128),
        lambda i, o: i == (jnp.where(o < 64, o // 2, 127 - (127 - o) // 2) + 16 * iy) % 128,
    )
    u[...] = pltpu.roll(dot3(v3 / s3, pick), (32 - 4 * ix) % 32, 1)


def k_up2(u3, g2, c2, s2, q2, u, p2):
    p2[:, 14:18, :] = jnp.zeros((8, 4, 128), F32)
    for n in range(2):
        p2[:, pl.ds(n, 7, 2), :] = u3[:, 0:7, :]
        p2[:, pl.ds(18 + n, 3, 2), :] = u3[:, 29:32, :]
    w = p2[...]
    w = jnp.broadcast_to(w[:, None], (8, 2, 24, 128)).reshape(16, 24, 128)
    gv, cv, sv = g2[...], c2[...], s2[...]
    zero = jnp.zeros((1, 24, 128), F32)
    v = (q2[...] + 0.8 * gv) + sv * w
    for _ in range(2):
        w = jnp.concatenate([zero, v, zero], axis=0)
        v = (0.2 * v + gv) + cv * around(w[:16], v, w[2:])
    pick = select_matrix(
        (128, 128),
        lambda i, o: i == jnp.where(o < 96, o // 2, 127 - (127 - o) // 2),
    )
    u[...] = dot3(unscale(v, sv), pick)


def k_up1(u2, g1, c1, s1, q1, u, p1, va, vb):
    for n in range(2):
        p1[:, pl.ds(n, 14, 2), :] = u2[:, 0:14, :]
        p1[:, pl.ds(28 + n, 6, 2), :] = u2[:, 18:24, :]
    for ref in (va, vb, u):
        ref[0] = jnp.zeros((40, 128), F32)
        ref[33] = jnp.zeros((40, 128), F32)

    def start(z, at):
        t = p1[pl.ds((z - 1) // 2, A1 // 2)]
        t = jnp.broadcast_to(t[:, None], (A1 // 2, 2, 40, 128)).reshape(A1, 40, 128)
        va[at] = (q1[at] + 0.8 * g1[at]) + s1[pl.ds(z - 1, A1)] * t

    blocks(1, 32, A1, start, U1)

    def sweep(z, at):
        vb[at] = (0.2 * va[at] + g1[at]) + c1[pl.ds(z - 1, A1)] * near(va, z, A1)

    blocks(1, 32, A1, sweep, U1)

    def last(z, at):
        own = pl.ds(z - 1, A1)
        v = (0.2 * vb[at] + g1[at]) + c1[own] * near(vb, z, A1)
        u[at] = unscale(v, s1[own])

    blocks(1, 32, A1, last, U1)


def k_up0(u1, gm, cm, sm, q, gw, cw, sw, qw, out, pm, pw, wa, wb, ea, eb, done, sem):
    iz = lax.axis_index("gz")

    def source(i, o):
        y = jnp.where(o % 16 < 8, 125 + o % 16, o % 16 - 11)
        return i == jnp.where(o < 128, o // 2, ((y + 256) // 2) % 128)

    u = u1[pl.ds(16 * iz, 18)]
    sub = iota((18, 8, 128), 1)
    u = jnp.concatenate([u[:, :16], jnp.where(sub < 4, u[:, 16:24], u[:, 32:40])], axis=1)
    u = dot3(u, select_matrix((128, 256), source))
    for h, ref in enumerate((pm, pw)):
        w = u[:, :, 128 * h : 128 * h + 128]
        for n in range(2):
            ref[:, pl.ds(n, 18, 2), :] = w[:, 0:18]
            ref[:, pl.ds(36 + n, 2, 2), :] = w[:, 22:24]
    slot = iota((40, 128), 1) // 16
    parts = []
    for group in range(5):
        total = None
        for j in range(8):
            part = pw[min(max((8 * group + j - 1) // 2, 0), 17)]
            total = part if total is None else jnp.where(slot >= j, part, total)
        parts.append(total[None])
    g, c = gw[...], cw[...]
    v = (qw[...] + 0.8 * g) + sw[...] * jnp.concatenate(parts, axis=0)
    ea[...] = joint(v)
    eb[...] = joint((0.2 * v + g) + c * near_edges(v))

    def start(z, at):
        t = jnp.stack([pm[(z + i - 1) // 2] for i in range(A0)])
        wa[at] = (q[at] + 0.8 * gm[at]) + sm[at] * t

    blocks(1, 36, A0, start, U0)
    wa[0] = jnp.zeros((40, 128), F32)
    wa[37] = jnp.zeros((40, 128), F32)

    def sweep(z, at):
        wb[at] = (0.2 * wa[at] + gm[at]) + cm[at] * near_main(wa, ea, z, A0)

    blocks(1, 36, A0, sweep, U0)

    copies = []
    for b in range(32 // B0):
        z = 3 + b * B0
        at = pl.ds(z, B0)
        n = near_main(wb, eb, z, B0)[:, :32]
        v = (0.2 * wb[at, :32, :] + gm[at, :32, :]) + cm[at, :32, :] * n
        part = pl.ds(z - 3, B0)
        done[part] = v / sm[at, :32, :]
        copies.append(pltpu.make_async_copy(done.at[part], out.at[part], sem.at[b]))
        copies[-1].start()
    for copy in copies:
        copy.wait()


def ring(v, axis, step):
    n = lax.axis_size(axis)
    return lax.ppermute(v, axis, [(i, (i + step) % n) for i in range(n)])


def pair(to_right, to_left, axis):
    return ring(to_right, axis, 1), ring(to_left, axis, -1)


def pack_level1(own):
    n = own.shape[0]
    full, *msg = run(k_pack, (own,), [(n, 16, 128)] + [(n // 4, 16, 128)] * 2)
    return jnp.concatenate([full, *pair(*msg, "gy")], axis=0)


def after(values, *others):
    return lax.optimization_barrier((values, others))[0]


def shards(f, s, k):
    first = jnp.where(lax.axis_index("gz") == 0, 29, 0)
    near = jnp.concatenate([lax.dynamic_slice_in_dim(v, first, 3, 0) for v in (f, s, k)], axis=0)
    zr = ring(run(k_face_z, (near,), [(7, 32, 128)])[0], "gz", 1)
    g, c, sk1 = run(
        k_load, (f, s, k), [(32, 32, 128)] * 2 + [(16, 16, 128)], [(16, 32, 128)] * 2
    )
    sk1 = after(sk1, zr)
    sk_z = ring(sk1, "gz", 1)
    xs = pair(*run(k_face_x, (g, c, s, zr), [(38, 8, 128)] * 2), "gx")
    (edges,) = run(k_pack_own, (g, c, s), [(5, 40, 128)])
    (ymsg,) = run(k_face_y, (edges, zr, *xs), [(5, 40, 128)])
    ys = pair(ymsg, ymsg, "gy")
    gm, cm, sm = run(k_assemble, (g, c, s, zr, *xs), [(38, 40, 128)] * 3)
    sk1, sk_z = after((sk1, sk_z), ymsg)
    sk_y = pack_level1(jnp.concatenate([sk1, sk_z], axis=0))
    small = [(5, 40, 128)]
    gw, cw, sw, q0, qw, f1 = run(
        k_down0,
        (f, gm, cm, sm, ymsg, *ys),
        small * 3 + [(38, 40, 128)] + small + [(8, 16, 128)],
        [(16, 32, 128)] + small * 2,
    )
    sk = after(sk_y, f1)
    f1 = jnp.concatenate([f1, ring(f1, "gz", 1)], axis=0)
    s1, c1, w1, s2, c2, w2, sk3 = run(
        k_coeff,
        (sk, *pair(sk, sk, "gx")),
        [(32, 40, 128)] * 3 + [(16, 24, 128)] * 3 + [(8, 128)],
        [(16, 40, 128)] * 2 + [(16, 24, 128), (8, 8, 128)],
    )
    f1 = pack_level1(f1)
    g1, q1, g2, q2, chunk = run(
        k_down12,
        (f1, *pair(f1, f1, "gx"), s1, c1, w1, s2, c2, w2, sk3),
        [(34, 40, 128)] * 2 + [(16, 24, 128)] * 2 + [(192, 4, 128)],
        [(32, 40, 128), (16, 40, 128), (16, 24, 128), (8, 8, 128)],
    )
    gathered = lax.all_to_all(chunk, ("gx", "gy"), 0, 0, tiled=True)
    (u3,) = run(
        k_whole, (gathered,), [(8, 32, 128)], [(3, 8, 32, 128), (4, 32, 128), (4, 32, 128)]
    )
    (u2,) = run(k_up2, (u3, g2, c2, s2, q2), [(16, 24, 128)], [(8, 24, 128)])
    (u1,) = run(
        k_up1, (u2, g1, c1, s1, q1), [(34, 40, 128)], [(16, 40, 128)] + [(34, 40, 128)] * 2
    )
    (out,) = run(
        k_up0,
        (u1, gm, cm, sm, q0, gw, cw, sw, qw),
        [(32, 32, 128)],
        [(18, 40, 128)] * 2 + [(38, 40, 128)] * 2 + small * 2 + [(32, 32, 128)],
        HBM,
        [(32 // B0,)],
    )
    return out


def solution(mesh):
    return jax.shard_map(
        shards,
        mesh=mesh,
        in_specs=(P("gz", "gx", "gy"),) * 3,
        out_specs=P("gz", "gx", "gy"),
        check_vma=False,
    )
```

```python
import math

import jax
import jax.numpy as jnp
from jax import lax
from jax.experimental import pallas as pl
from jax.experimental.pallas import tpu as pltpu
from jax.sharding import PartitionSpec as P

F32 = jnp.float32
VM = pl.BlockSpec(memory_space=pltpu.VMEM)
HBM = pl.BlockSpec(memory_space=pltpu.HBM)
BF16 = jnp.bfloat16
COARSE_SWEEPS = 11
MICROSECONDS = dict(
    k_face_z=0.2,
    k_load=4.0,
    k_face_x=0.2,
    k_pack_own=1.0,
    k_face_y=0.6,
    k_assemble=1.0,
    k_pack=0.3,
    k_down0=2.0,
    k_coeff=2.0,
    k_down12=3.0,
    k_whole=2.0,
    k_up2=0.5,
    k_up1=1.5,
    k_up0=2.5,
)
A0, B0, U0 = 12, 8, 3
A1, U1 = 4, 8


def run(body, args, outs, scratch=(), out_spec=VM, sems=()):
    words = sum(math.prod(s) for s in (*outs, *scratch)) + sum(a.size for a in args)
    return pl.pallas_call(
        body,
        out_shape=[jax.ShapeDtypeStruct(o, F32) for o in outs],
        in_specs=[VM] * len(args),
        out_specs=[out_spec] * len(outs),
        scratch_shapes=[pltpu.VMEM(s, F32) for s in scratch]
        + [pltpu.SemaphoreType.DMA(n) for n in sems],
        compiler_params=pltpu.CompilerParams(vmem_limit_bytes=6 * words + (6 << 20)),
        cost_estimate=pl.CostEstimate(
            flops=0, transcendentals=0, bytes_accessed=int(3.5e6 * MICROSECONDS[body.__name__])
        ),
    )(*args)


def weights(level):
    wh = 0.25**level
    return wh, 2.0 * (0.25 * wh + 2.0 * wh)


def iota(shape, dim):
    return lax.broadcasted_iota(jnp.int32, shape, dim)


def lanes(v, shift):
    return pltpu.roll(v, shift % v.shape[-1], v.ndim - 1)


def rows(v, shift):
    return pltpu.roll(v, shift % v.shape[-2], v.ndim - 2)


def beside(v):
    return (rows(v, 1) + rows(v, -1)) + (lanes(v, 1) + lanes(v, -1))


def around(above, v, below):
    return 0.25 * (above + below) + beside(v)


def factors(s, k, level):
    wh, full = weights(level)
    diagonal = k + full * (s * s)
    sw = s * (0.8 / jnp.where(diagonal > 0.0, diagonal, 1.0))
    return sw, (wh * s) * sw


def unscale(v, s):
    inside = s > 0.0
    return jnp.where(inside, v / jnp.where(inside, s, 1.0), 0.0)


def dot(a, b):
    b = b.astype(BF16)
    high = a.astype(BF16)
    rest = a - high.astype(F32)
    middle = rest.astype(BF16)
    low = (rest - middle.astype(F32)).astype(BF16)
    terms = [jnp.dot(t, b, preferred_element_type=F32) for t in (high, middle, low)]
    return terms[0] + (terms[1] + terms[2])


def dot3(a, b):
    n, r, c = a.shape
    return dot(a.reshape(n * r, c), b).reshape(n, r, b.shape[1])


def blocks(first, count, size, body, unroll=1):
    def one(b, _):
        z = first + size * b
        body(z, pl.ds(z, size))
        return 0

    lax.fori_loop(0, count // size, one, 0, unroll=unroll)


def pair_sum(v):
    v = v.reshape(v.shape[0] // 2, 2, *v.shape[1:])
    return v[:, 0] + v[:, 1]


def select_matrix(shape, source_of, scale=1.0):
    i, o = iota(shape, 0), iota(shape, 1)
    return jnp.where(source_of(i, o), scale, 0.0).astype(F32)


def k_face_z(g, c, s, zmsg):
    upper = lax.axis_index("gz") == 0
    zmsg[0:3] = g[...]
    zmsg[3:5] = jnp.where(upper, c[1:], c[:2])
    zmsg[5:7] = jnp.where(upper, s[1:], s[:2])


def k_load(f, s, k, g, c, sk1, ps, pk):
    def one(z, at):
        sv, kv = s[at], k[at]
        sw, cv = factors(sv, kv, 0)
        g[at] = sw * f[at]
        c[at] = cv
        ps[pl.ds(z // 2, 2)] = pair_sum(sv)
        pk[pl.ds(z // 2, 2)] = pair_sum(kv)

    blocks(0, 32, 4, one, 2)
    a = ps[:, pl.ds(0, 16, 2), :] + ps[:, pl.ds(1, 16, 2), :]
    b = pk[:, pl.ds(0, 16, 2), :] + pk[:, pl.ds(1, 16, 2), :]
    left = select_matrix((128, 128), lambda i, o: i // 2 == o, 0.125)
    right = select_matrix((128, 128), lambda i, o: i // 2 == o - 64, 0.125)
    sk1[...] = dot3(a, left) + dot3(b, right)


def halo_rows(zr, iz, field, z):
    first, depth = ((0, 3), (3, 2), (5, 2))[field]
    d = z - 35 if z > 34 else 2 - z
    if d >= depth:
        return jnp.zeros(zr.shape[1:], F32)
    row = first + (d if z > 34 else depth - 1 - d)
    return jnp.where(iz == (0 if z > 34 else 1), zr[row], 0.0)


def k_face_x(g, c, s, zr, to_right, to_left):
    iz = lax.axis_index("gz")
    sub = iota((8, 128), 0)

    def put(z, gz, cz, sz):
        a, b, d = gz[24:32], cz[24:32], sz[24:32]
        to_right[z] = jnp.where(sub >= 5, a, jnp.where(sub >= 3, rows(b, -3), rows(d, -5)))
        a, b, d = gz[0:8], cz[0:8], sz[0:8]
        to_left[z] = jnp.where(sub < 3, a, jnp.where(sub < 5, rows(b, 3), rows(d, 5)))

    def one(z, _):
        put(z + 3, g[z], c[z], s[z])
        return 0

    lax.fori_loop(0, 32, one, 0, unroll=4)
    for z in (0, 1, 2, 35, 36, 37):
        put(z, *[halo_rows(zr, iz, n, z) for n in range(3)])


def k_pack_own(g, c, s, *own):
    slot = iota((32, 128), 1)
    for ref, out in zip((g, c, s), own):
        out[...] = jnp.zeros((3, 40, 128), F32)
        for group in range(3):
            total = jnp.zeros((32, 128), F32)
            for j in range(16):
                z = 16 * group + j - 3
                if 0 <= z < 32:
                    total = jnp.where(slot >= 8 * j, lanes(ref[z], 8 * j + 3), total)
                elif z == 32:
                    total = jnp.where(slot >= 8 * j, 0.0, total)
            out[group, :32, :] = total


def side_rows(from_left, from_right, ix, z):
    sub = iota((8, 128), 0)
    lf = jnp.where(ix > 0, from_left[z], 0.0)
    rt = jnp.where(ix < 7, from_right[z], 0.0)
    return (
        jnp.where(sub >= 4, lf, rt),
        jnp.where(sub >= 4, rows(lf, 3), rows(rt, -3)),
        jnp.where(sub >= 4, rows(lf, 5), rows(rt, -5)),
    )


def k_face_y(og, oc, os, zr, from_left, from_right, ag, ac, a_s, to_right, to_left):
    ix, iz = lax.axis_index("gx"), lax.axis_index("gz")
    slot = iota((8, 128), 1)
    wide = iota((32, 128), 1)
    lane = iota((40, 128), 1) % 8
    for group in range(3):
        side = [jnp.zeros((8, 128), F32)] * 3
        mid = [ref[group, :32, :] for ref in (og, oc, os)]
        for j in range(16 if group < 2 else 6):
            z = 16 * group + j
            here = side_rows(from_left, from_right, ix, z)
            for n in range(3):
                side[n] = jnp.where(slot >= 8 * j, lanes(here[n], 8 * j + 3), side[n])
                if z < 3 or z > 34:
                    edge = lanes(halo_rows(zr, iz, n, z), 8 * j + 3)
                    mid[n] = jnp.where(wide // 8 == j, edge, mid[n])
        g, c, s = [jnp.concatenate(parts, axis=0) for parts in zip(mid, side)]
        ag[group] = g
        ac[group] = c
        a_s[group] = s
        to_right[group] = jnp.where(
            lane < 3, g, jnp.where(lane < 5, lanes(c, 2), lanes(s, 4))
        )
        to_left[group] = jnp.where(
            lane >= 6, lanes(c, 3), jnp.where(lane >= 3, g, lanes(s, -2))
        )


def k_assemble(g, c, s, zr, from_left, from_right, gm, cm, sm):
    ix, iz = lax.axis_index("gx"), lax.axis_index("gz")

    def put(z, values):
        for ref, mid, side in zip(
            (gm, cm, sm), values, side_rows(from_left, from_right, ix, z)
        ):
            ref[z] = jnp.concatenate([mid, side], axis=0)

    def one(z, _):
        put(z + 3, (g[z], c[z], s[z]))
        return 0

    lax.fori_loop(0, 32, one, 0, unroll=4)
    for z in (0, 1, 2, 35, 36, 37):
        put(z, [halo_rows(zr, iz, n, z) for n in range(3)])


def near_edges(v):
    lane = iota(v.shape, 2)
    zero = jnp.zeros((1,) + v.shape[1:], F32)
    up, down = lanes(v, 8), lanes(v, -8)
    above = jnp.where(lane < 8, jnp.concatenate([zero, up[:-1]], axis=0), up)
    below = jnp.where(lane >= 120, jnp.concatenate([down[1:], zero], axis=0), down)
    return around(above, v, below)


def joint(v):
    lane = iota((3,) + v.shape[1:], 2)
    return jnp.where(lane % 8 == 4, lanes(v[3:], 2), v[:3])


def near_main(ref, edge, z, n):
    v = ref[pl.ds(z, n)]
    lane = iota(v.shape, 2)
    e = jnp.stack(
        [
            pltpu.roll(edge[(z + i) // 16], (124 - 8 * ((z + i) % 16)) % 128, 1)
            for i in range(n)
        ]
    )
    across = jnp.where(lane == 0, e, lanes(v, 1)) + jnp.where(lane == 127, e, lanes(v, -1))
    above, below = ref[pl.ds(z - 1, n)], ref[pl.ds(z + 1, n)]
    return 0.25 * (above + below) + ((rows(v, 1) + rows(v, -1)) + across)


def near(ref, z, n):
    return around(ref[pl.ds(z - 1, n)], ref[pl.ds(z, n)], ref[pl.ds(z + 1, n)])


def k_down0(
    f, gm, cm, sm, og, oc, os, from_left, from_right, gw, cw, sw, q, qw, f1, e, eg, eq
):
    iy = lax.axis_index("gy")
    own = iota((3, 40, 128), 2) % 8 < 3
    lf = jnp.where(iy > 0, from_left[...], 0.0)
    rt = jnp.where(iy < 7, from_right[...], 0.0)

    def windows(ref, right, left):
        mid = ref[...]
        return jnp.concatenate(
            [jnp.where(own, mid, right), jnp.where(own, left, mid)], axis=0
        )

    g = windows(og, rt, lf)
    c = windows(oc, lanes(rt, -3), lanes(lf, -2))
    gw[...] = g
    cw[...] = c
    sw[...] = windows(os, lanes(rt, 2), lanes(lf, -4))
    w = 0.4 * g + c * near_edges(g)
    qw[...] = w
    eg[...] = joint(g)
    eq[...] = joint(w)
    q[0] = jnp.zeros((40, 128), F32)
    q[37] = jnp.zeros((40, 128), F32)

    def relax(z, at):
        q[at] = 0.4 * gm[at] + cm[at] * near_main(gm, eg, z, A0)

    blocks(1, 36, A0, relax, U0)

    def residual(z, at):
        v = 0.04 * f[pl.ds(z - 3, B0)] + sm[at, :32, :] * near_main(q, eq, z, B0)[:, :32]
        e[pl.ds((z - 3) // 2, B0 // 2)] = pair_sum(v)

    blocks(3, 32, B0, residual, U0)
    a = e[:, pl.ds(0, 16, 2), :] + e[:, pl.ds(1, 16, 2), :]
    lo = select_matrix((128, 128), lambda i, o: i // 2 == o, 0.125)
    hi = select_matrix((128, 128), lambda i, o: i // 2 == o - 64, 0.125)
    f1[...] = dot3(a[:8], lo) + dot3(a[8:], hi)


SLOTS = 5


def k_pack(own, full, to_right, to_left):
    iz = lax.axis_index("gz")
    lane = iota((16, 128), 1) % 64
    n = own.shape[0]
    for group in range(to_right.shape[0]):
        count = min(SLOTS, n - SLOTS * group)
        a, b, kept = None, None, []
        for j in range(count):
            z = SLOTS * group + j
            own_half = iz == (0 if z < n // 2 else 1)
            v = own[z % (n // 2) + jnp.where(own_half, 0, n // 2)]
            kept.append(v)
            last, first = lanes(v, 12 * j - 52), lanes(v, 12 * j) if j else v
            a = last if a is None else jnp.where(lane >= 12 * j, last, a)
            b = first if b is None else jnp.where(lane >= 12 * j, first, b)
        full[SLOTS * group : SLOTS * group + count] = jnp.stack(kept)
        to_right[group] = a
        to_left[group] = b


def joined(own, xl, xr, at, ix):
    lf = jnp.where(ix > 0, xl[at], 0.0)
    rt = jnp.where(ix < 7, xr[at], 0.0)
    sub = iota((rt.shape[0], 8, 128), 1)
    edge = jnp.where(sub < 4, rt[:, 8:16], lf[:, 0:8])
    return jnp.concatenate([own[at], rt[:, 0:8], edge, lf[:, 8:16]], axis=1)


def opened(own, xl, xr, z, n, ix, iy):
    groups = -(-n // SLOTS)
    mid = joined(own, xl, xr, pl.ds(z, 4), ix)
    need = range(z // SLOTS, (z + 3) // SLOTS + 1)
    lf = [joined(own, xl, xr, pl.ds(n + i, 1), ix)[0] for i in need]
    rt = [joined(own, xl, xr, pl.ds(n + groups + i, 1), ix)[0] for i in need]
    lf = [jnp.where(iy > 0, v, 0.0) for v in lf]
    rt = [jnp.where(iy < 7, v, 0.0) for v in rt]
    at = [((z + i) // SLOTS - need[0], (z + i) % SLOTS) for i in range(4)]
    lf = jnp.stack([lanes(lf[i], 116 - 12 * j) for i, j in at])
    rt = jnp.stack([lanes(rt[i], 64 - 12 * j) for i, j in at])
    lane = iota(mid.shape, 2)
    first = jnp.where(lane < 64, mid, jnp.where(lane < 96, rt, lf))
    second = jnp.where(lane >= 64, mid, jnp.where(lane < 32, rt, lf))
    return first, lanes(second, 64)


def halve_x(ref, n, x2):
    x2[:, 14:18, :] = jnp.zeros((n, 4, 128), F32)
    x2[:, 0:14, :] = ref[:, pl.ds(0, 14, 2), :] + ref[:, pl.ds(1, 14, 2), :]
    x2[:, 18:24, :] = ref[:, pl.ds(28, 6, 2), :] + ref[:, pl.ds(29, 6, 2), :]
    return x2[...]


def down_matrix():
    return select_matrix(
        (128, 128),
        lambda i, o: ((i // 2 == o) & (o < 38)) | ((i // 2 == o - 64) & (o >= 122)),
        0.125,
    )


def level3_rows(v, e2):
    half = select_matrix((128, 128), lambda i, o: (i // 2 == o) & (o < 16), 0.125)
    v = v.reshape(8, 2, 24, 128)
    e2[...] = v[:, 0, :8, :] + v[:, 1, :8, :]
    pairs = e2[:, pl.ds(0, 4, 2), :] + e2[:, pl.ds(1, 4, 2), :]
    total = dot(pairs[0], half)
    for j in range(1, 8):
        total = total + lanes(dot(pairs[j], half), 16 * j)
    return total


def k_coeff(own, xl, xr, s1, c1, w1, s2, c2, w2, sk3, ps, pk, x2, e2):
    ix, iy = lax.axis_index("gx"), lax.axis_index("gy")

    for z in range(0, 32, 4):
        at = pl.ds(z, 4)
        s, k = opened(own, xl, xr, z, 32, ix, iy)
        s1[at] = s
        w1[at], c1[at] = factors(s, k, 1)
        ps[pl.ds(z // 2, 2)] = pair_sum(s)
        pk[pl.ds(z // 2, 2)] = pair_sum(k)
    down = down_matrix()
    s = dot3(halve_x(ps, 16, x2), down)
    k = dot3(halve_x(pk, 16, x2), down)
    s2[...] = s
    w2[...], c2[...] = factors(s, k, 2)
    sk3[...] = jnp.concatenate([level3_rows(s, e2), level3_rows(k, e2)], axis=0)


def k_down12(own, xl, xr, s1, c1, w1, s2, c2, w2, sk3, g, q, g2, q2, chunk, f, e, x2, e2):
    ix, iy = lax.axis_index("gx"), lax.axis_index("gy")
    for ref in (g, q):
        ref[0] = jnp.zeros((40, 128), F32)
        ref[33] = jnp.zeros((40, 128), F32)

    for z in range(0, 16, 4):
        for i, v in enumerate(opened(own, xl, xr, z, 16, ix, iy)):
            first = z + 8 * (z // 8) + 8 * i
            f[pl.ds(first, 4)] = v
            g[pl.ds(first + 1, 4)] = w1[pl.ds(first, 4)] * v

    def relax(z, at):
        q[at] = 0.4 * g[at] + c1[pl.ds(z - 1, A1)] * near(g, z, A1)

    blocks(1, 32, A1, relax, U1)
    wh, _ = weights(1)

    def residual(z, at):
        own = pl.ds(z - 1, A1)
        v = 0.04 * f[own] + (wh * s1[own]) * near(q, z, A1)
        e[pl.ds((z - 1) // 2, A1 // 2)] = pair_sum(v)

    blocks(1, 32, A1, residual, U1)
    fv = dot3(halve_x(e, 16, x2), down_matrix())
    gv = w2[...] * fv
    zero = jnp.zeros((1, 24, 128), F32)

    def spread(v):
        w = jnp.concatenate([zero, v, zero], axis=0)
        return around(w[:16], v, w[2:])

    qv = 0.4 * gv + c2[...] * spread(gv)
    wh, _ = weights(2)
    ev = 0.04 * fv + (wh * s2[...]) * spread(qv)
    g2[...] = gv
    q2[...] = qv
    parts = [level3_rows(ev, e2), sk3[:4], sk3[4:]]
    parts = [pltpu.roll(part, 16 * iy, 1) for part in parts]

    def copy(n, _):
        for i in range(3):
            chunk[3 * n + i] = parts[i]
        return 0

    lax.fori_loop(0, 64, copy, 0, unroll=8)


def spread_in(shape, last):
    n, r, _ = shape
    row, col = iota(shape, 1), iota(shape, 2)
    zero = jnp.zeros((1,) + shape[1:], F32)

    def apply(v):
        w = jnp.concatenate([zero, v, zero], axis=0)
        x = jnp.where(row > 0, rows(v, 1), 0.0) + jnp.where(row < r - 1, rows(v, -1), 0.0)
        y = jnp.where(col > 0, lanes(v, 1), 0.0) + jnp.where(col < last, lanes(v, -1), 0.0)
        return 0.25 * (w[:n] + w[2:]) + x + y

    return apply


def k_whole(gathered, u, t3, x4, p3):
    ix, iy = lax.axis_index("gx"), lax.axis_index("gy")
    lane = iota((4, 128), 1) // 16
    for j in range(8):
        for n in range(3):
            for x in range(8):
                v = gathered[x * 24 + n]
                for y in range(1, 8):
                    v = jnp.where(lane == (j + y) % 8, gathered[x * 24 + 3 * y + n], v)
                t3[n, j, 4 * x : 4 * x + 4, :] = lanes(v, -16 * j) if j else v
    f3, s3, k3 = t3[0], t3[1], t3[2]
    near3 = spread_in((8, 32, 128), 127)
    w3, c3 = factors(s3, k3, 3)
    g3 = w3 * f3
    q3 = 0.4 * g3 + c3 * near3(g3)
    e3 = 0.04 * f3 + (weights(3)[0] * s3) * near3(q3)
    half = select_matrix((128, 128), lambda i, o: i // 2 == o, 0.125)
    fields = []
    for v in (e3, s3, k3):
        w = v.reshape(4, 2, 32, 128)
        x4[...] = w[:, 0] + w[:, 1]
        fields.append(dot3(x4[:, pl.ds(0, 16, 2), :] + x4[:, pl.ds(1, 16, 2), :], half))
    f4, s4, k4 = fields
    near4 = spread_in((4, 16, 128), 63)
    w4, c4 = factors(s4, k4, 4)
    g4 = w4 * f4
    v4 = g4
    for _ in range(COARSE_SWEEPS):
        v4 = (0.2 * v4 + g4) + c4 * near4(v4)
    u4 = dot3(unscale(v4, s4), select_matrix((128, 128), lambda i, o: i == o // 2))
    p3[:, pl.ds(0, 16, 2), :] = u4
    p3[:, pl.ds(1, 16, 2), :] = u4
    w = p3[...]
    w = jnp.broadcast_to(w[:, None], (4, 2, 32, 128)).reshape(8, 32, 128)
    v3 = (q3 + 0.8 * g3) + s3 * w
    for _ in range(2):
        v3 = (0.2 * v3 + g3) + c3 * near3(v3)
    pick = select_matrix(
        (128, 128),
        lambda i, o: i == (jnp.where(o < 64, o // 2, 127 - (127 - o) // 2) + 16 * iy) % 128,
    )
    u[...] = pltpu.roll(dot3(v3 / s3, pick), (32 - 4 * ix) % 32, 1)


def k_up2(u3, g2, c2, s2, q2, u, p2):
    p2[:, 14:18, :] = jnp.zeros((8, 4, 128), F32)
    for n in range(2):
        p2[:, pl.ds(n, 7, 2), :] = u3[:, 0:7, :]
        p2[:, pl.ds(18 + n, 3, 2), :] = u3[:, 29:32, :]
    w = p2[...]
    w = jnp.broadcast_to(w[:, None], (8, 2, 24, 128)).reshape(16, 24, 128)
    gv, cv, sv = g2[...], c2[...], s2[...]
    zero = jnp.zeros((1, 24, 128), F32)
    v = (q2[...] + 0.8 * gv) + sv * w
    for _ in range(2):
        w = jnp.concatenate([zero, v, zero], axis=0)
        v = (0.2 * v + gv) + cv * around(w[:16], v, w[2:])
    pick = select_matrix(
        (128, 128),
        lambda i, o: i == jnp.where(o < 96, o // 2, 127 - (127 - o) // 2),
    )
    u[...] = dot3(unscale(v, sv), pick)


def k_up1(u2, g1, c1, s1, q1, u, p1, va, vb):
    for n in range(2):
        p1[:, pl.ds(n, 14, 2), :] = u2[:, 0:14, :]
        p1[:, pl.ds(28 + n, 6, 2), :] = u2[:, 18:24, :]
    for ref in (va, vb, u):
        ref[0] = jnp.zeros((40, 128), F32)
        ref[33] = jnp.zeros((40, 128), F32)

    def start(z, at):
        t = p1[pl.ds((z - 1) // 2, A1 // 2)]
        t = jnp.broadcast_to(t[:, None], (A1 // 2, 2, 40, 128)).reshape(A1, 40, 128)
        va[at] = (q1[at] + 0.8 * g1[at]) + s1[pl.ds(z - 1, A1)] * t

    blocks(1, 32, A1, start, U1)

    def sweep(z, at):
        vb[at] = (0.2 * va[at] + g1[at]) + c1[pl.ds(z - 1, A1)] * near(va, z, A1)

    blocks(1, 32, A1, sweep, U1)

    def last(z, at):
        own = pl.ds(z - 1, A1)
        v = (0.2 * vb[at] + g1[at]) + c1[own] * near(vb, z, A1)
        u[at] = unscale(v, s1[own])

    blocks(1, 32, A1, last, U1)


def k_up0(
    u1, gm, cm, sm, q, gw, cw, sw, qw, out, pm, pw, pv, wa, wb, ea, eb, done, sem
):
    iz = lax.axis_index("gz")

    def source(i, o):
        y = jnp.where(o % 16 < 8, 125 + o % 16, o % 16 - 11)
        return i == jnp.where(o < 128, o // 2, ((y + 256) // 2) % 128)

    u = u1[pl.ds(16 * iz, 18)]
    sub = iota((18, 8, 128), 1)
    u = jnp.concatenate([u[:, :16], jnp.where(sub < 4, u[:, 16:24], u[:, 32:40])], axis=1)
    u = dot3(u, select_matrix((128, 256), source))
    for h, ref in enumerate((pm, pw)):
        w = u[:, :, 128 * h : 128 * h + 128]
        for n in range(2):
            ref[:, pl.ds(n, 18, 2), :] = w[:, 0:18]
            ref[:, pl.ds(36 + n, 2, 2), :] = w[:, 22:24]
    pv[...] = lanes(pw[...], 8)
    slot = iota((40, 128), 1) // 8
    parts = []
    for side in range(2):
        for group in range(3):
            total = None
            for j in range(16):
                ref = pw if j % 2 == side else pv
                part = ref[min(max((16 * group + j - 1) // 2, 0), 17)]
                total = part if total is None else jnp.where(slot >= j, part, total)
            parts.append(total[None])
    g, c = gw[...], cw[...]
    v = (qw[...] + 0.8 * g) + sw[...] * jnp.concatenate(parts, axis=0)
    ea[...] = joint(v)
    eb[...] = joint((0.2 * v + g) + c * near_edges(v))

    def start(z, at):
        t = jnp.stack([pm[(z + i - 1) // 2] for i in range(A0)])
        wa[at] = (q[at] + 0.8 * gm[at]) + sm[at] * t

    blocks(1, 36, A0, start, U0)
    wa[0] = jnp.zeros((40, 128), F32)
    wa[37] = jnp.zeros((40, 128), F32)

    def sweep(z, at):
        wb[at] = (0.2 * wa[at] + gm[at]) + cm[at] * near_main(wa, ea, z, A0)

    blocks(1, 36, A0, sweep, U0)

    copies = []
    for b in range(32 // B0):
        z = 3 + b * B0
        at = pl.ds(z, B0)
        n = near_main(wb, eb, z, B0)[:, :32]
        v = (0.2 * wb[at, :32, :] + gm[at, :32, :]) + cm[at, :32, :] * n
        part = pl.ds(z - 3, B0)
        done[part] = v / sm[at, :32, :]
        copies.append(pltpu.make_async_copy(done.at[part], out.at[part], sem.at[b]))
        copies[-1].start()
    for copy in copies:
        copy.wait()


def ring(v, axis, step):
    n = lax.axis_size(axis)
    return lax.ppermute(v, axis, [(i, (i + step) % n) for i in range(n)])


def pair(to_right, to_left, axis):
    return ring(to_right, axis, 1), ring(to_left, axis, -1)


def pack_level1(own):
    n = own.shape[0]
    full, *msg = run(k_pack, (own,), [(n, 16, 128)] + [(-(-n // SLOTS), 16, 128)] * 2)
    return jnp.concatenate([full, *pair(*msg, "gy")], axis=0)


def after(values, *others):
    return lax.optimization_barrier((values, others))[0]


def shards(f, s, k):
    first = jnp.where(lax.axis_index("gz") == 0, 29, 0)
    fz, sz, kz = [lax.dynamic_slice_in_dim(v, first, 3, 0) for v in (f, s, k)]
    sw, c = factors(sz, kz, 0)
    near = (sw * fz, c, jnp.where(kz > 0.0, sz, 0.0))
    zr = ring(run(k_face_z, near, [(7, 32, 128)])[0], "gz", 1)
    g, c, sk1 = run(
        k_load, (f, s, k), [(32, 32, 128)] * 2 + [(16, 16, 128)], [(16, 32, 128)] * 2
    )
    sk1 = after(sk1, zr)
    sk_z = ring(sk1, "gz", 1)
    xs = pair(*run(k_face_x, (g, c, s, zr), [(38, 8, 128)] * 2), "gx")
    small, both = [(3, 40, 128)], [(6, 40, 128)]
    edges = run(k_pack_own, (g, c, s), small * 3)
    *edges, to_right, to_left = run(k_face_y, (*edges, zr, *xs), small * 5)
    ys = pair(to_right, to_left, "gy")
    gm, cm, sm = run(k_assemble, (g, c, s, zr, *xs), [(38, 40, 128)] * 3)
    sk1, sk_z = after((sk1, sk_z), to_left)
    sk_y = pack_level1(jnp.concatenate([sk1, sk_z], axis=0))
    gw, cw, sw, q0, qw, f1 = run(
        k_down0,
        (f, gm, cm, sm, *edges, *ys),
        both * 3 + [(38, 40, 128)] + both + [(8, 16, 128)],
        [(16, 32, 128)] + small * 2,
    )
    sk = after(sk_y, f1)
    f1 = jnp.concatenate([f1, ring(f1, "gz", 1)], axis=0)
    s1, c1, w1, s2, c2, w2, sk3 = run(
        k_coeff,
        (sk, *pair(sk, sk, "gx")),
        [(32, 40, 128)] * 3 + [(16, 24, 128)] * 3 + [(8, 128)],
        [(16, 40, 128)] * 2 + [(16, 24, 128), (8, 8, 128)],
    )
    f1 = pack_level1(f1)
    g1, q1, g2, q2, chunk = run(
        k_down12,
        (f1, *pair(f1, f1, "gx"), s1, c1, w1, s2, c2, w2, sk3),
        [(34, 40, 128)] * 2 + [(16, 24, 128)] * 2 + [(192, 4, 128)],
        [(32, 40, 128), (16, 40, 128), (16, 24, 128), (8, 8, 128)],
    )
    gathered = lax.all_to_all(chunk, ("gx", "gy"), 0, 0, tiled=True)
    (u3,) = run(
        k_whole, (gathered,), [(8, 32, 128)], [(3, 8, 32, 128), (4, 32, 128), (4, 32, 128)]
    )
    (u2,) = run(k_up2, (u3, g2, c2, s2, q2), [(16, 24, 128)], [(8, 24, 128)])
    (u1,) = run(
        k_up1, (u2, g1, c1, s1, q1), [(34, 40, 128)], [(16, 40, 128)] + [(34, 40, 128)] * 2
    )
    (out,) = run(
        k_up0,
        (u1, gm, cm, sm, q0, gw, cw, sw, qw),
        [(32, 32, 128)],
        [(18, 40, 128)] * 3 + [(38, 40, 128)] * 2 + small * 2 + [(32, 32, 128)],
        HBM,
        [(32 // B0,)],
    )
    return out


def solution(mesh):
    return jax.shard_map(
        shards,
        mesh=mesh,
        in_specs=(P("gz", "gx", "gy"),) * 3,
        out_specs=P("gz", "gx", "gy"),
        check_vma=False,
    )
```

```python
import math

import jax
import jax.numpy as jnp
from jax import lax
from jax.experimental import pallas as pl
from jax.experimental.pallas import tpu as pltpu
from jax.sharding import PartitionSpec as P

F32 = jnp.float32
VM = pl.BlockSpec(memory_space=pltpu.VMEM)
HBM = pl.BlockSpec(memory_space=pltpu.HBM)
BF16 = jnp.bfloat16
COARSE_SWEEPS = 11
MICROSECONDS = dict(
    k_face_z=0.2,
    k_load=4.0,
    k_face_x=0.2,
    k_pack_own=1.0,
    k_face_y=0.6,
    k_assemble=1.0,
    k_pack=0.3,
    k_down0=2.0,
    k_coeff=2.0,
    k_down12=3.0,
    k_whole=2.0,
    k_up2=0.5,
    k_up1=1.5,
    k_up0=2.5,
)
A0, B0, U0 = 12, 8, 3
A1, U1 = 4, 8


def run(body, args, outs, scratch=(), out_spec=VM, sems=()):
    words = sum(math.prod(s) for s in (*outs, *scratch)) + sum(a.size for a in args)
    return pl.pallas_call(
        body,
        out_shape=[jax.ShapeDtypeStruct(o, F32) for o in outs],
        in_specs=[VM] * len(args),
        out_specs=[out_spec] * len(outs),
        scratch_shapes=[pltpu.VMEM(s, F32) for s in scratch]
        + [pltpu.SemaphoreType.DMA(n) for n in sems],
        compiler_params=pltpu.CompilerParams(vmem_limit_bytes=6 * words + (6 << 20)),
        cost_estimate=pl.CostEstimate(
            flops=0, transcendentals=0, bytes_accessed=int(3.5e6 * MICROSECONDS[body.__name__])
        ),
    )(*args)


def weights(level):
    wh = 0.25**level
    return wh, 2.0 * (0.25 * wh + 2.0 * wh)


def iota(shape, dim):
    return lax.broadcasted_iota(jnp.int32, shape, dim)


def lanes(v, shift):
    return pltpu.roll(v, shift % v.shape[-1], v.ndim - 1)


def rows(v, shift):
    return pltpu.roll(v, shift % v.shape[-2], v.ndim - 2)


def beside(v):
    return (rows(v, 1) + rows(v, -1)) + (lanes(v, 1) + lanes(v, -1))


def around(above, v, below):
    return 0.25 * (above + below) + beside(v)


def factors(s, k, level):
    wh, full = weights(level)
    diagonal = k + full * (s * s)
    sw = s * (0.8 / jnp.where(diagonal > 0.0, diagonal, 1.0))
    return sw, (wh * s) * sw


def unscale(v, s):
    inside = s > 0.0
    return jnp.where(inside, v / jnp.where(inside, s, 1.0), 0.0)


def dot(a, b):
    b = b.astype(BF16)
    high = a.astype(BF16)
    rest = a - high.astype(F32)
    middle = rest.astype(BF16)
    low = (rest - middle.astype(F32)).astype(BF16)
    terms = [jnp.dot(t, b, preferred_element_type=F32) for t in (high, middle, low)]
    return terms[0] + (terms[1] + terms[2])


def dot3(a, b):
    n, r, c = a.shape
    return dot(a.reshape(n * r, c), b).reshape(n, r, b.shape[1])


def blocks(first, count, size, body, unroll=1):
    def one(b, _):
        z = first + size * b
        body(z, pl.ds(z, size))
        return 0

    lax.fori_loop(0, count // size, one, 0, unroll=unroll)


def pair_sum(v):
    v = v.reshape(v.shape[0] // 2, 2, *v.shape[1:])
    return v[:, 0] + v[:, 1]


def select_matrix(shape, source_of, scale=1.0):
    i, o = iota(shape, 0), iota(shape, 1)
    return jnp.where(source_of(i, o), scale, 0.0).astype(F32)


def k_face_z(g, c, s, zmsg):
    upper = lax.axis_index("gz") == 0
    zmsg[0:3] = g[...]
    zmsg[3:5] = jnp.where(upper, c[1:], c[:2])
    zmsg[5:7] = jnp.where(upper, s[1:], s[:2])


def k_load(f, s, k, g, c, sk1, ps, pk):
    def one(z, at):
        sv, kv = s[at], k[at]
        sw, cv = factors(sv, kv, 0)
        g[at] = sw * f[at]
        c[at] = cv
        ps[pl.ds(z // 2, 2)] = pair_sum(sv)
        pk[pl.ds(z // 2, 2)] = pair_sum(kv)

    blocks(0, 32, 4, one, 2)
    a = ps[:, pl.ds(0, 16, 2), :] + ps[:, pl.ds(1, 16, 2), :]
    b = pk[:, pl.ds(0, 16, 2), :] + pk[:, pl.ds(1, 16, 2), :]
    left = select_matrix((128, 128), lambda i, o: i // 2 == o, 0.125)
    right = select_matrix((128, 128), lambda i, o: i // 2 == o - 64, 0.125)
    sk1[...] = dot3(a, left) + dot3(b, right)


def halo_rows(zr, iz, field, z):
    first, depth = ((0, 3), (3, 2), (5, 2))[field]
    d = z - 35 if z > 34 else 2 - z
    if d >= depth:
        return jnp.zeros(zr.shape[1:], F32)
    row = first + (d if z > 34 else depth - 1 - d)
    return jnp.where(iz == (0 if z > 34 else 1), zr[row], 0.0)


def k_face_x(g, c, s, zr, to_right, to_left):
    iz = lax.axis_index("gz")
    sub = iota((8, 128), 0)

    def put(z, gz, cz, sz):
        a, b, d = gz[24:32], cz[24:32], sz[24:32]
        to_right[z] = jnp.where(sub >= 5, a, jnp.where(sub >= 3, rows(b, -3), rows(d, -5)))
        a, b, d = gz[0:8], cz[0:8], sz[0:8]
        to_left[z] = jnp.where(sub < 3, a, jnp.where(sub < 5, rows(b, 3), rows(d, 5)))

    def one(z, _):
        put(z + 3, g[z], c[z], s[z])
        return 0

    lax.fori_loop(0, 32, one, 0, unroll=4)
    for z in (0, 1, 2, 35, 36, 37):
        put(z, *[halo_rows(zr, iz, n, z) for n in range(3)])


def k_pack_own(g, c, s, *own):
    slot = iota((32, 128), 1)
    for ref, out in zip((g, c, s), own):
        out[...] = jnp.zeros((3, 40, 128), F32)
        for group in range(3):
            total = jnp.zeros((32, 128), F32)
            for j in range(16):
                z = 16 * group + j - 3
                if 0 <= z < 32:
                    total = jnp.where(slot >= 8 * j, lanes(ref[z], 8 * j + 3), total)
                elif z == 32:
                    total = jnp.where(slot >= 8 * j, 0.0, total)
            out[group, :32, :] = total


def side_rows(from_left, from_right, ix, z):
    sub = iota((8, 128), 0)
    lf = jnp.where(ix > 0, from_left[z], 0.0)
    rt = jnp.where(ix < 7, from_right[z], 0.0)
    return (
        jnp.where(sub >= 4, lf, rt),
        jnp.where(sub >= 4, rows(lf, 3), rows(rt, -3)),
        jnp.where(sub >= 4, rows(lf, 5), rows(rt, -5)),
    )


def k_face_y(og, oc, os, zr, from_left, from_right, ag, ac, a_s, to_right, to_left):
    ix, iz = lax.axis_index("gx"), lax.axis_index("gz")
    slot = iota((8, 128), 1)
    wide = iota((32, 128), 1)
    lane = iota((40, 128), 1) % 8
    for group in range(3):
        side = [jnp.zeros((8, 128), F32)] * 3
        mid = [ref[group, :32, :] for ref in (og, oc, os)]
        for j in range(16 if group < 2 else 6):
            z = 16 * group + j
            here = side_rows(from_left, from_right, ix, z)
            for n in range(3):
                side[n] = jnp.where(slot >= 8 * j, lanes(here[n], 8 * j + 3), side[n])
                if z < 3 or z > 34:
                    edge = lanes(halo_rows(zr, iz, n, z), 8 * j + 3)
                    mid[n] = jnp.where(wide // 8 == j, edge, mid[n])
        g, c, s = [jnp.concatenate(parts, axis=0) for parts in zip(mid, side)]
        ag[group] = g
        ac[group] = c
        a_s[group] = s
        to_right[group] = jnp.where(
            lane < 3, g, jnp.where(lane < 5, lanes(c, 2), lanes(s, 4))
        )
        to_left[group] = jnp.where(
            lane >= 6, lanes(c, 3), jnp.where(lane >= 3, g, lanes(s, -2))
        )


def k_assemble(g, c, s, zr, from_left, from_right, gm, cm, sm):
    ix, iz = lax.axis_index("gx"), lax.axis_index("gz")

    def put(z, values):
        for ref, mid, side in zip(
            (gm, cm, sm), values, side_rows(from_left, from_right, ix, z)
        ):
            ref[z] = jnp.concatenate([mid, side], axis=0)

    def one(z, _):
        put(z + 3, (g[z], c[z], s[z]))
        return 0

    lax.fori_loop(0, 32, one, 0, unroll=4)
    for z in (0, 1, 2, 35, 36, 37):
        put(z, [halo_rows(zr, iz, n, z) for n in range(3)])


def near_edges(v):
    lane = iota(v.shape, 2)
    zero = jnp.zeros((1,) + v.shape[1:], F32)
    up, down = lanes(v, 8), lanes(v, -8)
    above = jnp.where(lane < 8, jnp.concatenate([zero, up[:-1]], axis=0), up)
    below = jnp.where(lane >= 120, jnp.concatenate([down[1:], zero], axis=0), down)
    return around(above, v, below)


def joint(v):
    lane = iota((3,) + v.shape[1:], 2)
    return jnp.where(lane % 8 == 4, lanes(v[3:], 2), v[:3])


def near_main(ref, edge, z, n, product=False):
    v = ref[pl.ds(z, n)]
    lane = iota(v.shape, 2)
    e = jnp.stack(
        [
            pltpu.roll(edge[(z + i) // 16], (124 - 8 * ((z + i) % 16)) % 128, 1)
            for i in range(n)
        ]
    )
    if product:
        across = dot3(v, select_matrix((128, 128), lambda i, o: (i == o + 1) | (i == o - 1)))
        across = jnp.where((lane == 0) | (lane == 127), e + across, across)
    else:
        across = jnp.where(lane == 0, e, lanes(v, 1)) + jnp.where(lane == 127, e, lanes(v, -1))
    above, below = ref[pl.ds(z - 1, n)], ref[pl.ds(z + 1, n)]
    return 0.25 * (above + below) + ((rows(v, 1) + rows(v, -1)) + across)


def near(ref, z, n):
    return around(ref[pl.ds(z - 1, n)], ref[pl.ds(z, n)], ref[pl.ds(z + 1, n)])


def k_down0(
    f, gm, cm, sm, og, oc, os, from_left, from_right, gw, cw, sw, q, qw, f1, e, eg, eq
):
    iy = lax.axis_index("gy")
    own = iota((3, 40, 128), 2) % 8 < 3
    lf = jnp.where(iy > 0, from_left[...], 0.0)
    rt = jnp.where(iy < 7, from_right[...], 0.0)

    def windows(ref, right, left):
        mid = ref[...]
        return jnp.concatenate(
            [jnp.where(own, mid, right), jnp.where(own, left, mid)], axis=0
        )

    g = windows(og, rt, lf)
    c = windows(oc, lanes(rt, -3), lanes(lf, -2))
    gw[...] = g
    cw[...] = c
    sw[...] = windows(os, lanes(rt, 2), lanes(lf, -4))
    w = 0.4 * g + c * near_edges(g)
    qw[...] = w
    eg[...] = joint(g)
    eq[...] = joint(w)
    q[0] = jnp.zeros((40, 128), F32)
    q[37] = jnp.zeros((40, 128), F32)

    def relax(z, at):
        q[at] = 0.4 * gm[at] + cm[at] * near_main(gm, eg, z, A0, True)

    blocks(1, 36, A0, relax, U0)

    def residual(z, at):
        v = 0.04 * f[pl.ds(z - 3, B0)] + sm[at, :32, :] * near_main(q, eq, z, B0, True)[:, :32]
        e[pl.ds((z - 3) // 2, B0 // 2)] = pair_sum(v)

    blocks(3, 32, B0, residual, U0)
    a = e[:, pl.ds(0, 16, 2), :] + e[:, pl.ds(1, 16, 2), :]
    lo = select_matrix((128, 128), lambda i, o: i // 2 == o, 0.125)
    hi = select_matrix((128, 128), lambda i, o: i // 2 == o - 64, 0.125)
    f1[...] = dot3(a[:8], lo) + dot3(a[8:], hi)


SLOTS = 5


def k_pack(own, full, to_right, to_left):
    iz = lax.axis_index("gz")
    lane = iota((16, 128), 1) % 64
    n = own.shape[0]
    for group in range(to_right.shape[0]):
        count = min(SLOTS, n - SLOTS * group)
        a, b, kept = None, None, []
        for j in range(count):
            z = SLOTS * group + j
            own_half = iz == (0 if z < n // 2 else 1)
            v = own[z % (n // 2) + jnp.where(own_half, 0, n // 2)]
            kept.append(v)
            last, first = lanes(v, 12 * j - 52), lanes(v, 12 * j) if j else v
            a = last if a is None else jnp.where(lane >= 12 * j, last, a)
            b = first if b is None else jnp.where(lane >= 12 * j, first, b)
        full[SLOTS * group : SLOTS * group + count] = jnp.stack(kept)
        to_right[group] = a
        to_left[group] = b


def joined(own, xl, xr, at, ix):
    lf = jnp.where(ix > 0, xl[at], 0.0)
    rt = jnp.where(ix < 7, xr[at], 0.0)
    sub = iota((rt.shape[0], 8, 128), 1)
    edge = jnp.where(sub < 4, rt[:, 8:16], lf[:, 0:8])
    return jnp.concatenate([own[at], rt[:, 0:8], edge, lf[:, 8:16]], axis=1)


def opened(own, xl, xr, z, n, ix, iy):
    groups = -(-n // SLOTS)
    mid = joined(own, xl, xr, pl.ds(z, 4), ix)
    need = range(z // SLOTS, (z + 3) // SLOTS + 1)
    lf = [joined(own, xl, xr, pl.ds(n + i, 1), ix)[0] for i in need]
    rt = [joined(own, xl, xr, pl.ds(n + groups + i, 1), ix)[0] for i in need]
    lf = [jnp.where(iy > 0, v, 0.0) for v in lf]
    rt = [jnp.where(iy < 7, v, 0.0) for v in rt]
    at = [((z + i) // SLOTS - need[0], (z + i) % SLOTS) for i in range(4)]
    lf = jnp.stack([lanes(lf[i], 116 - 12 * j) for i, j in at])
    rt = jnp.stack([lanes(rt[i], 64 - 12 * j) for i, j in at])
    lane = iota(mid.shape, 2)
    first = jnp.where(lane < 64, mid, jnp.where(lane < 96, rt, lf))
    second = jnp.where(lane >= 64, mid, jnp.where(lane < 32, rt, lf))
    return first, lanes(second, 64)


def halve_x(ref, n, x2):
    x2[:, 14:18, :] = jnp.zeros((n, 4, 128), F32)
    x2[:, 0:14, :] = ref[:, pl.ds(0, 14, 2), :] + ref[:, pl.ds(1, 14, 2), :]
    x2[:, 18:24, :] = ref[:, pl.ds(28, 6, 2), :] + ref[:, pl.ds(29, 6, 2), :]
    return x2[...]


def down_matrix():
    return select_matrix(
        (128, 128),
        lambda i, o: ((i // 2 == o) & (o < 38)) | ((i // 2 == o - 64) & (o >= 122)),
        0.125,
    )


def level3_rows(v, e2):
    half = select_matrix((128, 128), lambda i, o: (i // 2 == o) & (o < 16), 0.125)
    v = v.reshape(8, 2, 24, 128)
    e2[...] = v[:, 0, :8, :] + v[:, 1, :8, :]
    pairs = e2[:, pl.ds(0, 4, 2), :] + e2[:, pl.ds(1, 4, 2), :]
    total = dot(pairs[0], half)
    for j in range(1, 8):
        total = total + lanes(dot(pairs[j], half), 16 * j)
    return total


def k_coeff(own, xl, xr, s1, c1, w1, s2, c2, w2, sk3, ps, pk, x2, e2):
    ix, iy = lax.axis_index("gx"), lax.axis_index("gy")

    for z in range(0, 32, 4):
        at = pl.ds(z, 4)
        s, k = opened(own, xl, xr, z, 32, ix, iy)
        s1[at] = s
        w1[at], c1[at] = factors(s, k, 1)
        ps[pl.ds(z // 2, 2)] = pair_sum(s)
        pk[pl.ds(z // 2, 2)] = pair_sum(k)
    down = down_matrix()
    s = dot3(halve_x(ps, 16, x2), down)
    k = dot3(halve_x(pk, 16, x2), down)
    s2[...] = s
    w2[...], c2[...] = factors(s, k, 2)
    sk3[...] = jnp.concatenate([level3_rows(s, e2), level3_rows(k, e2)], axis=0)


def k_down12(own, xl, xr, s1, c1, w1, s2, c2, w2, sk3, g, q, g2, q2, chunk, f, e, x2, e2):
    ix, iy = lax.axis_index("gx"), lax.axis_index("gy")
    for ref in (g, q):
        ref[0] = jnp.zeros((40, 128), F32)
        ref[33] = jnp.zeros((40, 128), F32)

    for z in range(0, 16, 4):
        for i, v in enumerate(opened(own, xl, xr, z, 16, ix, iy)):
            first = z + 8 * (z // 8) + 8 * i
            f[pl.ds(first, 4)] = v
            g[pl.ds(first + 1, 4)] = w1[pl.ds(first, 4)] * v

    def relax(z, at):
        q[at] = 0.4 * g[at] + c1[pl.ds(z - 1, A1)] * near(g, z, A1)

    blocks(1, 32, A1, relax, U1)
    wh, _ = weights(1)

    def residual(z, at):
        own = pl.ds(z - 1, A1)
        v = 0.04 * f[own] + (wh * s1[own]) * near(q, z, A1)
        e[pl.ds((z - 1) // 2, A1 // 2)] = pair_sum(v)

    blocks(1, 32, A1, residual, U1)
    fv = dot3(halve_x(e, 16, x2), down_matrix())
    gv = w2[...] * fv
    zero = jnp.zeros((1, 24, 128), F32)

    def spread(v):
        w = jnp.concatenate([zero, v, zero], axis=0)
        return around(w[:16], v, w[2:])

    qv = 0.4 * gv + c2[...] * spread(gv)
    wh, _ = weights(2)
    ev = 0.04 * fv + (wh * s2[...]) * spread(qv)
    g2[...] = gv
    q2[...] = qv
    parts = [level3_rows(ev, e2), sk3[:4], sk3[4:]]
    parts = [pltpu.roll(part, 16 * iy, 1) for part in parts]

    def copy(n, _):
        for i in range(3):
            chunk[3 * n + i] = parts[i]
        return 0

    lax.fori_loop(0, 64, copy, 0, unroll=8)


def spread_in(shape, last):
    n, r, _ = shape
    row, col = iota(shape, 1), iota(shape, 2)
    zero = jnp.zeros((1,) + shape[1:], F32)

    def apply(v):
        w = jnp.concatenate([zero, v, zero], axis=0)
        x = jnp.where(row > 0, rows(v, 1), 0.0) + jnp.where(row < r - 1, rows(v, -1), 0.0)
        y = jnp.where(col > 0, lanes(v, 1), 0.0) + jnp.where(col < last, lanes(v, -1), 0.0)
        return 0.25 * (w[:n] + w[2:]) + x + y

    return apply


def k_whole(gathered, u, t3, x4, p3):
    ix, iy = lax.axis_index("gx"), lax.axis_index("gy")
    lane = iota((4, 128), 1) // 16
    for j in range(8):
        for n in range(3):
            for x in range(8):
                v = gathered[x * 24 + n]
                for y in range(1, 8):
                    v = jnp.where(lane == (j + y) % 8, gathered[x * 24 + 3 * y + n], v)
                t3[n, j, 4 * x : 4 * x + 4, :] = lanes(v, -16 * j) if j else v
    f3, s3, k3 = t3[0], t3[1], t3[2]
    near3 = spread_in((8, 32, 128), 127)
    w3, c3 = factors(s3, k3, 3)
    g3 = w3 * f3
    q3 = 0.4 * g3 + c3 * near3(g3)
    e3 = 0.04 * f3 + (weights(3)[0] * s3) * near3(q3)
    half = select_matrix((128, 128), lambda i, o: i // 2 == o, 0.125)
    fields = []
    for v in (e3, s3, k3):
        w = v.reshape(4, 2, 32, 128)
        x4[...] = w[:, 0] + w[:, 1]
        fields.append(dot3(x4[:, pl.ds(0, 16, 2), :] + x4[:, pl.ds(1, 16, 2), :], half))
    f4, s4, k4 = fields
    near4 = spread_in((4, 16, 128), 63)
    w4, c4 = factors(s4, k4, 4)
    g4 = w4 * f4
    v4 = g4
    for _ in range(COARSE_SWEEPS):
        v4 = (0.2 * v4 + g4) + c4 * near4(v4)
    u4 = dot3(unscale(v4, s4), select_matrix((128, 128), lambda i, o: i == o // 2))
    p3[:, pl.ds(0, 16, 2), :] = u4
    p3[:, pl.ds(1, 16, 2), :] = u4
    w = p3[...]
    w = jnp.broadcast_to(w[:, None], (4, 2, 32, 128)).reshape(8, 32, 128)
    v3 = (q3 + 0.8 * g3) + s3 * w
    for _ in range(2):
        v3 = (0.2 * v3 + g3) + c3 * near3(v3)
    pick = select_matrix(
        (128, 128),
        lambda i, o: i == (jnp.where(o < 64, o // 2, 127 - (127 - o) // 2) + 16 * iy) % 128,
    )
    u[...] = pltpu.roll(dot3(v3 / s3, pick), (32 - 4 * ix) % 32, 1)


def k_up2(u3, g2, c2, s2, q2, u, p2):
    p2[:, 14:18, :] = jnp.zeros((8, 4, 128), F32)
    for n in range(2):
        p2[:, pl.ds(n, 7, 2), :] = u3[:, 0:7, :]
        p2[:, pl.ds(18 + n, 3, 2), :] = u3[:, 29:32, :]
    w = p2[...]
    w = jnp.broadcast_to(w[:, None], (8, 2, 24, 128)).reshape(16, 24, 128)
    gv, cv, sv = g2[...], c2[...], s2[...]
    zero = jnp.zeros((1, 24, 128), F32)
    v = (q2[...] + 0.8 * gv) + sv * w
    for _ in range(2):
        w = jnp.concatenate([zero, v, zero], axis=0)
        v = (0.2 * v + gv) + cv * around(w[:16], v, w[2:])
    pick = select_matrix(
        (128, 128),
        lambda i, o: i == jnp.where(o < 96, o // 2, 127 - (127 - o) // 2),
    )
    u[...] = dot3(unscale(v, sv), pick)


def k_up1(u2, g1, c1, s1, q1, u, p1, va, vb):
    for n in range(2):
        p1[:, pl.ds(n, 14, 2), :] = u2[:, 0:14, :]
        p1[:, pl.ds(28 + n, 6, 2), :] = u2[:, 18:24, :]
    for ref in (va, vb, u):
        ref[0] = jnp.zeros((40, 128), F32)
        ref[33] = jnp.zeros((40, 128), F32)

    def start(z, at):
        t = p1[pl.ds((z - 1) // 2, A1 // 2)]
        t = jnp.broadcast_to(t[:, None], (A1 // 2, 2, 40, 128)).reshape(A1, 40, 128)
        va[at] = (q1[at] + 0.8 * g1[at]) + s1[pl.ds(z - 1, A1)] * t

    blocks(1, 32, A1, start, U1)

    def sweep(z, at):
        vb[at] = (0.2 * va[at] + g1[at]) + c1[pl.ds(z - 1, A1)] * near(va, z, A1)

    blocks(1, 32, A1, sweep, U1)

    def last(z, at):
        own = pl.ds(z - 1, A1)
        v = (0.2 * vb[at] + g1[at]) + c1[own] * near(vb, z, A1)
        u[at] = unscale(v, s1[own])

    blocks(1, 32, A1, last, U1)


def k_up0(
    u1, gm, cm, sm, q, gw, cw, sw, qw, out, pm, pw, pv, wa, wb, ea, eb, done, sem
):
    iz = lax.axis_index("gz")

    def source(i, o):
        y = jnp.where(o % 16 < 8, 125 + o % 16, o % 16 - 11)
        return i == jnp.where(o < 128, o // 2, ((y + 256) // 2) % 128)

    u = u1[pl.ds(16 * iz, 18)]
    sub = iota((18, 8, 128), 1)
    u = jnp.concatenate([u[:, :16], jnp.where(sub < 4, u[:, 16:24], u[:, 32:40])], axis=1)
    u = dot3(u, select_matrix((128, 256), source))
    for h, ref in enumerate((pm, pw)):
        w = u[:, :, 128 * h : 128 * h + 128]
        for n in range(2):
            ref[:, pl.ds(n, 18, 2), :] = w[:, 0:18]
            ref[:, pl.ds(36 + n, 2, 2), :] = w[:, 22:24]
    pv[...] = lanes(pw[...], 8)
    slot = iota((40, 128), 1) // 8
    parts = []
    for side in range(2):
        for group in range(3):
            total = None
            for j in range(16):
                ref = pw if j % 2 == side else pv
                part = ref[min(max((16 * group + j - 1) // 2, 0), 17)]
                total = part if total is None else jnp.where(slot >= j, part, total)
            parts.append(total[None])
    g, c = gw[...], cw[...]
    v = (qw[...] + 0.8 * g) + sw[...] * jnp.concatenate(parts, axis=0)
    ea[...] = joint(v)
    eb[...] = joint((0.2 * v + g) + c * near_edges(v))

    def start(z, at):
        t = jnp.stack([pm[(z + i - 1) // 2] for i in range(A0)])
        wa[at] = (q[at] + 0.8 * gm[at]) + sm[at] * t

    blocks(1, 36, A0, start, U0)
    wa[0] = jnp.zeros((40, 128), F32)
    wa[37] = jnp.zeros((40, 128), F32)

    def sweep(z, at):
        wb[at] = (0.2 * wa[at] + gm[at]) + cm[at] * near_main(wa, ea, z, A0, True)

    blocks(1, 36, A0, sweep, U0)

    copies = []
    for b in range(32 // B0):
        z = 3 + b * B0
        at = pl.ds(z, B0)
        n = near_main(wb, eb, z, B0)[:, :32]
        v = (0.2 * wb[at, :32, :] + gm[at, :32, :]) + cm[at, :32, :] * n
        part = pl.ds(z - 3, B0)
        done[part] = v / sm[at, :32, :]
        copies.append(pltpu.make_async_copy(done.at[part], out.at[part], sem.at[b]))
        copies[-1].start()
    for copy in copies:
        copy.wait()


def ring(v, axis, step):
    n = lax.axis_size(axis)
    return lax.ppermute(v, axis, [(i, (i + step) % n) for i in range(n)])


def pair(to_right, to_left, axis):
    return ring(to_right, axis, 1), ring(to_left, axis, -1)


def pack_level1(own):
    n = own.shape[0]
    full, *msg = run(k_pack, (own,), [(n, 16, 128)] + [(-(-n // SLOTS), 16, 128)] * 2)
    return jnp.concatenate([full, *pair(*msg, "gy")], axis=0)


def after(values, *others):
    return lax.optimization_barrier((values, others))[0]


def shards(f, s, k):
    first = jnp.where(lax.axis_index("gz") == 0, 29, 0)
    fz, sz, kz = [lax.dynamic_slice_in_dim(v, first, 3, 0) for v in (f, s, k)]
    sw, c = factors(sz, kz, 0)
    near = (sw * fz, c, jnp.where(kz > 0.0, sz, 0.0))
    zr = ring(run(k_face_z, near, [(7, 32, 128)])[0], "gz", 1)
    g, c, sk1 = run(
        k_load, (f, s, k), [(32, 32, 128)] * 2 + [(16, 16, 128)], [(16, 32, 128)] * 2
    )
    sk1 = after(sk1, zr)
    sk_z = ring(sk1, "gz", 1)
    xs = pair(*run(k_face_x, (g, c, s, zr), [(38, 8, 128)] * 2), "gx")
    small, both = [(3, 40, 128)], [(6, 40, 128)]
    edges = run(k_pack_own, (g, c, s), small * 3)
    *edges, to_right, to_left = run(k_face_y, (*edges, zr, *xs), small * 5)
    ys = pair(to_right, to_left, "gy")
    gm, cm, sm = run(k_assemble, (g, c, s, zr, *xs), [(38, 40, 128)] * 3)
    sk1, sk_z = after((sk1, sk_z), gm)
    sk_y = pack_level1(jnp.concatenate([sk1, sk_z], axis=0))
    gw, cw, sw, q0, qw, f1 = run(
        k_down0,
        (f, gm, cm, sm, *edges, *ys),
        both * 3 + [(38, 40, 128)] + both + [(8, 16, 128)],
        [(16, 32, 128)] + small * 2,
    )
    sk = after(sk_y, f1)
    f1 = jnp.concatenate([f1, ring(f1, "gz", 1)], axis=0)
    s1, c1, w1, s2, c2, w2, sk3 = run(
        k_coeff,
        (sk, *pair(sk, sk, "gx")),
        [(32, 40, 128)] * 3 + [(16, 24, 128)] * 3 + [(8, 128)],
        [(16, 40, 128)] * 2 + [(16, 24, 128), (8, 8, 128)],
    )
    f1 = pack_level1(f1)
    g1, q1, g2, q2, chunk = run(
        k_down12,
        (f1, *pair(f1, f1, "gx"), s1, c1, w1, s2, c2, w2, sk3),
        [(34, 40, 128)] * 2 + [(16, 24, 128)] * 2 + [(192, 4, 128)],
        [(32, 40, 128), (16, 40, 128), (16, 24, 128), (8, 8, 128)],
    )
    gathered = lax.all_to_all(chunk, ("gx", "gy"), 0, 0, tiled=True)
    (u3,) = run(
        k_whole, (gathered,), [(8, 32, 128)], [(3, 8, 32, 128), (4, 32, 128), (4, 32, 128)]
    )
    (u2,) = run(k_up2, (u3, g2, c2, s2, q2), [(16, 24, 128)], [(8, 24, 128)])
    (u1,) = run(
        k_up1, (u2, g1, c1, s1, q1), [(34, 40, 128)], [(16, 40, 128)] + [(34, 40, 128)] * 2
    )
    (out,) = run(
        k_up0,
        (u1, gm, cm, sm, q0, gw, cw, sw, qw),
        [(32, 32, 128)],
        [(18, 40, 128)] * 3 + [(38, 40, 128)] * 2 + small * 2 + [(32, 32, 128)],
        HBM,
        [(32 // B0,)],
    )
    return out


def solution(mesh):
    return jax.shard_map(
        shards,
        mesh=mesh,
        in_specs=(P("gz", "gx", "gy"),) * 3,
        out_specs=P("gz", "gx", "gy"),
        check_vma=False,
    )
```

```python
import math

import jax
import jax.numpy as jnp
from jax import lax
from jax.experimental import pallas as pl
from jax.experimental.pallas import tpu as pltpu
from jax.sharding import PartitionSpec as P

F32 = jnp.float32
VM = pl.BlockSpec(memory_space=pltpu.VMEM)
HBM = pl.BlockSpec(memory_space=pltpu.HBM)
BF16 = jnp.bfloat16
COARSE_SWEEPS = 11
MICROSECONDS = dict(
    k_face_z=0.2,
    k_load=4.0,
    k_face_x=0.2,
    k_pack_own=1.0,
    k_face_y=0.6,
    k_assemble=1.0,
    k_pack=0.3,
    k_down0=2.0,
    k_coeff=2.0,
    k_down12=3.0,
    k_whole=2.0,
    k_up2=0.5,
    k_up1=1.5,
    k_up0=2.5,
)
A0, B0, U0 = 12, 8, 3
A1, U1 = 4, 8


def run(body, args, outs, scratch=(), out_spec=VM, sems=()):
    words = sum(math.prod(s) for s in (*outs, *scratch)) + sum(a.size for a in args)
    return pl.pallas_call(
        body,
        out_shape=[jax.ShapeDtypeStruct(o, F32) for o in outs],
        in_specs=[VM] * len(args),
        out_specs=[out_spec] * len(outs),
        scratch_shapes=[pltpu.VMEM(s, F32) for s in scratch]
        + [pltpu.SemaphoreType.DMA(n) for n in sems],
        compiler_params=pltpu.CompilerParams(vmem_limit_bytes=6 * words + (6 << 20)),
        cost_estimate=pl.CostEstimate(
            flops=0, transcendentals=0, bytes_accessed=int(3.5e6 * MICROSECONDS[body.__name__])
        ),
    )(*args)


def weights(level):
    wh = 0.25**level
    return wh, 2.0 * (0.25 * wh + 2.0 * wh)


def iota(shape, dim):
    return lax.broadcasted_iota(jnp.int32, shape, dim)


def lanes(v, shift):
    return pltpu.roll(v, shift % v.shape[-1], v.ndim - 1)


def rows(v, shift):
    return pltpu.roll(v, shift % v.shape[-2], v.ndim - 2)


def beside(v):
    return (rows(v, 1) + rows(v, -1)) + (lanes(v, 1) + lanes(v, -1))


def around(above, v, below):
    return 0.25 * (above + below) + beside(v)


def factors(s, k, level):
    wh, full = weights(level)
    diagonal = k + full * (s * s)
    sw = s * (0.8 / jnp.where(diagonal > 0.0, diagonal, 1.0))
    return sw, (wh * s) * sw


def unscale(v, s):
    inside = s > 0.0
    return jnp.where(inside, v / jnp.where(inside, s, 1.0), 0.0)


def dot(a, b):
    b = b.astype(BF16)
    high = a.astype(BF16)
    rest = a - high.astype(F32)
    middle = rest.astype(BF16)
    low = (rest - middle.astype(F32)).astype(BF16)
    terms = [jnp.dot(t, b, preferred_element_type=F32) for t in (high, middle, low)]
    return terms[0] + (terms[1] + terms[2])


def dot3(a, b):
    n, r, c = a.shape
    return dot(a.reshape(n * r, c), b).reshape(n, r, b.shape[1])


def blocks(first, count, size, body, unroll=1):
    def one(b, _):
        z = first + size * b
        body(z, pl.ds(z, size))
        return 0

    lax.fori_loop(0, count // size, one, 0, unroll=unroll)


def pair_sum(v):
    v = v.reshape(v.shape[0] // 2, 2, *v.shape[1:])
    return v[:, 0] + v[:, 1]


def select_matrix(shape, source_of, scale=1.0):
    i, o = iota(shape, 0), iota(shape, 1)
    return jnp.where(source_of(i, o), scale, 0.0).astype(F32)


def k_face_z(g, c, s, zmsg):
    upper = lax.axis_index("gz") == 0
    zmsg[0:3] = g[...]
    zmsg[3:5] = jnp.where(upper, c[1:], c[:2])
    zmsg[5:7] = jnp.where(upper, s[1:], s[:2])


def k_load(f, s, k, g, c, sk1, ps, pk):
    def one(z, at):
        sv, kv = s[at], k[at]
        sw, cv = factors(sv, kv, 0)
        g[at] = sw * f[at]
        c[at] = cv
        ps[pl.ds(z // 2, 2)] = pair_sum(sv)
        pk[pl.ds(z // 2, 2)] = pair_sum(kv)

    blocks(0, 32, 4, one, 2)
    a = ps[:, pl.ds(0, 16, 2), :] + ps[:, pl.ds(1, 16, 2), :]
    b = pk[:, pl.ds(0, 16, 2), :] + pk[:, pl.ds(1, 16, 2), :]
    left = select_matrix((128, 128), lambda i, o: i // 2 == o, 0.125)
    right = select_matrix((128, 128), lambda i, o: i // 2 == o - 64, 0.125)
    sk1[...] = dot3(a, left) + dot3(b, right)


def halo_rows(zr, iz, field, z):
    first, depth = ((0, 3), (3, 2), (5, 2))[field]
    d = z - 35 if z > 34 else 2 - z
    if d >= depth:
        return jnp.zeros(zr.shape[1:], F32)
    row = first + (d if z > 34 else depth - 1 - d)
    return jnp.where(iz == (0 if z > 34 else 1), zr[row], 0.0)


def k_face_x(g, c, s, zr, to_right, to_left):
    iz = lax.axis_index("gz")
    sub = iota((8, 128), 0)

    def put(z, gz, cz, sz):
        a, b, d = gz[24:32], cz[24:32], sz[24:32]
        to_right[z] = jnp.where(sub >= 5, a, jnp.where(sub >= 3, rows(b, -3), rows(d, -5)))
        a, b, d = gz[0:8], cz[0:8], sz[0:8]
        to_left[z] = jnp.where(sub < 3, a, jnp.where(sub < 5, rows(b, 3), rows(d, 5)))

    def one(z, _):
        put(z + 3, g[z], c[z], s[z])
        return 0

    lax.fori_loop(0, 32, one, 0, unroll=4)
    for z in (0, 1, 2, 35, 36, 37):
        put(z, *[halo_rows(zr, iz, n, z) for n in range(3)])


def k_pack_own(g, c, s, zr, *own):
    iz = lax.axis_index("gz")
    slot = iota((32, 128), 1)
    for n, (ref, out) in enumerate(zip((g, c, s), own)):
        for group in range(3):
            total = jnp.zeros((32, 128), F32)
            for j in range(16 if group < 2 else 6):
                z = 16 * group + j
                here = ref[z - 3] if 3 <= z < 35 else halo_rows(zr, iz, n, z)
                total = jnp.where(slot >= 8 * j, lanes(here, 8 * j + 3), total)
            out[group] = total


def side_rows(from_left, from_right, ix, z):
    sub = iota((8, 128), 0)
    lf = jnp.where(ix > 0, from_left[z], 0.0)
    rt = jnp.where(ix < 7, from_right[z], 0.0)
    return (
        jnp.where(sub >= 4, lf, rt),
        jnp.where(sub >= 4, rows(lf, 3), rows(rt, -3)),
        jnp.where(sub >= 4, rows(lf, 5), rows(rt, -5)),
    )


def k_face_y(og, oc, os, from_left, from_right, ag, ac, a_s, to_right, to_left):
    ix = lax.axis_index("gx")
    slot = iota((8, 128), 1)
    lane = iota((40, 128), 1) % 8
    for group in range(3):
        side = [jnp.zeros((8, 128), F32)] * 3
        mid = [ref[group] for ref in (og, oc, os)]
        for j in range(16 if group < 2 else 6):
            here = side_rows(from_left, from_right, ix, 16 * group + j)
            for n in range(3):
                side[n] = jnp.where(slot >= 8 * j, lanes(here[n], 8 * j + 3), side[n])
        g, c, s = [jnp.concatenate(parts, axis=0) for parts in zip(mid, side)]
        ag[group] = g
        ac[group] = c
        a_s[group] = s
        to_right[group] = jnp.where(
            lane < 3, g, jnp.where(lane < 5, lanes(c, 2), lanes(s, 4))
        )
        to_left[group] = jnp.where(
            lane >= 6, lanes(c, 3), jnp.where(lane >= 3, g, lanes(s, -2))
        )


def k_assemble(g, c, s, zr, from_left, from_right, gm, cm, sm):
    ix, iz = lax.axis_index("gx"), lax.axis_index("gz")

    def put(z, values):
        for ref, mid, side in zip(
            (gm, cm, sm), values, side_rows(from_left, from_right, ix, z)
        ):
            ref[z] = jnp.concatenate([mid, side], axis=0)

    def one(z, _):
        put(z + 3, (g[z], c[z], s[z]))
        return 0

    lax.fori_loop(0, 32, one, 0, unroll=4)
    for z in (0, 1, 2, 35, 36, 37):
        put(z, [halo_rows(zr, iz, n, z) for n in range(3)])


def near_edges(v):
    lane = iota(v.shape, 2)
    zero = jnp.zeros((1,) + v.shape[1:], F32)
    up, down = lanes(v, 8), lanes(v, -8)
    above = jnp.where(lane < 8, jnp.concatenate([zero, up[:-1]], axis=0), up)
    below = jnp.where(lane >= 120, jnp.concatenate([down[1:], zero], axis=0), down)
    return around(above, v, below)


def joint(v):
    lane = iota((3,) + v.shape[1:], 2)
    return jnp.where(lane % 8 == 4, lanes(v[3:], 2), v[:3])


def near_main(ref, edge, z, n, product=False):
    v = ref[pl.ds(z, n)]
    lane = iota(v.shape, 2)
    e = jnp.stack(
        [
            pltpu.roll(edge[(z + i) // 16], (124 - 8 * ((z + i) % 16)) % 128, 1)
            for i in range(n)
        ]
    )
    if product:
        across = dot3(v, select_matrix((128, 128), lambda i, o: (i == o + 1) | (i == o - 1)))
        across = jnp.where((lane == 0) | (lane == 127), e + across, across)
    else:
        across = jnp.where(lane == 0, e, lanes(v, 1)) + jnp.where(lane == 127, e, lanes(v, -1))
    above, below = ref[pl.ds(z - 1, n)], ref[pl.ds(z + 1, n)]
    return 0.25 * (above + below) + ((rows(v, 1) + rows(v, -1)) + across)


def near(ref, z, n):
    return around(ref[pl.ds(z - 1, n)], ref[pl.ds(z, n)], ref[pl.ds(z + 1, n)])


def k_down0(
    f, gm, cm, sm, og, oc, os, from_left, from_right, gw, cw, sw, q, qw, f1, e, eg, eq
):
    iy = lax.axis_index("gy")
    own = iota((3, 40, 128), 2) % 8 < 3
    lf = jnp.where(iy > 0, from_left[...], 0.0)
    rt = jnp.where(iy < 7, from_right[...], 0.0)

    def windows(ref, right, left):
        mid = ref[...]
        return jnp.concatenate(
            [jnp.where(own, mid, right), jnp.where(own, left, mid)], axis=0
        )

    g = windows(og, rt, lf)
    c = windows(oc, lanes(rt, -3), lanes(lf, -2))
    gw[...] = g
    cw[...] = c
    sw[...] = windows(os, lanes(rt, 2), lanes(lf, -4))
    w = 0.4 * g + c * near_edges(g)
    qw[...] = w
    eg[...] = joint(g)
    eq[...] = joint(w)
    q[0] = jnp.zeros((40, 128), F32)
    q[37] = jnp.zeros((40, 128), F32)

    def relax(z, at):
        q[at] = 0.4 * gm[at] + cm[at] * near_main(gm, eg, z, A0, True)

    blocks(1, 36, A0, relax, U0)

    def residual(z, at):
        v = 0.04 * f[pl.ds(z - 3, B0)] + sm[at, :32, :] * near_main(q, eq, z, B0, True)[:, :32]
        e[pl.ds((z - 3) // 2, B0 // 2)] = pair_sum(v)

    blocks(3, 32, B0, residual, U0)
    a = e[:, pl.ds(0, 16, 2), :] + e[:, pl.ds(1, 16, 2), :]
    lo = select_matrix((128, 128), lambda i, o: i // 2 == o, 0.125)
    hi = select_matrix((128, 128), lambda i, o: i // 2 == o - 64, 0.125)
    f1[...] = dot3(a[:8], lo) + dot3(a[8:], hi)


SLOTS = 5


def k_pack(own, full, to_right, to_left):
    iz = lax.axis_index("gz")
    lane = iota((16, 128), 1) % 64
    n = own.shape[0]
    for group in range(to_right.shape[0]):
        count = min(SLOTS, n - SLOTS * group)
        a, b, kept = None, None, []
        for j in range(count):
            z = SLOTS * group + j
            own_half = iz == (0 if z < n // 2 else 1)
            v = own[z % (n // 2) + jnp.where(own_half, 0, n // 2)]
            kept.append(v)
            last, first = lanes(v, 12 * j - 52), lanes(v, 12 * j) if j else v
            a = last if a is None else jnp.where(lane >= 12 * j, last, a)
            b = first if b is None else jnp.where(lane >= 12 * j, first, b)
        full[SLOTS * group : SLOTS * group + count] = jnp.stack(kept)
        to_right[group] = a
        to_left[group] = b


def joined(own, xl, xr, at, ix):
    lf = jnp.where(ix > 0, xl[at], 0.0)
    rt = jnp.where(ix < 7, xr[at], 0.0)
    sub = iota((rt.shape[0], 8, 128), 1)
    edge = jnp.where(sub < 4, rt[:, 8:16], lf[:, 0:8])
    return jnp.concatenate([own[at], rt[:, 0:8], edge, lf[:, 8:16]], axis=1)


def opened(own, xl, xr, z, n, ix, iy):
    groups = -(-n // SLOTS)
    mid = joined(own, xl, xr, pl.ds(z, 4), ix)
    need = range(z // SLOTS, (z + 3) // SLOTS + 1)
    lf = [joined(own, xl, xr, pl.ds(n + i, 1), ix)[0] for i in need]
    rt = [joined(own, xl, xr, pl.ds(n + groups + i, 1), ix)[0] for i in need]
    lf = [jnp.where(iy > 0, v, 0.0) for v in lf]
    rt = [jnp.where(iy < 7, v, 0.0) for v in rt]
    at = [((z + i) // SLOTS - need[0], (z + i) % SLOTS) for i in range(4)]
    lf = jnp.stack([lanes(lf[i], 116 - 12 * j) for i, j in at])
    rt = jnp.stack([lanes(rt[i], 64 - 12 * j) for i, j in at])
    lane = iota(mid.shape, 2)
    first = jnp.where(lane < 64, mid, jnp.where(lane < 96, rt, lf))
    second = jnp.where(lane >= 64, mid, jnp.where(lane < 32, rt, lf))
    return first, lanes(second, 64)


def halve_x(ref, n, x2):
    x2[:, 14:18, :] = jnp.zeros((n, 4, 128), F32)
    x2[:, 0:14, :] = ref[:, pl.ds(0, 14, 2), :] + ref[:, pl.ds(1, 14, 2), :]
    x2[:, 18:24, :] = ref[:, pl.ds(28, 6, 2), :] + ref[:, pl.ds(29, 6, 2), :]
    return x2[...]


def down_matrix():
    return select_matrix(
        (128, 128),
        lambda i, o: ((i // 2 == o) & (o < 38)) | ((i // 2 == o - 64) & (o >= 122)),
        0.125,
    )


def level3_rows(v, e2, rows2):
    half = select_matrix((128, 128), lambda i, o: (i // 2 == o) & (o < 16), 0.125)
    e2[...] = pair_sum(v)[:, :8, :]
    for j in range(8):
        rows2[4 * j : 4 * j + 4] = e2[j, pl.ds(0, 4, 2), :] + e2[j, pl.ds(1, 4, 2), :]
    pieces = dot(rows2[...], half)
    total = pieces[0:4]
    for j in range(1, 8):
        total = total + lanes(pieces[4 * j : 4 * j + 4], 16 * j)
    return total


def k_coeff(own, xl, xr, s1, c1, w1, s2, c2, w2, sk3, ps, pk, x2, e2, r2):
    ix, iy = lax.axis_index("gx"), lax.axis_index("gy")

    for z in range(0, 32, 4):
        at = pl.ds(z, 4)
        s, k = opened(own, xl, xr, z, 32, ix, iy)
        s1[at] = s
        w1[at], c1[at] = factors(s, k, 1)
        ps[pl.ds(z // 2, 2)] = pair_sum(s)
        pk[pl.ds(z // 2, 2)] = pair_sum(k)
    down = down_matrix()
    s = dot3(halve_x(ps, 16, x2), down)
    k = dot3(halve_x(pk, 16, x2), down)
    s2[...] = s
    w2[...], c2[...] = factors(s, k, 2)
    sk3[...] = jnp.concatenate([level3_rows(s, e2, r2), level3_rows(k, e2, r2)], axis=0)


def k_down12(own, xl, xr, s1, c1, w1, s2, c2, w2, sk3, g, q, g2, q2, chunk, f, e, x2, e2, r2):
    ix, iy = lax.axis_index("gx"), lax.axis_index("gy")
    for ref in (g, q):
        ref[0] = jnp.zeros((40, 128), F32)
        ref[33] = jnp.zeros((40, 128), F32)

    for z in range(0, 16, 4):
        for i, v in enumerate(opened(own, xl, xr, z, 16, ix, iy)):
            first = z + 8 * (z // 8) + 8 * i
            f[pl.ds(first, 4)] = v
            g[pl.ds(first + 1, 4)] = w1[pl.ds(first, 4)] * v

    def relax(z, at):
        q[at] = 0.4 * g[at] + c1[pl.ds(z - 1, A1)] * near(g, z, A1)

    blocks(1, 32, A1, relax, U1)
    wh, _ = weights(1)

    def residual(z, at):
        own = pl.ds(z - 1, A1)
        v = 0.04 * f[own] + (wh * s1[own]) * near(q, z, A1)
        e[pl.ds((z - 1) // 2, A1 // 2)] = pair_sum(v)

    blocks(1, 32, A1, residual, U1)
    fv = dot3(halve_x(e, 16, x2), down_matrix())
    gv = w2[...] * fv
    zero = jnp.zeros((1, 24, 128), F32)

    def spread(v):
        w = jnp.concatenate([zero, v, zero], axis=0)
        return around(w[:16], v, w[2:])

    qv = 0.4 * gv + c2[...] * spread(gv)
    wh, _ = weights(2)
    ev = 0.04 * fv + (wh * s2[...]) * spread(qv)
    g2[...] = gv
    q2[...] = qv
    parts = [level3_rows(ev, e2, r2), sk3[:4], sk3[4:]]
    parts = [pltpu.roll(part, 16 * iy, 1) for part in parts]

    def copy(n, _):
        for i in range(3):
            chunk[3 * n + i] = parts[i]
        return 0

    lax.fori_loop(0, 64, copy, 0, unroll=8)


def spread_in(shape, last):
    n, r, _ = shape
    row, col = iota(shape, 1), iota(shape, 2)
    zero = jnp.zeros((1,) + shape[1:], F32)

    def apply(v):
        w = jnp.concatenate([zero, v, zero], axis=0)
        x = jnp.where(row > 0, rows(v, 1), 0.0) + jnp.where(row < r - 1, rows(v, -1), 0.0)
        y = jnp.where(col > 0, lanes(v, 1), 0.0) + jnp.where(col < last, lanes(v, -1), 0.0)
        return 0.25 * (w[:n] + w[2:]) + x + y

    return apply


def k_whole(gathered, u, t3, x4, p3):
    ix, iy = lax.axis_index("gx"), lax.axis_index("gy")
    lane = iota((4, 128), 1) // 16
    for j in range(8):
        for n in range(3):
            for x in range(8):
                v = gathered[x * 24 + n]
                for y in range(1, 8):
                    v = jnp.where(lane == (j + y) % 8, gathered[x * 24 + 3 * y + n], v)
                t3[n, j, 4 * x : 4 * x + 4, :] = lanes(v, -16 * j) if j else v
    f3, s3, k3 = t3[0], t3[1], t3[2]
    near3 = spread_in((8, 32, 128), 127)
    w3, c3 = factors(s3, k3, 3)
    g3 = w3 * f3
    q3 = 0.4 * g3 + c3 * near3(g3)
    e3 = 0.04 * f3 + (weights(3)[0] * s3) * near3(q3)
    half = select_matrix((128, 128), lambda i, o: i // 2 == o, 0.125)
    fields = []
    for v in (e3, s3, k3):
        w = v.reshape(4, 2, 32, 128)
        x4[...] = w[:, 0] + w[:, 1]
        fields.append(dot3(x4[:, pl.ds(0, 16, 2), :] + x4[:, pl.ds(1, 16, 2), :], half))
    f4, s4, k4 = fields
    zero4, row4 = jnp.zeros((1, 16, 128), F32), iota((4, 16, 128), 1)

    def near4(v, before, after):
        w = jnp.concatenate([zero4, v, zero4], axis=0)
        x = jnp.where(row4 > 0, rows(v, 1), 0.0) + jnp.where(row4 < 15, rows(v, -1), 0.0)
        return (0.25 * (w[:4] + w[2:]) + x) + (before + after)

    w4, c4 = factors(s4, k4, 4)
    g4 = w4 * f4
    v4 = (0.2 * g4 + g4) + c4 * near4(g4, lanes(g4, 1), lanes(g4, -1))
    g4m, g4p, c4m, c4p = lanes(g4, 1), lanes(g4, -1), lanes(c4, 1), lanes(c4, -1)
    for _ in range(COARSE_SWEEPS // 2):
        vm, vp = lanes(v4, 1), lanes(v4, -1)
        am = (0.2 * vm + g4m) + c4m * near4(vm, lanes(v4, 2), v4)
        ap = (0.2 * vp + g4p) + c4p * near4(vp, v4, lanes(v4, -2))
        a = (0.2 * v4 + g4) + c4 * near4(v4, vm, vp)
        v4 = (0.2 * a + g4) + c4 * near4(a, am, ap)
    u4 = dot3(unscale(v4, s4), select_matrix((128, 128), lambda i, o: i == o // 2))
    p3[:, pl.ds(0, 16, 2), :] = u4
    p3[:, pl.ds(1, 16, 2), :] = u4
    w = p3[...]
    w = jnp.broadcast_to(w[:, None], (4, 2, 32, 128)).reshape(8, 32, 128)
    v3 = (q3 + 0.8 * g3) + s3 * w
    for _ in range(2):
        v3 = (0.2 * v3 + g3) + c3 * near3(v3)
    pick = select_matrix(
        (128, 128),
        lambda i, o: i == (jnp.where(o < 64, o // 2, 127 - (127 - o) // 2) + 16 * iy) % 128,
    )
    u[...] = pltpu.roll(dot3(v3 / s3, pick), (32 - 4 * ix) % 32, 1)


def k_up2(u3, g2, c2, s2, q2, u, p2):
    p2[:, 14:18, :] = jnp.zeros((8, 4, 128), F32)
    for n in range(2):
        p2[:, pl.ds(n, 7, 2), :] = u3[:, 0:7, :]
        p2[:, pl.ds(18 + n, 3, 2), :] = u3[:, 29:32, :]
    w = p2[...]
    w = jnp.broadcast_to(w[:, None], (8, 2, 24, 128)).reshape(16, 24, 128)
    gv, cv, sv = g2[...], c2[...], s2[...]
    zero = jnp.zeros((1, 24, 128), F32)
    v = (q2[...] + 0.8 * gv) + sv * w
    for _ in range(2):
        w = jnp.concatenate([zero, v, zero], axis=0)
        v = (0.2 * v + gv) + cv * around(w[:16], v, w[2:])
    pick = select_matrix(
        (128, 128),
        lambda i, o: i == jnp.where(o < 96, o // 2, 127 - (127 - o) // 2),
    )
    u[...] = dot3(unscale(v, sv), pick)


def k_up1(u2, g1, c1, s1, q1, u, p1, va, vb):
    for n in range(2):
        p1[:, pl.ds(n, 14, 2), :] = u2[:, 0:14, :]
        p1[:, pl.ds(28 + n, 6, 2), :] = u2[:, 18:24, :]
    for ref in (va, vb, u):
        ref[0] = jnp.zeros((40, 128), F32)
        ref[33] = jnp.zeros((40, 128), F32)

    def start(z, at):
        t = p1[pl.ds((z - 1) // 2, A1 // 2)]
        t = jnp.broadcast_to(t[:, None], (A1 // 2, 2, 40, 128)).reshape(A1, 40, 128)
        va[at] = (q1[at] + 0.8 * g1[at]) + s1[pl.ds(z - 1, A1)] * t

    blocks(1, 32, A1, start, U1)

    def sweep(z, at):
        vb[at] = (0.2 * va[at] + g1[at]) + c1[pl.ds(z - 1, A1)] * near(va, z, A1)

    blocks(1, 32, A1, sweep, U1)

    def last(z, at):
        own = pl.ds(z - 1, A1)
        v = (0.2 * vb[at] + g1[at]) + c1[own] * near(vb, z, A1)
        u[at] = unscale(v, s1[own])

    blocks(1, 32, A1, last, U1)


def k_up0(
    u1, gm, cm, sm, q, gw, cw, sw, qw, out, pm, pw, pv, wa, wb, ea, eb, done, sem
):
    iz = lax.axis_index("gz")

    def source(i, o):
        y = jnp.where(o % 16 < 8, 125 + o % 16, o % 16 - 11)
        return i == jnp.where(o < 128, o // 2, ((y + 256) // 2) % 128)

    u = u1[pl.ds(16 * iz, 18)]
    sub = iota((18, 8, 128), 1)
    u = jnp.concatenate([u[:, :16], jnp.where(sub < 4, u[:, 16:24], u[:, 32:40])], axis=1)
    u = dot3(u, select_matrix((128, 256), source))
    for h, ref in enumerate((pm, pw)):
        w = u[:, :, 128 * h : 128 * h + 128]
        for n in range(2):
            ref[:, pl.ds(n, 18, 2), :] = w[:, 0:18]
            ref[:, pl.ds(36 + n, 2, 2), :] = w[:, 22:24]
    pv[...] = lanes(pw[...], 8)
    slot = iota((40, 128), 1) // 8
    parts = []
    for side in range(2):
        for group in range(3):
            total = None
            for j in range(16):
                ref = pw if j % 2 == side else pv
                part = ref[min(max((16 * group + j - 1) // 2, 0), 17)]
                total = part if total is None else jnp.where(slot >= j, part, total)
            parts.append(total[None])
    g, c = gw[...], cw[...]
    v = (qw[...] + 0.8 * g) + sw[...] * jnp.concatenate(parts, axis=0)
    ea[...] = joint(v)
    eb[...] = joint((0.2 * v + g) + c * near_edges(v))

    def start(z, at):
        t = jnp.stack([pm[(z + i - 1) // 2] for i in range(A0)])
        wa[at] = (q[at] + 0.8 * gm[at]) + sm[at] * t

    blocks(1, 36, A0, start, U0)
    wa[0] = jnp.zeros((40, 128), F32)
    wa[37] = jnp.zeros((40, 128), F32)

    def sweep(z, at):
        wb[at] = (0.2 * wa[at] + gm[at]) + cm[at] * near_main(wa, ea, z, A0, True)

    blocks(1, 36, A0, sweep, U0)

    copies = []
    for b in range(32 // B0):
        z = 3 + b * B0
        at = pl.ds(z, B0)
        n = near_main(wb, eb, z, B0)[:, :32]
        v = (0.2 * wb[at, :32, :] + gm[at, :32, :]) + cm[at, :32, :] * n
        part = pl.ds(z - 3, B0)
        done[part] = v / sm[at, :32, :]
        copies.append(pltpu.make_async_copy(done.at[part], out.at[part], sem.at[b]))
        copies[-1].start()
    for copy in copies:
        copy.wait()


def ring(v, axis, step):
    n = lax.axis_size(axis)
    return lax.ppermute(v, axis, [(i, (i + step) % n) for i in range(n)])


def pair(to_right, to_left, axis):
    return ring(to_right, axis, 1), ring(to_left, axis, -1)


def pack_level1(own):
    n = own.shape[0]
    full, *msg = run(k_pack, (own,), [(n, 16, 128)] + [(-(-n // SLOTS), 16, 128)] * 2)
    return jnp.concatenate([full, *pair(*msg, "gy")], axis=0)


def after(values, *others):
    return lax.optimization_barrier((values, others))[0]


def shards(f, s, k):
    first = jnp.where(lax.axis_index("gz") == 0, 29, 0)
    fz, sz, kz = [lax.dynamic_slice_in_dim(v, first, 3, 0) for v in (f, s, k)]
    sw, c = factors(sz, kz, 0)
    near = (sw * fz, c, jnp.where(kz > 0.0, sz, 0.0))
    zr = ring(run(k_face_z, near, [(7, 32, 128)])[0], "gz", 1)
    g, c, sk1 = run(
        k_load, (f, s, k), [(32, 32, 128)] * 2 + [(16, 16, 128)], [(16, 32, 128)] * 2
    )
    sk1 = after(sk1, zr)
    sk_z = ring(sk1, "gz", 1)
    xs = pair(*run(k_face_x, (g, c, s, zr), [(38, 8, 128)] * 2), "gx")
    small, both = [(3, 40, 128)], [(6, 40, 128)]
    edges = run(k_pack_own, (g, c, s, zr), [(3, 32, 128)] * 3)
    *edges, to_right, to_left = run(k_face_y, (*edges, *xs), small * 5)
    ys = pair(to_right, to_left, "gy")
    gm, cm, sm = run(k_assemble, (g, c, s, zr, *xs), [(38, 40, 128)] * 3)
    sk1, sk_z = after((sk1, sk_z), gm)
    sk_y = pack_level1(jnp.concatenate([sk1, sk_z], axis=0))
    gw, cw, sw, q0, qw, f1 = run(
        k_down0,
        (f, gm, cm, sm, *edges, *ys),
        both * 3 + [(38, 40, 128)] + both + [(8, 16, 128)],
        [(16, 32, 128)] + small * 2,
    )
    sk = after(sk_y, f1)
    f1 = jnp.concatenate([f1, ring(f1, "gz", 1)], axis=0)
    s1, c1, w1, s2, c2, w2, sk3 = run(
        k_coeff,
        (sk, *pair(sk, sk, "gx")),
        [(32, 40, 128)] * 3 + [(16, 24, 128)] * 3 + [(8, 128)],
        [(16, 40, 128)] * 2 + [(16, 24, 128), (8, 8, 128), (32, 128)],
    )
    f1 = pack_level1(f1)
    g1, q1, g2, q2, chunk = run(
        k_down12,
        (f1, *pair(f1, f1, "gx"), s1, c1, w1, s2, c2, w2, sk3),
        [(34, 40, 128)] * 2 + [(16, 24, 128)] * 2 + [(192, 4, 128)],
        [(32, 40, 128), (16, 40, 128), (16, 24, 128), (8, 8, 128), (32, 128)],
    )
    gathered = lax.all_to_all(chunk, ("gx", "gy"), 0, 0, tiled=True)
    (u3,) = run(
        k_whole, (gathered,), [(8, 32, 128)], [(3, 8, 32, 128), (4, 32, 128), (4, 32, 128)]
    )
    (u2,) = run(k_up2, (u3, g2, c2, s2, q2), [(16, 24, 128)], [(8, 24, 128)])
    (u1,) = run(
        k_up1, (u2, g1, c1, s1, q1), [(34, 40, 128)], [(16, 40, 128)] + [(34, 40, 128)] * 2
    )
    (out,) = run(
        k_up0,
        (u1, gm, cm, sm, q0, gw, cw, sw, qw),
        [(32, 32, 128)],
        [(18, 40, 128)] * 3 + [(38, 40, 128)] * 2 + small * 2 + [(32, 32, 128)],
        HBM,
        [(32 // B0,)],
    )
    return out


def solution(mesh):
    return jax.shard_map(
        shards,
        mesh=mesh,
        in_specs=(P("gz", "gx", "gy"),) * 3,
        out_specs=P("gz", "gx", "gy"),
        check_vma=False,
    )
```

```python
import math

import jax
import jax.numpy as jnp
from jax import lax
from jax.experimental import pallas as pl
from jax.experimental.pallas import tpu as pltpu
from jax.sharding import PartitionSpec as P

F32 = jnp.float32
VM = pl.BlockSpec(memory_space=pltpu.VMEM)
HBM = pl.BlockSpec(memory_space=pltpu.HBM)
BF16 = jnp.bfloat16
COARSE_SWEEPS = 11
MICROSECONDS = dict(
    k_face_z=0.2,
    k_load=4.0,
    k_face_x=0.2,
    k_pack_own=1.0,
    k_face_y=0.6,
    k_assemble=1.0,
    k_pack=0.3,
    k_down0=2.0,
    k_coeff=2.0,
    k_down12=3.0,
    k_whole=2.0,
    k_up2=0.5,
    k_up1=1.5,
    k_up0=2.5,
)
A0, B0, U0 = 12, 8, 3
A1, U1 = 4, 8


def run(body, args, outs, scratch=(), out_spec=VM, sems=()):
    words = sum(math.prod(s) for s in (*outs, *scratch)) + sum(a.size for a in args)
    return pl.pallas_call(
        body,
        out_shape=[jax.ShapeDtypeStruct(o, F32) for o in outs],
        in_specs=[VM] * len(args),
        out_specs=[out_spec] * len(outs),
        scratch_shapes=[pltpu.VMEM(s, F32) for s in scratch]
        + [pltpu.SemaphoreType.DMA(n) for n in sems],
        compiler_params=pltpu.CompilerParams(vmem_limit_bytes=6 * words + (6 << 20)),
        cost_estimate=pl.CostEstimate(
            flops=0, transcendentals=0, bytes_accessed=int(3.5e6 * MICROSECONDS[body.__name__])
        ),
    )(*args)


def weights(level):
    wh = 0.25**level
    return wh, 2.0 * (0.25 * wh + 2.0 * wh)


def iota(shape, dim):
    return lax.broadcasted_iota(jnp.int32, shape, dim)


def lanes(v, shift):
    return pltpu.roll(v, shift % v.shape[-1], v.ndim - 1)


def rows(v, shift):
    return pltpu.roll(v, shift % v.shape[-2], v.ndim - 2)


def beside(v):
    return (rows(v, 1) + rows(v, -1)) + (lanes(v, 1) + lanes(v, -1))


def around(above, v, below):
    return 0.25 * (above + below) + beside(v)


def factors(s, k, level):
    wh, full = weights(level)
    diagonal = k + full * (s * s)
    sw = s * (0.8 / jnp.where(diagonal > 0.0, diagonal, 1.0))
    return sw, (wh * s) * sw


def unscale(v, s):
    inside = s > 0.0
    return jnp.where(inside, v / jnp.where(inside, s, 1.0), 0.0)


def dot(a, b):
    b = b.astype(BF16)
    high = a.astype(BF16)
    rest = a - high.astype(F32)
    middle = rest.astype(BF16)
    low = (rest - middle.astype(F32)).astype(BF16)
    terms = [jnp.dot(t, b, preferred_element_type=F32) for t in (high, middle, low)]
    return terms[0] + (terms[1] + terms[2])


def dot3(a, b):
    n, r, c = a.shape
    return dot(a.reshape(n * r, c), b).reshape(n, r, b.shape[1])


def blocks(first, count, size, body, unroll=1):
    def one(b, _):
        z = first + size * b
        body(z, pl.ds(z, size))
        return 0

    lax.fori_loop(0, count // size, one, 0, unroll=unroll)


def pair_sum(v):
    v = v.reshape(v.shape[0] // 2, 2, *v.shape[1:])
    return v[:, 0] + v[:, 1]


def select_matrix(shape, source_of, scale=1.0):
    i, o = iota(shape, 0), iota(shape, 1)
    return jnp.where(source_of(i, o), scale, 0.0).astype(F32)


def k_face_z(g, c, s, zmsg):
    upper = lax.axis_index("gz") == 0
    zmsg[0:3] = g[...]
    zmsg[3:5] = jnp.where(upper, c[1:], c[:2])
    zmsg[5:7] = jnp.where(upper, s[1:], s[:2])


def k_load(f, s, k, g, c, sk1, ps, pk):
    def one(z, at):
        sv, kv = s[at], k[at]
        sw, cv = factors(sv, kv, 0)
        g[at] = sw * f[at]
        c[at] = cv
        ps[pl.ds(z // 2, 2)] = pair_sum(sv)
        pk[pl.ds(z // 2, 2)] = pair_sum(kv)

    blocks(0, 32, 4, one, 2)
    a = ps[:, pl.ds(0, 16, 2), :] + ps[:, pl.ds(1, 16, 2), :]
    b = pk[:, pl.ds(0, 16, 2), :] + pk[:, pl.ds(1, 16, 2), :]
    left = select_matrix((128, 128), lambda i, o: i // 2 == o, 0.125)
    right = select_matrix((128, 128), lambda i, o: i // 2 == o - 64, 0.125)
    sk1[...] = dot3(a, left) + dot3(b, right)


def halo_rows(zr, iz, field, z):
    first, depth = ((0, 3), (3, 2), (5, 2))[field]
    d = z - 35 if z > 34 else 2 - z
    if d >= depth:
        return jnp.zeros(zr.shape[1:], F32)
    row = first + (d if z > 34 else depth - 1 - d)
    return jnp.where(iz == (0 if z > 34 else 1), zr[row], 0.0)


def k_face_x(g, c, s, zr, to_right, to_left):
    iz = lax.axis_index("gz")
    sub = iota((8, 128), 0)

    def put(z, gz, cz, sz):
        a, b, d = gz[24:32], cz[24:32], sz[24:32]
        to_right[z] = jnp.where(sub >= 5, a, jnp.where(sub >= 3, rows(b, -3), rows(d, -5)))
        a, b, d = gz[0:8], cz[0:8], sz[0:8]
        to_left[z] = jnp.where(sub < 3, a, jnp.where(sub < 5, rows(b, 3), rows(d, 5)))

    def one(z, _):
        put(z + 3, g[z], c[z], s[z])
        return 0

    lax.fori_loop(0, 32, one, 0, unroll=4)
    for z in (0, 1, 2, 35, 36, 37):
        put(z, *[halo_rows(zr, iz, n, z) for n in range(3)])


def k_pack_own(g, c, s, zr, *own):
    iz = lax.axis_index("gz")
    slot = iota((32, 128), 1)
    for n, (ref, out) in enumerate(zip((g, c, s), own)):
        for group in range(3):
            total = jnp.zeros((32, 128), F32)
            for j in range(16 if group < 2 else 6):
                z = 16 * group + j
                here = ref[z - 3] if 3 <= z < 35 else halo_rows(zr, iz, n, z)
                total = jnp.where(slot >= 8 * j, lanes(here, 8 * j + 3), total)
            out[group] = total


def side_rows(from_left, from_right, ix, z):
    sub = iota((8, 128), 0)
    lf = jnp.where(ix > 0, from_left[z], 0.0)
    rt = jnp.where(ix < 7, from_right[z], 0.0)
    return (
        jnp.where(sub >= 4, lf, rt),
        jnp.where(sub >= 4, rows(lf, 3), rows(rt, -3)),
        jnp.where(sub >= 4, rows(lf, 5), rows(rt, -5)),
    )


def k_face_y(og, oc, os, from_left, from_right, ag, ac, a_s, to_right, to_left):
    ix = lax.axis_index("gx")
    slot = iota((8, 128), 1)
    lane = iota((40, 128), 1) % 8
    for group in range(3):
        side = [jnp.zeros((8, 128), F32)] * 3
        mid = [ref[group] for ref in (og, oc, os)]
        for j in range(16 if group < 2 else 6):
            here = side_rows(from_left, from_right, ix, 16 * group + j)
            for n in range(3):
                side[n] = jnp.where(slot >= 8 * j, lanes(here[n], 8 * j + 3), side[n])
        g, c, s = [jnp.concatenate(parts, axis=0) for parts in zip(mid, side)]
        ag[group] = g
        ac[group] = c
        a_s[group] = s
        to_right[group] = jnp.where(
            lane < 3, g, jnp.where(lane < 5, lanes(c, 2), lanes(s, 4))
        )
        to_left[group] = jnp.where(
            lane >= 6, lanes(c, 3), jnp.where(lane >= 3, g, lanes(s, -2))
        )


def k_assemble(g, c, s, zr, from_left, from_right, gm, cm, sm):
    ix, iz = lax.axis_index("gx"), lax.axis_index("gz")

    def put(z, values):
        for ref, mid, side in zip(
            (gm, cm, sm), values, side_rows(from_left, from_right, ix, z)
        ):
            ref[z] = jnp.concatenate([mid, side], axis=0)

    def one(z, _):
        put(z + 3, (g[z], c[z], s[z]))
        return 0

    lax.fori_loop(0, 32, one, 0, unroll=4)
    for z in (0, 1, 2, 35, 36, 37):
        put(z, [halo_rows(zr, iz, n, z) for n in range(3)])


def near_edges(v):
    lane = iota(v.shape, 2)
    zero = jnp.zeros((1,) + v.shape[1:], F32)
    up, down = lanes(v, 8), lanes(v, -8)
    above = jnp.where(lane < 8, jnp.concatenate([zero, up[:-1]], axis=0), up)
    below = jnp.where(lane >= 120, jnp.concatenate([down[1:], zero], axis=0), down)
    return around(above, v, below)


def joint(v):
    lane = iota((3,) + v.shape[1:], 2)
    return jnp.where(lane % 8 == 4, lanes(v[3:], 2), v[:3])


def near_main(ref, edge, z, n, product=False):
    v = ref[pl.ds(z, n)]
    lane = iota(v.shape, 2)
    e = jnp.stack(
        [
            pltpu.roll(edge[(z + i) // 16], (124 - 8 * ((z + i) % 16)) % 128, 1)
            for i in range(n)
        ]
    )
    if product:
        across = dot3(v, select_matrix((128, 128), lambda i, o: (i == o + 1) | (i == o - 1)))
        across = jnp.where((lane == 0) | (lane == 127), e + across, across)
    else:
        across = jnp.where(lane == 0, e, lanes(v, 1)) + jnp.where(lane == 127, e, lanes(v, -1))
    above, below = ref[pl.ds(z - 1, n)], ref[pl.ds(z + 1, n)]
    return 0.25 * (above + below) + ((rows(v, 1) + rows(v, -1)) + across)


def near(ref, z, n):
    return around(ref[pl.ds(z - 1, n)], ref[pl.ds(z, n)], ref[pl.ds(z + 1, n)])


def k_down0(
    f, gm, cm, sm, og, oc, os, from_left, from_right, gw, cw, sw, q, qw, f1, e, eg, eq
):
    iy = lax.axis_index("gy")
    own = iota((3, 40, 128), 2) % 8 < 3
    lf = jnp.where(iy > 0, from_left[...], 0.0)
    rt = jnp.where(iy < 7, from_right[...], 0.0)

    def windows(ref, right, left):
        mid = ref[...]
        return jnp.concatenate(
            [jnp.where(own, mid, right), jnp.where(own, left, mid)], axis=0
        )

    g = windows(og, rt, lf)
    c = windows(oc, lanes(rt, -3), lanes(lf, -2))
    gw[...] = g
    cw[...] = c
    sw[...] = windows(os, lanes(rt, 2), lanes(lf, -4))
    w = 0.4 * g + c * near_edges(g)
    qw[...] = w
    eg[...] = joint(g)
    eq[...] = joint(w)
    q[0] = jnp.zeros((40, 128), F32)
    q[37] = jnp.zeros((40, 128), F32)

    def relax(z, at):
        q[at] = 0.4 * gm[at] + cm[at] * near_main(gm, eg, z, A0, True)

    blocks(1, 36, A0, relax, U0)

    def residual(z, at):
        v = 0.04 * f[pl.ds(z - 3, B0)] + sm[at, :32, :] * near_main(q, eq, z, B0, True)[:, :32]
        e[pl.ds((z - 3) // 2, B0 // 2)] = pair_sum(v)

    blocks(3, 32, B0, residual, U0)
    a = e[:, pl.ds(0, 16, 2), :] + e[:, pl.ds(1, 16, 2), :]
    lo = select_matrix((128, 128), lambda i, o: i // 2 == o, 0.125)
    hi = select_matrix((128, 128), lambda i, o: i // 2 == o - 64, 0.125)
    f1[...] = dot3(a[:8], lo) + dot3(a[8:], hi)


SLOTS = 5


def k_pack(own, full, to_right, to_left):
    iz = lax.axis_index("gz")
    lane = iota((16, 128), 1) % 64
    n = own.shape[0]
    for group in range(to_right.shape[0]):
        count = min(SLOTS, n - SLOTS * group)
        a, b, kept = None, None, []
        for j in range(count):
            z = SLOTS * group + j
            own_half = iz == (0 if z < n // 2 else 1)
            v = own[z % (n // 2) + jnp.where(own_half, 0, n // 2)]
            kept.append(v)
            last, first = lanes(v, 12 * j - 52), lanes(v, 12 * j) if j else v
            a = last if a is None else jnp.where(lane >= 12 * j, last, a)
            b = first if b is None else jnp.where(lane >= 12 * j, first, b)
        full[SLOTS * group : SLOTS * group + count] = jnp.stack(kept)
        to_right[group] = a
        to_left[group] = b


def joined(own, xl, xr, at, ix):
    lf = jnp.where(ix > 0, xl[at], 0.0)
    rt = jnp.where(ix < 7, xr[at], 0.0)
    sub = iota((rt.shape[0], 8, 128), 1)
    edge = jnp.where(sub < 4, rt[:, 8:16], lf[:, 0:8])
    return jnp.concatenate([own[at], rt[:, 0:8], edge, lf[:, 8:16]], axis=1)


def opened(own, xl, xr, z, n, ix, iy):
    groups = -(-n // SLOTS)
    mid = joined(own, xl, xr, pl.ds(z, 4), ix)
    need = range(z // SLOTS, (z + 3) // SLOTS + 1)
    lf = [joined(own, xl, xr, pl.ds(n + i, 1), ix)[0] for i in need]
    rt = [joined(own, xl, xr, pl.ds(n + groups + i, 1), ix)[0] for i in need]
    lf = [jnp.where(iy > 0, v, 0.0) for v in lf]
    rt = [jnp.where(iy < 7, v, 0.0) for v in rt]
    at = [((z + i) // SLOTS - need[0], (z + i) % SLOTS) for i in range(4)]
    lf = jnp.stack([lanes(lf[i], 116 - 12 * j) for i, j in at])
    rt = jnp.stack([lanes(rt[i], 64 - 12 * j) for i, j in at])
    lane = iota(mid.shape, 2)
    first = jnp.where(lane < 64, mid, jnp.where(lane < 96, rt, lf))
    second = jnp.where(lane >= 64, mid, jnp.where(lane < 32, rt, lf))
    return first, lanes(second, 64)


def halve_x(ref, n, x2):
    x2[:, 14:18, :] = jnp.zeros((n, 4, 128), F32)
    x2[:, 0:14, :] = ref[:, pl.ds(0, 14, 2), :] + ref[:, pl.ds(1, 14, 2), :]
    x2[:, 18:24, :] = ref[:, pl.ds(28, 6, 2), :] + ref[:, pl.ds(29, 6, 2), :]
    return x2[...]


def down_matrix():
    return select_matrix(
        (128, 128),
        lambda i, o: ((i // 2 == o) & (o < 38)) | ((i // 2 == o - 64) & (o >= 122)),
        0.125,
    )


def level3_rows(v, e2, rows2):
    half = select_matrix((128, 128), lambda i, o: (i // 2 == o) & (o < 16), 0.125)
    e2[...] = pair_sum(v)[:, :8, :]
    for j in range(8):
        rows2[4 * j : 4 * j + 4] = e2[j, pl.ds(0, 4, 2), :] + e2[j, pl.ds(1, 4, 2), :]
    pieces = dot(rows2[...], half)
    total = pieces[0:4]
    for j in range(1, 8):
        total = total + lanes(pieces[4 * j : 4 * j + 4], 16 * j)
    return total


def k_coeff(own, xl, xr, s1, c1, w1, s2, c2, w2, sk3, ps, pk, x2, e2, r2):
    ix, iy = lax.axis_index("gx"), lax.axis_index("gy")

    for z in range(0, 32, 4):
        at = pl.ds(z, 4)
        s, k = opened(own, xl, xr, z, 32, ix, iy)
        s1[at] = s
        w1[at], c1[at] = factors(s, k, 1)
        ps[pl.ds(z // 2, 2)] = pair_sum(s)
        pk[pl.ds(z // 2, 2)] = pair_sum(k)
    down = down_matrix()
    s = dot3(halve_x(ps, 16, x2), down)
    k = dot3(halve_x(pk, 16, x2), down)
    s2[...] = s
    w2[...], c2[...] = factors(s, k, 2)
    sk3[...] = jnp.concatenate([level3_rows(s, e2, r2), level3_rows(k, e2, r2)], axis=0)


def k_down12(own, xl, xr, s1, c1, w1, s2, c2, w2, sk3, g, q, g2, q2, chunk, f, e, x2, e2, r2):
    ix, iy = lax.axis_index("gx"), lax.axis_index("gy")
    for ref in (g, q):
        ref[0] = jnp.zeros((40, 128), F32)
        ref[33] = jnp.zeros((40, 128), F32)

    for z in range(0, 16, 4):
        for i, v in enumerate(opened(own, xl, xr, z, 16, ix, iy)):
            first = z + 8 * (z // 8) + 8 * i
            f[pl.ds(first, 4)] = v
            g[pl.ds(first + 1, 4)] = w1[pl.ds(first, 4)] * v

    def relax(z, at):
        q[at] = 0.4 * g[at] + c1[pl.ds(z - 1, A1)] * near(g, z, A1)

    blocks(1, 32, A1, relax, U1)
    wh, _ = weights(1)

    def residual(z, at):
        own = pl.ds(z - 1, A1)
        v = 0.04 * f[own] + (wh * s1[own]) * near(q, z, A1)
        e[pl.ds((z - 1) // 2, A1 // 2)] = pair_sum(v)

    blocks(1, 32, A1, residual, U1)
    fv = dot3(halve_x(e, 16, x2), down_matrix())
    gv = w2[...] * fv
    zero = jnp.zeros((1, 24, 128), F32)

    def spread(v):
        w = jnp.concatenate([zero, v, zero], axis=0)
        return around(w[:16], v, w[2:])

    qv = 0.4 * gv + c2[...] * spread(gv)
    wh, _ = weights(2)
    ev = 0.04 * fv + (wh * s2[...]) * spread(qv)
    g2[...] = gv
    q2[...] = qv
    parts = [level3_rows(ev, e2, r2), sk3[:4], sk3[4:]]
    parts = [pltpu.roll(part, 16 * iy, 1) for part in parts]

    tiles = [jnp.concatenate([parts[i], parts[(i + 1) % 3]], axis=0) for i in (0, 2, 1)]

    def copy(n, _):
        for i in range(3):
            chunk[3 * n + i] = tiles[i]
        return 0

    lax.fori_loop(0, 32, copy, 0, unroll=8)


def spread_in(shape, last):
    n, r, _ = shape
    row, col = iota(shape, 1), iota(shape, 2)
    zero = jnp.zeros((1,) + shape[1:], F32)

    def apply(v):
        w = jnp.concatenate([zero, v, zero], axis=0)
        x = jnp.where(row > 0, rows(v, 1), 0.0) + jnp.where(row < r - 1, rows(v, -1), 0.0)
        y = jnp.where(col > 0, lanes(v, 1), 0.0) + jnp.where(col < last, lanes(v, -1), 0.0)
        return 0.25 * (w[:n] + w[2:]) + x + y

    return apply


def k_whole(gathered, u, t3, x4, p3):
    ix, iy = lax.axis_index("gx"), lax.axis_index("gy")
    lane = iota((4, 128), 1) // 16
    for j in range(8):
        for n in range(3):
            for x in range(8):
                v = gathered[x * 24 + n]
                for y in range(1, 8):
                    v = jnp.where(lane == (j + y) % 8, gathered[x * 24 + 3 * y + n], v)
                t3[n, j, 4 * x : 4 * x + 4, :] = lanes(v, -16 * j) if j else v
    f3, s3, k3 = t3[0], t3[1], t3[2]
    near3 = spread_in((8, 32, 128), 127)
    w3, c3 = factors(s3, k3, 3)
    g3 = w3 * f3
    q3 = 0.4 * g3 + c3 * near3(g3)
    e3 = 0.04 * f3 + (weights(3)[0] * s3) * near3(q3)
    half = select_matrix((128, 128), lambda i, o: i // 2 == o, 0.125)
    fields = []
    for v in (e3, s3, k3):
        w = v.reshape(4, 2, 32, 128)
        x4[...] = w[:, 0] + w[:, 1]
        fields.append(dot3(x4[:, pl.ds(0, 16, 2), :] + x4[:, pl.ds(1, 16, 2), :], half))
    f4, s4, k4 = fields
    zero4, row4 = jnp.zeros((1, 16, 128), F32), iota((4, 16, 128), 1)

    def near4(v, before, after):
        w = jnp.concatenate([zero4, v, zero4], axis=0)
        x = jnp.where(row4 > 0, rows(v, 1), 0.0) + jnp.where(row4 < 15, rows(v, -1), 0.0)
        return (0.25 * (w[:4] + w[2:]) + x) + (before + after)

    w4, c4 = factors(s4, k4, 4)
    g4 = w4 * f4
    v4 = (0.2 * g4 + g4) + c4 * near4(g4, lanes(g4, 1), lanes(g4, -1))
    g4m, g4p, c4m, c4p = lanes(g4, 1), lanes(g4, -1), lanes(c4, 1), lanes(c4, -1)
    for _ in range(COARSE_SWEEPS // 2):
        vm, vp = lanes(v4, 1), lanes(v4, -1)
        am = (0.2 * vm + g4m) + c4m * near4(vm, lanes(v4, 2), v4)
        ap = (0.2 * vp + g4p) + c4p * near4(vp, v4, lanes(v4, -2))
        a = (0.2 * v4 + g4) + c4 * near4(v4, vm, vp)
        v4 = (0.2 * a + g4) + c4 * near4(a, am, ap)
    u4 = dot3(unscale(v4, s4), select_matrix((128, 128), lambda i, o: i == o // 2))
    p3[:, pl.ds(0, 16, 2), :] = u4
    p3[:, pl.ds(1, 16, 2), :] = u4
    w = p3[...]
    w = jnp.broadcast_to(w[:, None], (4, 2, 32, 128)).reshape(8, 32, 128)
    v3 = (q3 + 0.8 * g3) + s3 * w
    for _ in range(2):
        v3 = (0.2 * v3 + g3) + c3 * near3(v3)
    pick = select_matrix(
        (128, 128),
        lambda i, o: i == (jnp.where(o < 64, o // 2, 127 - (127 - o) // 2) + 16 * iy) % 128,
    )
    u[...] = pltpu.roll(dot3(v3 / s3, pick), (32 - 4 * ix) % 32, 1)


def k_up2(u3, g2, c2, s2, q2, u, p2):
    p2[:, 14:18, :] = jnp.zeros((8, 4, 128), F32)
    for n in range(2):
        p2[:, pl.ds(n, 7, 2), :] = u3[:, 0:7, :]
        p2[:, pl.ds(18 + n, 3, 2), :] = u3[:, 29:32, :]
    w = p2[...]
    w = jnp.broadcast_to(w[:, None], (8, 2, 24, 128)).reshape(16, 24, 128)
    gv, cv, sv = g2[...], c2[...], s2[...]
    zero = jnp.zeros((1, 24, 128), F32)
    v = (q2[...] + 0.8 * gv) + sv * w
    for _ in range(2):
        w = jnp.concatenate([zero, v, zero], axis=0)
        v = (0.2 * v + gv) + cv * around(w[:16], v, w[2:])
    pick = select_matrix(
        (128, 128),
        lambda i, o: i == jnp.where(o < 96, o // 2, 127 - (127 - o) // 2),
    )
    u[...] = dot3(unscale(v, sv), pick)


def k_up1(u2, g1, c1, s1, q1, u, p1, va, vb):
    for n in range(2):
        p1[:, pl.ds(n, 14, 2), :] = u2[:, 0:14, :]
        p1[:, pl.ds(28 + n, 6, 2), :] = u2[:, 18:24, :]
    for ref in (va, vb, u):
        ref[0] = jnp.zeros((40, 128), F32)
        ref[33] = jnp.zeros((40, 128), F32)

    def start(z, at):
        t = p1[pl.ds((z - 1) // 2, A1 // 2)]
        t = jnp.broadcast_to(t[:, None], (A1 // 2, 2, 40, 128)).reshape(A1, 40, 128)
        va[at] = (q1[at] + 0.8 * g1[at]) + s1[pl.ds(z - 1, A1)] * t

    blocks(1, 32, A1, start, U1)

    def sweep(z, at):
        vb[at] = (0.2 * va[at] + g1[at]) + c1[pl.ds(z - 1, A1)] * near(va, z, A1)

    blocks(1, 32, A1, sweep, U1)

    def last(z, at):
        own = pl.ds(z - 1, A1)
        v = (0.2 * vb[at] + g1[at]) + c1[own] * near(vb, z, A1)
        u[at] = unscale(v, s1[own])

    blocks(1, 32, A1, last, U1)


def k_up0(
    u1, gm, cm, sm, q, gw, cw, sw, qw, out, pm, pw, pv, wa, wb, ea, eb, done, sem
):
    iz = lax.axis_index("gz")

    def source(i, o):
        y = jnp.where(o % 16 < 8, 125 + o % 16, o % 16 - 11)
        return i == jnp.where(o < 128, o // 2, ((y + 256) // 2) % 128)

    u = u1[pl.ds(16 * iz, 18)]
    sub = iota((18, 8, 128), 1)
    u = jnp.concatenate([u[:, :16], jnp.where(sub < 4, u[:, 16:24], u[:, 32:40])], axis=1)
    u = dot3(u, select_matrix((128, 256), source))
    for h, ref in enumerate((pm, pw)):
        w = u[:, :, 128 * h : 128 * h + 128]
        for n in range(2):
            ref[:, pl.ds(n, 18, 2), :] = w[:, 0:18]
            ref[:, pl.ds(36 + n, 2, 2), :] = w[:, 22:24]
    pv[...] = lanes(pw[...], 8)
    slot = iota((40, 128), 1) // 8
    parts = []
    for side in range(2):
        for group in range(3):
            total = None
            for j in range(16):
                ref = pw if j % 2 == side else pv
                part = ref[min(max((16 * group + j - 1) // 2, 0), 17)]
                total = part if total is None else jnp.where(slot >= j, part, total)
            parts.append(total[None])
    g, c = gw[...], cw[...]
    v = (qw[...] + 0.8 * g) + sw[...] * jnp.concatenate(parts, axis=0)
    ea[...] = joint(v)
    eb[...] = joint((0.2 * v + g) + c * near_edges(v))

    def start(z, at):
        t = jnp.stack([pm[(z + i - 1) // 2] for i in range(A0)])
        wa[at] = (q[at] + 0.8 * gm[at]) + sm[at] * t

    blocks(1, 36, A0, start, U0)
    wa[0] = jnp.zeros((40, 128), F32)
    wa[37] = jnp.zeros((40, 128), F32)

    def sweep(z, at):
        wb[at] = (0.2 * wa[at] + gm[at]) + cm[at] * near_main(wa, ea, z, A0, True)

    blocks(1, 36, A0, sweep, U0)

    copies = []
    for b in range(32 // B0):
        z = 3 + b * B0
        at = pl.ds(z, B0)
        n = near_main(wb, eb, z, B0)[:, :32]
        v = (0.2 * wb[at, :32, :] + gm[at, :32, :]) + cm[at, :32, :] * n
        part = pl.ds(z - 3, B0)
        done[part] = v / sm[at, :32, :]
        copies.append(pltpu.make_async_copy(done.at[part], out.at[part], sem.at[b]))
        copies[-1].start()
    for copy in copies:
        copy.wait()


def ring(v, axis, step):
    n = lax.axis_size(axis)
    return lax.ppermute(v, axis, [(i, (i + step) % n) for i in range(n)])


def pair(to_right, to_left, axis):
    return ring(to_right, axis, 1), ring(to_left, axis, -1)


def pack_level1(own):
    n = own.shape[0]
    full, *msg = run(k_pack, (own,), [(n, 16, 128)] + [(-(-n // SLOTS), 16, 128)] * 2)
    return jnp.concatenate([full, *pair(*msg, "gy")], axis=0)


def after(values, *others):
    return lax.optimization_barrier((values, others))[0]


def shards(f, s, k):
    first = jnp.where(lax.axis_index("gz") == 0, 29, 0)
    fz, sz, kz = [lax.dynamic_slice_in_dim(v, first, 3, 0) for v in (f, s, k)]
    sw, c = factors(sz, kz, 0)
    near = (sw * fz, c, jnp.where(kz > 0.0, sz, 0.0))
    zr = ring(run(k_face_z, near, [(7, 32, 128)])[0], "gz", 1)
    g, c, sk1 = run(
        k_load, (f, s, k), [(32, 32, 128)] * 2 + [(16, 16, 128)], [(16, 32, 128)] * 2
    )
    sk1 = after(sk1, zr)
    sk_z = ring(sk1, "gz", 1)
    xs = pair(*run(k_face_x, (g, c, s, zr), [(38, 8, 128)] * 2), "gx")
    small, both = [(3, 40, 128)], [(6, 40, 128)]
    edges = run(k_pack_own, (g, c, s, zr), [(3, 32, 128)] * 3)
    *edges, to_right, to_left = run(k_face_y, (*edges, *xs), small * 5)
    ys = pair(to_right, to_left, "gy")
    gm, cm, sm = run(k_assemble, (g, c, s, zr, *xs), [(38, 40, 128)] * 3)
    sk1, sk_z = after((sk1, sk_z), gm)
    sk_y = pack_level1(jnp.concatenate([sk1, sk_z], axis=0))
    gw, cw, sw, q0, qw, f1 = run(
        k_down0,
        (f, gm, cm, sm, *edges, *ys),
        both * 3 + [(38, 40, 128)] + both + [(8, 16, 128)],
        [(16, 32, 128)] + small * 2,
    )
    sk = after(sk_y, f1)
    f1 = jnp.concatenate([f1, ring(f1, "gz", 1)], axis=0)
    s1, c1, w1, s2, c2, w2, sk3 = run(
        k_coeff,
        (sk, *pair(sk, sk, "gx")),
        [(32, 40, 128)] * 3 + [(16, 24, 128)] * 3 + [(8, 128)],
        [(16, 40, 128)] * 2 + [(16, 24, 128), (8, 8, 128), (32, 128)],
    )
    f1 = pack_level1(f1)
    g1, q1, g2, q2, chunk = run(
        k_down12,
        (f1, *pair(f1, f1, "gx"), s1, c1, w1, s2, c2, w2, sk3),
        [(34, 40, 128)] * 2 + [(16, 24, 128)] * 2 + [(96, 8, 128)],
        [(32, 40, 128), (16, 40, 128), (16, 24, 128), (8, 8, 128), (32, 128)],
    )
    gathered = lax.all_to_all(chunk.reshape(64, 1, 1536), ("gx", "gy"), 0, 0, tiled=True)
    gathered = gathered.reshape(192, 4, 128)
    (u3,) = run(
        k_whole, (gathered,), [(8, 32, 128)], [(3, 8, 32, 128), (4, 32, 128), (4, 32, 128)]
    )
    (u2,) = run(k_up2, (u3, g2, c2, s2, q2), [(16, 24, 128)], [(8, 24, 128)])
    (u1,) = run(
        k_up1, (u2, g1, c1, s1, q1), [(34, 40, 128)], [(16, 40, 128)] + [(34, 40, 128)] * 2
    )
    (out,) = run(
        k_up0,
        (u1, gm, cm, sm, q0, gw, cw, sw, qw),
        [(32, 32, 128)],
        [(18, 40, 128)] * 3 + [(38, 40, 128)] * 2 + small * 2 + [(32, 32, 128)],
        HBM,
        [(32 // B0,)],
    )
    return out


def solution(mesh):
    return jax.shard_map(
        shards,
        mesh=mesh,
        in_specs=(P("gz", "gx", "gy"),) * 3,
        out_specs=P("gz", "gx", "gy"),
        check_vma=False,
    )
```

```python
import math

import jax
import jax.numpy as jnp
from jax import lax
from jax.experimental import pallas as pl
from jax.experimental.pallas import tpu as pltpu
from jax.sharding import PartitionSpec as P

F32 = jnp.float32
VM = pl.BlockSpec(memory_space=pltpu.VMEM)
HBM = pl.BlockSpec(memory_space=pltpu.HBM)
BF16 = jnp.bfloat16
COARSE_SWEEPS = 11
MICROSECONDS = dict(
    k_face_z=0.2,
    k_load=4.0,
    k_face_x=0.2,
    k_pack_own=1.0,
    k_face_y=0.6,
    k_assemble=1.0,
    k_pack=0.3,
    k_relax=0.6,
    k_down0=1.5,
    k_coeff=2.0,
    k_down12=3.0,
    k_whole=2.0,
    k_up2=0.5,
    k_up1=1.5,
    k_up0=2.5,
)
A0, B0, U0 = 12, 8, 3
A1, U1 = 4, 8


def run(body, args, outs, scratch=(), out_spec=VM, sems=()):
    words = sum(math.prod(s) for s in (*outs, *scratch)) + sum(a.size for a in args)
    return pl.pallas_call(
        body,
        out_shape=[jax.ShapeDtypeStruct(o, F32) for o in outs],
        in_specs=[VM] * len(args),
        out_specs=[out_spec] * len(outs),
        scratch_shapes=[pltpu.VMEM(s, F32) for s in scratch]
        + [pltpu.SemaphoreType.DMA(n) for n in sems],
        compiler_params=pltpu.CompilerParams(vmem_limit_bytes=6 * words + (6 << 20)),
        cost_estimate=pl.CostEstimate(
            flops=0, transcendentals=0, bytes_accessed=int(3.5e6 * MICROSECONDS[body.__name__])
        ),
    )(*args)


def weights(level):
    wh = 0.25**level
    return wh, 2.0 * (0.25 * wh + 2.0 * wh)


def iota(shape, dim):
    return lax.broadcasted_iota(jnp.int32, shape, dim)


def lanes(v, shift):
    return pltpu.roll(v, shift % v.shape[-1], v.ndim - 1)


def rows(v, shift):
    return pltpu.roll(v, shift % v.shape[-2], v.ndim - 2)


def beside(v):
    return (rows(v, 1) + rows(v, -1)) + (lanes(v, 1) + lanes(v, -1))


def around(above, v, below):
    return 0.25 * (above + below) + beside(v)


def factors(s, k, level):
    wh, full = weights(level)
    diagonal = k + full * (s * s)
    sw = s * (0.8 / jnp.where(diagonal > 0.0, diagonal, 1.0))
    return sw, (wh * s) * sw


def unscale(v, s):
    inside = s > 0.0
    return jnp.where(inside, v / jnp.where(inside, s, 1.0), 0.0)


def dot(a, b):
    b = b.astype(BF16)
    high = a.astype(BF16)
    rest = a - high.astype(F32)
    middle = rest.astype(BF16)
    low = (rest - middle.astype(F32)).astype(BF16)
    terms = [jnp.dot(t, b, preferred_element_type=F32) for t in (high, middle, low)]
    return terms[0] + (terms[1] + terms[2])


def dot3(a, b):
    n, r, c = a.shape
    return dot(a.reshape(n * r, c), b).reshape(n, r, b.shape[1])


def blocks(first, count, size, body, unroll=1):
    def one(b, _):
        z = first + size * b
        body(z, pl.ds(z, size))
        return 0

    lax.fori_loop(0, count // size, one, 0, unroll=unroll)


def pair_sum(v):
    v = v.reshape(v.shape[0] // 2, 2, *v.shape[1:])
    return v[:, 0] + v[:, 1]


def select_matrix(shape, source_of, scale=1.0):
    i, o = iota(shape, 0), iota(shape, 1)
    return jnp.where(source_of(i, o), scale, 0.0).astype(F32)


def k_face_z(g, c, s, zmsg):
    upper = lax.axis_index("gz") == 0
    zmsg[0:3] = g[...]
    zmsg[3:5] = jnp.where(upper, c[1:], c[:2])
    zmsg[5:7] = jnp.where(upper, s[1:], s[:2])


def k_load(f, s, k, g, c, sk1, ps, pk):
    def one(z, at):
        sv, kv = s[at], k[at]
        sw, cv = factors(sv, kv, 0)
        g[at] = sw * f[at]
        c[at] = cv
        ps[pl.ds(z // 2, 2)] = pair_sum(sv)
        pk[pl.ds(z // 2, 2)] = pair_sum(kv)

    blocks(0, 32, 4, one, 2)
    a = ps[:, pl.ds(0, 16, 2), :] + ps[:, pl.ds(1, 16, 2), :]
    b = pk[:, pl.ds(0, 16, 2), :] + pk[:, pl.ds(1, 16, 2), :]
    left = select_matrix((128, 128), lambda i, o: i // 2 == o, 0.125)
    right = select_matrix((128, 128), lambda i, o: i // 2 == o - 64, 0.125)
    sk1[...] = dot3(a, left) + dot3(b, right)


def halo_rows(zr, iz, field, z):
    first, depth = ((0, 3), (3, 2), (5, 2))[field]
    d = z - 35 if z > 34 else 2 - z
    if d >= depth:
        return jnp.zeros(zr.shape[1:], F32)
    row = first + (d if z > 34 else depth - 1 - d)
    return jnp.where(iz == (0 if z > 34 else 1), zr[row], 0.0)


def k_face_x(g, c, s, zr, to_right, to_left):
    iz = lax.axis_index("gz")
    sub = iota((8, 128), 0)

    def put(z, gz, cz, sz):
        a, b, d = gz[24:32], cz[24:32], sz[24:32]
        to_right[z] = jnp.where(sub >= 5, a, jnp.where(sub >= 3, rows(b, -3), rows(d, -5)))
        a, b, d = gz[0:8], cz[0:8], sz[0:8]
        to_left[z] = jnp.where(sub < 3, a, jnp.where(sub < 5, rows(b, 3), rows(d, 5)))

    def one(z, _):
        put(z + 3, g[z], c[z], s[z])
        return 0

    lax.fori_loop(0, 32, one, 0, unroll=4)
    for z in (0, 1, 2, 35, 36, 37):
        put(z, *[halo_rows(zr, iz, n, z) for n in range(3)])


def k_pack_own(g, c, s, zr, *own):
    iz = lax.axis_index("gz")
    slot = iota((32, 128), 1)
    for n, (ref, out) in enumerate(zip((g, c, s), own)):
        for group in range(3):
            total = jnp.zeros((32, 128), F32)
            for j in range(16 if group < 2 else 6):
                z = 16 * group + j
                here = ref[z - 3] if 3 <= z < 35 else halo_rows(zr, iz, n, z)
                total = jnp.where(slot >= 8 * j, lanes(here, 8 * j + 3), total)
            out[group] = total


def side_rows(from_left, from_right, ix, z):
    sub = iota((8, 128), 0)
    lf = jnp.where(ix > 0, from_left[z], 0.0)
    rt = jnp.where(ix < 7, from_right[z], 0.0)
    return (
        jnp.where(sub >= 4, lf, rt),
        jnp.where(sub >= 4, rows(lf, 3), rows(rt, -3)),
        jnp.where(sub >= 4, rows(lf, 5), rows(rt, -5)),
    )


def k_face_y(og, oc, os, from_left, from_right, ag, ac, a_s, to_right, to_left):
    ix = lax.axis_index("gx")
    slot = iota((8, 128), 1)
    lane = iota((40, 128), 1) % 8
    for group in range(3):
        side = [jnp.zeros((8, 128), F32)] * 3
        mid = [ref[group] for ref in (og, oc, os)]
        for j in range(16 if group < 2 else 6):
            here = side_rows(from_left, from_right, ix, 16 * group + j)
            for n in range(3):
                side[n] = jnp.where(slot >= 8 * j, lanes(here[n], 8 * j + 3), side[n])
        g, c, s = [jnp.concatenate(parts, axis=0) for parts in zip(mid, side)]
        ag[group] = g
        ac[group] = c
        a_s[group] = s
        to_right[group] = jnp.where(
            lane < 3, g, jnp.where(lane < 5, lanes(c, 2), lanes(s, 4))
        )
        to_left[group] = jnp.where(
            lane >= 6, lanes(c, 3), jnp.where(lane >= 3, g, lanes(s, -2))
        )


def k_assemble(g, c, s, zr, from_left, from_right, gm, cm, sm):
    ix, iz = lax.axis_index("gx"), lax.axis_index("gz")

    def put(z, values):
        for ref, mid, side in zip(
            (gm, cm, sm), values, side_rows(from_left, from_right, ix, z)
        ):
            ref[z] = jnp.concatenate([mid, side], axis=0)

    def one(z, _):
        put(z + 3, (g[z], c[z], s[z]))
        return 0

    lax.fori_loop(0, 32, one, 0, unroll=4)
    for z in (0, 1, 2, 35, 36, 37):
        put(z, [halo_rows(zr, iz, n, z) for n in range(3)])


def near_edges(v):
    lane = iota(v.shape, 2)
    zero = jnp.zeros((1,) + v.shape[1:], F32)
    up, down = lanes(v, 8), lanes(v, -8)
    above = jnp.where(lane < 8, jnp.concatenate([zero, up[:-1]], axis=0), up)
    below = jnp.where(lane >= 120, jnp.concatenate([down[1:], zero], axis=0), down)
    return around(above, v, below)


def joint(v):
    lane = iota((3,) + v.shape[1:], 2)
    return jnp.where(lane % 8 == 4, lanes(v[3:], 2), v[:3])


def near_main(ref, edge, z, n, product=False):
    v = ref[pl.ds(z, n)]
    lane = iota(v.shape, 2)
    e = jnp.stack(
        [
            pltpu.roll(edge[(z + i) // 16], (124 - 8 * ((z + i) % 16)) % 128, 1)
            for i in range(n)
        ]
    )
    if product:
        across = dot3(v, select_matrix((128, 128), lambda i, o: (i == o + 1) | (i == o - 1)))
        across = jnp.where((lane == 0) | (lane == 127), e + across, across)
    else:
        across = jnp.where(lane == 0, e, lanes(v, 1)) + jnp.where(lane == 127, e, lanes(v, -1))
    above, below = ref[pl.ds(z - 1, n)], ref[pl.ds(z + 1, n)]
    return 0.25 * (above + below) + ((rows(v, 1) + rows(v, -1)) + across)


def near(ref, z, n):
    return around(ref[pl.ds(z - 1, n)], ref[pl.ds(z, n)], ref[pl.ds(z + 1, n)])


def k_relax(gm, cm, p):
    p[0] = jnp.zeros((40, 128), F32)
    p[37] = jnp.zeros((40, 128), F32)

    def relax(z, at):
        v = gm[at]
        beside_y = select_matrix((128, 128), lambda i, o: (i == o + 1) | (i == o - 1))
        across = dot3(v, beside_y) + (rows(v, 1) + rows(v, -1))
        above, below = gm[pl.ds(z - 1, A0)], gm[pl.ds(z + 1, A0)]
        p[at] = 0.4 * v + cm[at] * (0.25 * (above + below) + across)

    blocks(1, 36, A0, relax, U0)


def edge_rows(edge, z, n):
    return jnp.stack(
        [
            pltpu.roll(edge[(z + i) // 16], (124 - 8 * ((z + i) % 16)) % 128, 1)
            for i in range(n)
        ]
    )


def k_down0(
    f, p, gm, cm, sm, og, oc, os, from_left, from_right, gw, cw, sw, q, qw, f1, e, eg, eq
):
    iy = lax.axis_index("gy")
    own = iota((3, 40, 128), 2) % 8 < 3
    lf = jnp.where(iy > 0, from_left[...], 0.0)
    rt = jnp.where(iy < 7, from_right[...], 0.0)

    def windows(ref, right, left):
        mid = ref[...]
        return jnp.concatenate(
            [jnp.where(own, mid, right), jnp.where(own, left, mid)], axis=0
        )

    g = windows(og, rt, lf)
    c = windows(oc, lanes(rt, -3), lanes(lf, -2))
    gw[...] = g
    cw[...] = c
    sw[...] = windows(os, lanes(rt, 2), lanes(lf, -4))
    w = 0.4 * g + c * near_edges(g)
    qw[...] = w
    eg[...] = joint(g)
    eq[...] = joint(w)
    q[0] = jnp.zeros((40, 128), F32)
    q[37] = jnp.zeros((40, 128), F32)

    def relax(z, at):
        lane = iota((A0, 40, 128), 2)
        e = jnp.where((lane == 0) | (lane == 127), edge_rows(eg, z, A0), 0.0)
        q[at] = p[at] + cm[at] * e

    blocks(1, 36, A0, relax, U0)

    def residual(z, at):
        v = 0.04 * f[pl.ds(z - 3, B0)] + sm[at, :32, :] * near_main(q, eq, z, B0, True)[:, :32]
        e[pl.ds((z - 3) // 2, B0 // 2)] = pair_sum(v)

    blocks(3, 32, B0, residual, U0)
    a = e[:, pl.ds(0, 16, 2), :] + e[:, pl.ds(1, 16, 2), :]
    lo = select_matrix((128, 128), lambda i, o: i // 2 == o, 0.125)
    hi = select_matrix((128, 128), lambda i, o: i // 2 == o - 64, 0.125)
    f1[...] = dot3(a[:8], lo) + dot3(a[8:], hi)


SLOTS = 5


def k_pack(own, full, to_right, to_left):
    iz = lax.axis_index("gz")
    lane = iota((16, 128), 1) % 64
    n = own.shape[0]
    for group in range(to_right.shape[0]):
        count = min(SLOTS, n - SLOTS * group)
        a, b, kept = None, None, []
        for j in range(count):
            z = SLOTS * group + j
            own_half = iz == (0 if z < n // 2 else 1)
            v = own[z % (n // 2) + jnp.where(own_half, 0, n // 2)]
            kept.append(v)
            last, first = lanes(v, 12 * j - 52), lanes(v, 12 * j) if j else v
            a = last if a is None else jnp.where(lane >= 12 * j, last, a)
            b = first if b is None else jnp.where(lane >= 12 * j, first, b)
        full[SLOTS * group : SLOTS * group + count] = jnp.stack(kept)
        to_right[group] = a
        to_left[group] = b


def joined(own, xl, xr, at, ix):
    lf = jnp.where(ix > 0, xl[at], 0.0)
    rt = jnp.where(ix < 7, xr[at], 0.0)
    sub = iota((rt.shape[0], 8, 128), 1)
    edge = jnp.where(sub < 4, rt[:, 8:16], lf[:, 0:8])
    return jnp.concatenate([own[at], rt[:, 0:8], edge, lf[:, 8:16]], axis=1)


def opened(own, xl, xr, z, n, ix, iy):
    groups = -(-n // SLOTS)
    mid = joined(own, xl, xr, pl.ds(z, 4), ix)
    need = range(z // SLOTS, (z + 3) // SLOTS + 1)
    lf = [joined(own, xl, xr, pl.ds(n + i, 1), ix)[0] for i in need]
    rt = [joined(own, xl, xr, pl.ds(n + groups + i, 1), ix)[0] for i in need]
    lf = [jnp.where(iy > 0, v, 0.0) for v in lf]
    rt = [jnp.where(iy < 7, v, 0.0) for v in rt]
    at = [((z + i) // SLOTS - need[0], (z + i) % SLOTS) for i in range(4)]
    lf = jnp.stack([lanes(lf[i], 116 - 12 * j) for i, j in at])
    rt = jnp.stack([lanes(rt[i], 64 - 12 * j) for i, j in at])
    lane = iota(mid.shape, 2)
    first = jnp.where(lane < 64, mid, jnp.where(lane < 96, rt, lf))
    second = jnp.where(lane >= 64, mid, jnp.where(lane < 32, rt, lf))
    return first, lanes(second, 64)


def halve_x(ref, n, x2):
    x2[:, 14:18, :] = jnp.zeros((n, 4, 128), F32)
    x2[:, 0:14, :] = ref[:, pl.ds(0, 14, 2), :] + ref[:, pl.ds(1, 14, 2), :]
    x2[:, 18:24, :] = ref[:, pl.ds(28, 6, 2), :] + ref[:, pl.ds(29, 6, 2), :]
    return x2[...]


def down_matrix():
    return select_matrix(
        (128, 128),
        lambda i, o: ((i // 2 == o) & (o < 38)) | ((i // 2 == o - 64) & (o >= 122)),
        0.125,
    )


def level3_rows(v, e2, rows2):
    half = select_matrix((128, 128), lambda i, o: (i // 2 == o) & (o < 16), 0.125)
    e2[...] = pair_sum(v)[:, :8, :]
    for j in range(8):
        rows2[4 * j : 4 * j + 4] = e2[j, pl.ds(0, 4, 2), :] + e2[j, pl.ds(1, 4, 2), :]
    pieces = dot(rows2[...], half)
    total = pieces[0:4]
    for j in range(1, 8):
        total = total + lanes(pieces[4 * j : 4 * j + 4], 16 * j)
    return total


def k_coeff(own, xl, xr, s1, c1, w1, s2, c2, w2, sk3, ps, pk, x2, e2, r2):
    ix, iy = lax.axis_index("gx"), lax.axis_index("gy")

    for z in range(0, 32, 4):
        at = pl.ds(z, 4)
        s, k = opened(own, xl, xr, z, 32, ix, iy)
        s1[at] = s
        w1[at], c1[at] = factors(s, k, 1)
        ps[pl.ds(z // 2, 2)] = pair_sum(s)
        pk[pl.ds(z // 2, 2)] = pair_sum(k)
    down = down_matrix()
    s = dot3(halve_x(ps, 16, x2), down)
    k = dot3(halve_x(pk, 16, x2), down)
    s2[...] = s
    w2[...], c2[...] = factors(s, k, 2)
    sk3[...] = jnp.concatenate([level3_rows(s, e2, r2), level3_rows(k, e2, r2)], axis=0)


def k_down12(own, xl, xr, s1, c1, w1, s2, c2, w2, sk3, g, q, g2, q2, chunk, f, e, x2, e2, r2):
    ix, iy = lax.axis_index("gx"), lax.axis_index("gy")
    for ref in (g, q):
        ref[0] = jnp.zeros((40, 128), F32)
        ref[33] = jnp.zeros((40, 128), F32)

    for z in range(0, 16, 4):
        for i, v in enumerate(opened(own, xl, xr, z, 16, ix, iy)):
            first = z + 8 * (z // 8) + 8 * i
            f[pl.ds(first, 4)] = v
            g[pl.ds(first + 1, 4)] = w1[pl.ds(first, 4)] * v

    def relax(z, at):
        q[at] = 0.4 * g[at] + c1[pl.ds(z - 1, A1)] * near(g, z, A1)

    blocks(1, 32, A1, relax, U1)
    wh, _ = weights(1)

    def residual(z, at):
        own = pl.ds(z - 1, A1)
        v = 0.04 * f[own] + (wh * s1[own]) * near(q, z, A1)
        e[pl.ds((z - 1) // 2, A1 // 2)] = pair_sum(v)

    blocks(1, 32, A1, residual, U1)
    fv = dot3(halve_x(e, 16, x2), down_matrix())
    gv = w2[...] * fv
    zero = jnp.zeros((1, 24, 128), F32)

    def spread(v):
        w = jnp.concatenate([zero, v, zero], axis=0)
        return around(w[:16], v, w[2:])

    qv = 0.4 * gv + c2[...] * spread(gv)
    wh, _ = weights(2)
    ev = 0.04 * fv + (wh * s2[...]) * spread(qv)
    g2[...] = gv
    q2[...] = qv
    parts = [level3_rows(ev, e2, r2), sk3[:4], sk3[4:]]
    parts = [pltpu.roll(part, 16 * iy, 1) for part in parts]

    tiles = [jnp.concatenate([parts[i], parts[(i + 1) % 3]], axis=0) for i in (0, 2, 1)]

    def copy(n, _):
        for i in range(3):
            chunk[3 * n + i] = tiles[i]
        return 0

    lax.fori_loop(0, 32, copy, 0, unroll=8)


def spread_in(shape, last):
    n, r, _ = shape
    row, col = iota(shape, 1), iota(shape, 2)
    zero = jnp.zeros((1,) + shape[1:], F32)

    def apply(v):
        w = jnp.concatenate([zero, v, zero], axis=0)
        x = jnp.where(row > 0, rows(v, 1), 0.0) + jnp.where(row < r - 1, rows(v, -1), 0.0)
        y = jnp.where(col > 0, lanes(v, 1), 0.0) + jnp.where(col < last, lanes(v, -1), 0.0)
        return 0.25 * (w[:n] + w[2:]) + x + y

    return apply


def k_whole(gathered, u, t3, x4, p3):
    ix, iy = lax.axis_index("gx"), lax.axis_index("gy")
    lane = iota((4, 128), 1) // 16
    for j in range(8):
        for n in range(3):
            for x in range(8):
                v = gathered[x * 24 + n]
                for y in range(1, 8):
                    v = jnp.where(lane == (j + y) % 8, gathered[x * 24 + 3 * y + n], v)
                t3[n, j, 4 * x : 4 * x + 4, :] = lanes(v, -16 * j) if j else v
    f3, s3, k3 = t3[0], t3[1], t3[2]
    near3 = spread_in((8, 32, 128), 127)
    w3, c3 = factors(s3, k3, 3)
    g3 = w3 * f3
    q3 = 0.4 * g3 + c3 * near3(g3)
    e3 = 0.04 * f3 + (weights(3)[0] * s3) * near3(q3)
    half = select_matrix((128, 128), lambda i, o: i // 2 == o, 0.125)
    fields = []
    for v in (e3, s3, k3):
        w = v.reshape(4, 2, 32, 128)
        x4[...] = w[:, 0] + w[:, 1]
        fields.append(dot3(x4[:, pl.ds(0, 16, 2), :] + x4[:, pl.ds(1, 16, 2), :], half))
    f4, s4, k4 = fields
    zero4, row4 = jnp.zeros((1, 16, 128), F32), iota((4, 16, 128), 1)

    def near4(v, before, after):
        w = jnp.concatenate([zero4, v, zero4], axis=0)
        x = jnp.where(row4 > 0, rows(v, 1), 0.0) + jnp.where(row4 < 15, rows(v, -1), 0.0)
        return (0.25 * (w[:4] + w[2:]) + x) + (before + after)

    w4, c4 = factors(s4, k4, 4)
    g4 = w4 * f4
    v4 = (0.2 * g4 + g4) + c4 * near4(g4, lanes(g4, 1), lanes(g4, -1))
    g4m, g4p, c4m, c4p = lanes(g4, 1), lanes(g4, -1), lanes(c4, 1), lanes(c4, -1)
    for _ in range(COARSE_SWEEPS // 2):
        vm, vp = lanes(v4, 1), lanes(v4, -1)
        am = (0.2 * vm + g4m) + c4m * near4(vm, lanes(v4, 2), v4)
        ap = (0.2 * vp + g4p) + c4p * near4(vp, v4, lanes(v4, -2))
        a = (0.2 * v4 + g4) + c4 * near4(v4, vm, vp)
        v4 = (0.2 * a + g4) + c4 * near4(a, am, ap)
    u4 = dot3(unscale(v4, s4), select_matrix((128, 128), lambda i, o: i == o // 2))
    p3[:, pl.ds(0, 16, 2), :] = u4
    p3[:, pl.ds(1, 16, 2), :] = u4
    w = p3[...]
    w = jnp.broadcast_to(w[:, None], (4, 2, 32, 128)).reshape(8, 32, 128)
    v3 = (q3 + 0.8 * g3) + s3 * w
    for _ in range(2):
        v3 = (0.2 * v3 + g3) + c3 * near3(v3)
    pick = select_matrix(
        (128, 128),
        lambda i, o: i == (jnp.where(o < 64, o // 2, 127 - (127 - o) // 2) + 16 * iy) % 128,
    )
    u[...] = pltpu.roll(dot3(v3 / s3, pick), (32 - 4 * ix) % 32, 1)


def k_up2(u3, g2, c2, s2, q2, u, p2):
    p2[:, 14:18, :] = jnp.zeros((8, 4, 128), F32)
    for n in range(2):
        p2[:, pl.ds(n, 7, 2), :] = u3[:, 0:7, :]
        p2[:, pl.ds(18 + n, 3, 2), :] = u3[:, 29:32, :]
    w = p2[...]
    w = jnp.broadcast_to(w[:, None], (8, 2, 24, 128)).reshape(16, 24, 128)
    gv, cv, sv = g2[...], c2[...], s2[...]
    zero = jnp.zeros((1, 24, 128), F32)
    v = (q2[...] + 0.8 * gv) + sv * w
    for _ in range(2):
        w = jnp.concatenate([zero, v, zero], axis=0)
        v = (0.2 * v + gv) + cv * around(w[:16], v, w[2:])
    pick = select_matrix(
        (128, 128),
        lambda i, o: i == jnp.where(o < 96, o // 2, 127 - (127 - o) // 2),
    )
    u[...] = dot3(unscale(v, sv), pick)


def k_up1(u2, g1, c1, s1, q1, u, p1, va, vb):
    for n in range(2):
        p1[:, pl.ds(n, 14, 2), :] = u2[:, 0:14, :]
        p1[:, pl.ds(28 + n, 6, 2), :] = u2[:, 18:24, :]
    for ref in (va, vb, u):
        ref[0] = jnp.zeros((40, 128), F32)
        ref[33] = jnp.zeros((40, 128), F32)

    def start(z, at):
        t = p1[pl.ds((z - 1) // 2, A1 // 2)]
        t = jnp.broadcast_to(t[:, None], (A1 // 2, 2, 40, 128)).reshape(A1, 40, 128)
        va[at] = (q1[at] + 0.8 * g1[at]) + s1[pl.ds(z - 1, A1)] * t

    blocks(1, 32, A1, start, U1)

    def sweep(z, at):
        vb[at] = (0.2 * va[at] + g1[at]) + c1[pl.ds(z - 1, A1)] * near(va, z, A1)

    blocks(1, 32, A1, sweep, U1)

    def last(z, at):
        own = pl.ds(z - 1, A1)
        v = (0.2 * vb[at] + g1[at]) + c1[own] * near(vb, z, A1)
        u[at] = unscale(v, s1[own])

    blocks(1, 32, A1, last, U1)


def k_up0(
    u1, gm, cm, sm, q, gw, cw, sw, qw, out, pm, pw, pv, wa, wb, ea, eb, done, sem
):
    iz = lax.axis_index("gz")

    def source(i, o):
        y = jnp.where(o % 16 < 8, 125 + o % 16, o % 16 - 11)
        return i == jnp.where(o < 128, o // 2, ((y + 256) // 2) % 128)

    u = u1[pl.ds(16 * iz, 18)]
    sub = iota((18, 8, 128), 1)
    u = jnp.concatenate([u[:, :16], jnp.where(sub < 4, u[:, 16:24], u[:, 32:40])], axis=1)
    u = dot3(u, select_matrix((128, 256), source))
    for h, ref in enumerate((pm, pw)):
        w = u[:, :, 128 * h : 128 * h + 128]
        for n in range(2):
            ref[:, pl.ds(n, 18, 2), :] = w[:, 0:18]
            ref[:, pl.ds(36 + n, 2, 2), :] = w[:, 22:24]
    pv[...] = lanes(pw[...], 8)
    slot = iota((40, 128), 1) // 8
    parts = []
    for side in range(2):
        for group in range(3):
            total = None
            for j in range(16):
                ref = pw if j % 2 == side else pv
                part = ref[min(max((16 * group + j - 1) // 2, 0), 17)]
                total = part if total is None else jnp.where(slot >= j, part, total)
            parts.append(total[None])
    g, c = gw[...], cw[...]
    v = (qw[...] + 0.8 * g) + sw[...] * jnp.concatenate(parts, axis=0)
    ea[...] = joint(v)
    eb[...] = joint((0.2 * v + g) + c * near_edges(v))

    def start(z, at):
        t = jnp.stack([pm[(z + i - 1) // 2] for i in range(A0)])
        wa[at] = (q[at] + 0.8 * gm[at]) + sm[at] * t

    blocks(1, 36, A0, start, U0)
    wa[0] = jnp.zeros((40, 128), F32)
    wa[37] = jnp.zeros((40, 128), F32)

    def sweep(z, at):
        wb[at] = (0.2 * wa[at] + gm[at]) + cm[at] * near_main(wa, ea, z, A0, True)

    blocks(1, 36, A0, sweep, U0)

    copies = []
    for b in range(32 // B0):
        z = 3 + b * B0
        at = pl.ds(z, B0)
        n = near_main(wb, eb, z, B0)[:, :32]
        v = (0.2 * wb[at, :32, :] + gm[at, :32, :]) + cm[at, :32, :] * n
        part = pl.ds(z - 3, B0)
        done[part] = v / sm[at, :32, :]
        copies.append(pltpu.make_async_copy(done.at[part], out.at[part], sem.at[b]))
        copies[-1].start()
    for copy in copies:
        copy.wait()


def ring(v, axis, step):
    n = lax.axis_size(axis)
    return lax.ppermute(v, axis, [(i, (i + step) % n) for i in range(n)])


def pair(to_right, to_left, axis):
    return ring(to_right, axis, 1), ring(to_left, axis, -1)


def pack_level1(own):
    n = own.shape[0]
    full, *msg = run(k_pack, (own,), [(n, 16, 128)] + [(-(-n // SLOTS), 16, 128)] * 2)
    return jnp.concatenate([full, *pair(*msg, "gy")], axis=0)


def after(values, *others):
    return lax.optimization_barrier((values, others))[0]


def shards(f, s, k):
    first = jnp.where(lax.axis_index("gz") == 0, 29, 0)
    fz, sz, kz = [lax.dynamic_slice_in_dim(v, first, 3, 0) for v in (f, s, k)]
    sw, c = factors(sz, kz, 0)
    near = (sw * fz, c, jnp.where(kz > 0.0, sz, 0.0))
    zr = ring(run(k_face_z, near, [(7, 32, 128)])[0], "gz", 1)
    g, c, sk1 = run(
        k_load, (f, s, k), [(32, 32, 128)] * 2 + [(16, 16, 128)], [(16, 32, 128)] * 2
    )
    sk1 = after(sk1, zr)
    sk_z = ring(sk1, "gz", 1)
    xs = pair(*run(k_face_x, (g, c, s, zr), [(38, 8, 128)] * 2), "gx")
    small, both = [(3, 40, 128)], [(6, 40, 128)]
    edges = run(k_pack_own, (g, c, s, zr), [(3, 32, 128)] * 3)
    *edges, to_right, to_left = run(k_face_y, (*edges, *xs), small * 5)
    ys = pair(to_right, to_left, "gy")
    gm, cm, sm = run(k_assemble, (g, c, s, zr, *xs), [(38, 40, 128)] * 3)
    sk1, sk_z = after((sk1, sk_z), gm)
    sk_y = pack_level1(jnp.concatenate([sk1, sk_z], axis=0))
    gw, cw, sw, q0, qw, f1 = run(
        k_down0,
        (f, *run(k_relax, (gm, cm), [(38, 40, 128)]), gm, cm, sm, *edges, *ys),
        both * 3 + [(38, 40, 128)] + both + [(8, 16, 128)],
        [(16, 32, 128)] + small * 2,
    )
    sk = after(sk_y, f1)
    f1 = jnp.concatenate([f1, ring(f1, "gz", 1)], axis=0)
    s1, c1, w1, s2, c2, w2, sk3 = run(
        k_coeff,
        (sk, *pair(sk, sk, "gx")),
        [(32, 40, 128)] * 3 + [(16, 24, 128)] * 3 + [(8, 128)],
        [(16, 40, 128)] * 2 + [(16, 24, 128), (8, 8, 128), (32, 128)],
    )
    f1 = pack_level1(f1)
    g1, q1, g2, q2, chunk = run(
        k_down12,
        (f1, *pair(f1, f1, "gx"), s1, c1, w1, s2, c2, w2, sk3),
        [(34, 40, 128)] * 2 + [(16, 24, 128)] * 2 + [(96, 8, 128)],
        [(32, 40, 128), (16, 40, 128), (16, 24, 128), (8, 8, 128), (32, 128)],
    )
    gathered = lax.all_to_all(chunk.reshape(64, 1, 1536), ("gx", "gy"), 0, 0, tiled=True)
    gathered = gathered.reshape(192, 4, 128)
    (u3,) = run(
        k_whole, (gathered,), [(8, 32, 128)], [(3, 8, 32, 128), (4, 32, 128), (4, 32, 128)]
    )
    (u2,) = run(k_up2, (u3, g2, c2, s2, q2), [(16, 24, 128)], [(8, 24, 128)])
    (u1,) = run(
        k_up1, (u2, g1, c1, s1, q1), [(34, 40, 128)], [(16, 40, 128)] + [(34, 40, 128)] * 2
    )
    (out,) = run(
        k_up0,
        (u1, gm, cm, sm, q0, gw, cw, sw, qw),
        [(32, 32, 128)],
        [(18, 40, 128)] * 3 + [(38, 40, 128)] * 2 + small * 2 + [(32, 32, 128)],
        HBM,
        [(32 // B0,)],
    )
    return out


def solution(mesh):
    return jax.shard_map(
        shards,
        mesh=mesh,
        in_specs=(P("gz", "gx", "gy"),) * 3,
        out_specs=P("gz", "gx", "gy"),
        check_vma=False,
    )
```

```python
import math

import jax
import jax.numpy as jnp
from jax import lax
from jax.experimental import pallas as pl
from jax.experimental.pallas import tpu as pltpu
from jax.sharding import PartitionSpec as P

F32 = jnp.float32
VM = pl.BlockSpec(memory_space=pltpu.VMEM)
HBM = pl.BlockSpec(memory_space=pltpu.HBM)
BF16 = jnp.bfloat16
COARSE_SWEEPS = 11
MICROSECONDS = dict(
    k_face_z=0.2,
    k_load=4.0,
    k_face_x=0.2,
    k_pack_own=1.0,
    k_face_y=0.6,
    k_assemble=1.0,
    k_pack=0.3,
    k_down0=2.0,
    k_coeff=2.0,
    k_down12=3.0,
    k_up=6.0,
)
A0, B0, U0 = 12, 8, 3
A1, U1 = 4, 8


def run(body, args, outs, scratch=(), out_spec=VM, sems=()):
    words = sum(math.prod(s) for s in (*outs, *scratch)) + sum(a.size for a in args)
    return pl.pallas_call(
        body,
        out_shape=[jax.ShapeDtypeStruct(o, F32) for o in outs],
        in_specs=[VM] * len(args),
        out_specs=[out_spec] * len(outs),
        scratch_shapes=[pltpu.VMEM(s, F32) for s in scratch]
        + [pltpu.SemaphoreType.DMA(n) for n in sems],
        compiler_params=pltpu.CompilerParams(vmem_limit_bytes=6 * words + (6 << 20)),
        cost_estimate=pl.CostEstimate(
            flops=0, transcendentals=0, bytes_accessed=int(3.5e6 * MICROSECONDS[body.__name__])
        ),
    )(*args)


def weights(level):
    wh = 0.25**level
    return wh, 2.0 * (0.25 * wh + 2.0 * wh)


def iota(shape, dim):
    return lax.broadcasted_iota(jnp.int32, shape, dim)


def lanes(v, shift):
    return pltpu.roll(v, shift % v.shape[-1], v.ndim - 1)


def rows(v, shift):
    return pltpu.roll(v, shift % v.shape[-2], v.ndim - 2)


def beside(v):
    return (rows(v, 1) + rows(v, -1)) + (lanes(v, 1) + lanes(v, -1))


def around(above, v, below):
    return 0.25 * (above + below) + beside(v)


def factors(s, k, level):
    wh, full = weights(level)
    diagonal = k + full * (s * s)
    sw = s * (0.8 / jnp.where(diagonal > 0.0, diagonal, 1.0))
    return sw, (wh * s) * sw


def unscale(v, s):
    inside = s > 0.0
    return jnp.where(inside, v / jnp.where(inside, s, 1.0), 0.0)


def dot(a, b):
    b = b.astype(BF16)
    high = a.astype(BF16)
    rest = a - high.astype(F32)
    middle = rest.astype(BF16)
    low = (rest - middle.astype(F32)).astype(BF16)
    terms = [jnp.dot(t, b, preferred_element_type=F32) for t in (high, middle, low)]
    return terms[0] + (terms[1] + terms[2])


def dot3(a, b):
    n, r, c = a.shape
    return dot(a.reshape(n * r, c), b).reshape(n, r, b.shape[1])


def blocks(first, count, size, body, unroll=1):
    def one(b, _):
        z = first + size * b
        body(z, pl.ds(z, size))
        return 0

    lax.fori_loop(0, count // size, one, 0, unroll=unroll)


def pair_sum(v):
    v = v.reshape(v.shape[0] // 2, 2, *v.shape[1:])
    return v[:, 0] + v[:, 1]


def select_matrix(shape, source_of, scale=1.0):
    i, o = iota(shape, 0), iota(shape, 1)
    return jnp.where(source_of(i, o), scale, 0.0).astype(F32)


def k_face_z(g, c, s, zmsg):
    upper = lax.axis_index("gz") == 0
    zmsg[0:3] = g[...]
    zmsg[3:5] = jnp.where(upper, c[1:], c[:2])
    zmsg[5:7] = jnp.where(upper, s[1:], s[:2])


def k_load(f, s, k, g, c, sk1, ps, pk):
    def one(z, at):
        sv, kv = s[at], k[at]
        sw, cv = factors(sv, kv, 0)
        g[at] = sw * f[at]
        c[at] = cv
        ps[pl.ds(z // 2, 2)] = pair_sum(sv)
        pk[pl.ds(z // 2, 2)] = pair_sum(kv)

    blocks(0, 32, 4, one, 2)
    a = ps[:, pl.ds(0, 16, 2), :] + ps[:, pl.ds(1, 16, 2), :]
    b = pk[:, pl.ds(0, 16, 2), :] + pk[:, pl.ds(1, 16, 2), :]
    left = select_matrix((128, 128), lambda i, o: i // 2 == o, 0.125)
    right = select_matrix((128, 128), lambda i, o: i // 2 == o - 64, 0.125)
    sk1[...] = dot3(a, left) + dot3(b, right)


def halo_rows(zr, iz, field, z):
    first, depth = ((0, 3), (3, 2), (5, 2))[field]
    d = z - 35 if z > 34 else 2 - z
    if d >= depth:
        return jnp.zeros(zr.shape[1:], F32)
    row = first + (d if z > 34 else depth - 1 - d)
    return jnp.where(iz == (0 if z > 34 else 1), zr[row], 0.0)


def k_face_x(g, c, s, zr, to_right, to_left):
    iz = lax.axis_index("gz")
    sub = iota((8, 128), 0)

    def put(z, gz, cz, sz):
        a, b, d = gz[24:32], cz[24:32], sz[24:32]
        to_right[z] = jnp.where(sub >= 5, a, jnp.where(sub >= 3, rows(b, -3), rows(d, -5)))
        a, b, d = gz[0:8], cz[0:8], sz[0:8]
        to_left[z] = jnp.where(sub < 3, a, jnp.where(sub < 5, rows(b, 3), rows(d, 5)))

    def one(z, _):
        put(z + 3, g[z], c[z], s[z])
        return 0

    lax.fori_loop(0, 32, one, 0, unroll=4)
    for z in (0, 1, 2, 35, 36, 37):
        put(z, *[halo_rows(zr, iz, n, z) for n in range(3)])


def k_pack_own(g, c, s, zr, *own):
    iz = lax.axis_index("gz")
    slot = iota((32, 128), 1)
    for n, (ref, out) in enumerate(zip((g, c, s), own)):
        for group in range(3):
            total = jnp.zeros((32, 128), F32)
            for j in range(16 if group < 2 else 6):
                z = 16 * group + j
                here = ref[z - 3] if 3 <= z < 35 else halo_rows(zr, iz, n, z)
                total = jnp.where(slot >= 8 * j, lanes(here, 8 * j + 3), total)
            out[group] = total


def side_rows(from_left, from_right, ix, z):
    sub = iota((8, 128), 0)
    lf = jnp.where(ix > 0, from_left[z], 0.0)
    rt = jnp.where(ix < 7, from_right[z], 0.0)
    return (
        jnp.where(sub >= 4, lf, rt),
        jnp.where(sub >= 4, rows(lf, 3), rows(rt, -3)),
        jnp.where(sub >= 4, rows(lf, 5), rows(rt, -5)),
    )


def k_face_y(og, oc, os, from_left, from_right, ag, ac, a_s, to_right, to_left):
    ix = lax.axis_index("gx")
    slot = iota((8, 128), 1)
    lane = iota((40, 128), 1) % 8
    for group in range(3):
        side = [jnp.zeros((8, 128), F32)] * 3
        mid = [ref[group] for ref in (og, oc, os)]
        for j in range(16 if group < 2 else 6):
            here = side_rows(from_left, from_right, ix, 16 * group + j)
            for n in range(3):
                side[n] = jnp.where(slot >= 8 * j, lanes(here[n], 8 * j + 3), side[n])
        g, c, s = [jnp.concatenate(parts, axis=0) for parts in zip(mid, side)]
        ag[group] = g
        ac[group] = c
        a_s[group] = s
        to_right[group] = jnp.where(
            lane < 3, g, jnp.where(lane < 5, lanes(c, 2), lanes(s, 4))
        )
        to_left[group] = jnp.where(
            lane >= 6, lanes(c, 3), jnp.where(lane >= 3, g, lanes(s, -2))
        )


def k_assemble(g, c, s, zr, from_left, from_right, gm, cm, sm):
    ix, iz = lax.axis_index("gx"), lax.axis_index("gz")

    def put(z, values):
        for ref, mid, side in zip(
            (gm, cm, sm), values, side_rows(from_left, from_right, ix, z)
        ):
            ref[z] = jnp.concatenate([mid, side], axis=0)

    def one(z, _):
        put(z + 3, (g[z], c[z], s[z]))
        return 0

    lax.fori_loop(0, 32, one, 0, unroll=4)
    for z in (0, 1, 2, 35, 36, 37):
        put(z, [halo_rows(zr, iz, n, z) for n in range(3)])


def near_edges(v):
    lane = iota(v.shape, 2)
    zero = jnp.zeros((1,) + v.shape[1:], F32)
    up, down = lanes(v, 8), lanes(v, -8)
    above = jnp.where(lane < 8, jnp.concatenate([zero, up[:-1]], axis=0), up)
    below = jnp.where(lane >= 120, jnp.concatenate([down[1:], zero], axis=0), down)
    return around(above, v, below)


def joint(v):
    lane = iota((3,) + v.shape[1:], 2)
    return jnp.where(lane % 8 == 4, lanes(v[3:], 2), v[:3])


def near_main(ref, edge, z, n, product=False):
    v = ref[pl.ds(z, n)]
    lane = iota(v.shape, 2)
    e = jnp.stack(
        [
            pltpu.roll(edge[(z + i) // 16], (124 - 8 * ((z + i) % 16)) % 128, 1)
            for i in range(n)
        ]
    )
    if product:
        across = dot3(v, select_matrix((128, 128), lambda i, o: (i == o + 1) | (i == o - 1)))
        across = jnp.where((lane == 0) | (lane == 127), e + across, across)
    else:
        across = jnp.where(lane == 0, e, lanes(v, 1)) + jnp.where(lane == 127, e, lanes(v, -1))
    above, below = ref[pl.ds(z - 1, n)], ref[pl.ds(z + 1, n)]
    return 0.25 * (above + below) + ((rows(v, 1) + rows(v, -1)) + across)


def near(ref, z, n):
    return around(ref[pl.ds(z - 1, n)], ref[pl.ds(z, n)], ref[pl.ds(z + 1, n)])


def k_down0(
    f, gm, cm, sm, og, oc, os, from_left, from_right, gw, cw, sw, q, qw, f1, e, eg, eq
):
    iy = lax.axis_index("gy")
    own = iota((3, 40, 128), 2) % 8 < 3
    lf = jnp.where(iy > 0, from_left[...], 0.0)
    rt = jnp.where(iy < 7, from_right[...], 0.0)

    def windows(ref, right, left):
        mid = ref[...]
        return jnp.concatenate(
            [jnp.where(own, mid, right), jnp.where(own, left, mid)], axis=0
        )

    g = windows(og, rt, lf)
    c = windows(oc, lanes(rt, -3), lanes(lf, -2))
    gw[...] = g
    cw[...] = c
    sw[...] = windows(os, lanes(rt, 2), lanes(lf, -4))
    w = 0.4 * g + c * near_edges(g)
    qw[...] = w
    eg[...] = joint(g)
    eq[...] = joint(w)
    q[0] = jnp.zeros((40, 128), F32)
    q[37] = jnp.zeros((40, 128), F32)

    def relax(z, at):
        q[at] = 0.4 * gm[at] + cm[at] * near_main(gm, eg, z, A0, True)

    blocks(1, 36, A0, relax, U0)

    def residual(z, at):
        v = 0.04 * f[pl.ds(z - 3, B0)] + sm[at, :32, :] * near_main(q, eq, z, B0, True)[:, :32]
        e[pl.ds((z - 3) // 2, B0 // 2)] = pair_sum(v)

    blocks(3, 32, B0, residual, U0)
    a = e[:, pl.ds(0, 16, 2), :] + e[:, pl.ds(1, 16, 2), :]
    lo = select_matrix((128, 128), lambda i, o: i // 2 == o, 0.125)
    hi = select_matrix((128, 128), lambda i, o: i // 2 == o - 64, 0.125)
    f1[...] = dot3(a[:8], lo) + dot3(a[8:], hi)


SLOTS = 5


def k_pack(own, full, to_right, to_left):
    iz = lax.axis_index("gz")
    lane = iota((16, 128), 1) % 64
    n = own.shape[0]
    for group in range(to_right.shape[0]):
        count = min(SLOTS, n - SLOTS * group)
        a, b, kept = None, None, []
        for j in range(count):
            z = SLOTS * group + j
            own_half = iz == (0 if z < n // 2 else 1)
            v = own[z % (n // 2) + jnp.where(own_half, 0, n // 2)]
            kept.append(v)
            last, first = lanes(v, 12 * j - 52), lanes(v, 12 * j) if j else v
            a = last if a is None else jnp.where(lane >= 12 * j, last, a)
            b = first if b is None else jnp.where(lane >= 12 * j, first, b)
        full[SLOTS * group : SLOTS * group + count] = jnp.stack(kept)
        to_right[group] = a
        to_left[group] = b


def joined(own, xl, xr, at, ix):
    lf = jnp.where(ix > 0, xl[at], 0.0)
    rt = jnp.where(ix < 7, xr[at], 0.0)
    sub = iota((rt.shape[0], 8, 128), 1)
    edge = jnp.where(sub < 4, rt[:, 8:16], lf[:, 0:8])
    return jnp.concatenate([own[at], rt[:, 0:8], edge, lf[:, 8:16]], axis=1)


def opened(own, xl, xr, z, n, ix, iy):
    groups = -(-n // SLOTS)
    mid = joined(own, xl, xr, pl.ds(z, 4), ix)
    need = range(z // SLOTS, (z + 3) // SLOTS + 1)
    lf = [joined(own, xl, xr, pl.ds(n + i, 1), ix)[0] for i in need]
    rt = [joined(own, xl, xr, pl.ds(n + groups + i, 1), ix)[0] for i in need]
    lf = [jnp.where(iy > 0, v, 0.0) for v in lf]
    rt = [jnp.where(iy < 7, v, 0.0) for v in rt]
    at = [((z + i) // SLOTS - need[0], (z + i) % SLOTS) for i in range(4)]
    lf = jnp.stack([lanes(lf[i], 116 - 12 * j) for i, j in at])
    rt = jnp.stack([lanes(rt[i], 64 - 12 * j) for i, j in at])
    lane = iota(mid.shape, 2)
    first = jnp.where(lane < 64, mid, jnp.where(lane < 96, rt, lf))
    second = jnp.where(lane >= 64, mid, jnp.where(lane < 32, rt, lf))
    return first, lanes(second, 64)


def halve_x(ref, n, x2):
    x2[:, 14:18, :] = jnp.zeros((n, 4, 128), F32)
    x2[:, 0:14, :] = ref[:, pl.ds(0, 14, 2), :] + ref[:, pl.ds(1, 14, 2), :]
    x2[:, 18:24, :] = ref[:, pl.ds(28, 6, 2), :] + ref[:, pl.ds(29, 6, 2), :]
    return x2[...]


def down_matrix():
    return select_matrix(
        (128, 128),
        lambda i, o: ((i // 2 == o) & (o < 38)) | ((i // 2 == o - 64) & (o >= 122)),
        0.125,
    )


def level3_rows(v, e2, rows2):
    half = select_matrix((128, 128), lambda i, o: (i // 2 == o) & (o < 16), 0.125)
    e2[...] = pair_sum(v)[:, :8, :]
    for j in range(8):
        rows2[4 * j : 4 * j + 4] = e2[j, pl.ds(0, 4, 2), :] + e2[j, pl.ds(1, 4, 2), :]
    pieces = dot(rows2[...], half)
    total = pieces[0:4]
    for j in range(1, 8):
        total = total + lanes(pieces[4 * j : 4 * j + 4], 16 * j)
    return total


def k_coeff(own, xl, xr, s1, c1, w1, s2, c2, w2, sk3, ps, pk, x2, e2, r2):
    ix, iy = lax.axis_index("gx"), lax.axis_index("gy")

    for z in range(0, 32, 4):
        at = pl.ds(z, 4)
        s, k = opened(own, xl, xr, z, 32, ix, iy)
        s1[at] = s
        w1[at], c1[at] = factors(s, k, 1)
        ps[pl.ds(z // 2, 2)] = pair_sum(s)
        pk[pl.ds(z // 2, 2)] = pair_sum(k)
    down = down_matrix()
    s = dot3(halve_x(ps, 16, x2), down)
    k = dot3(halve_x(pk, 16, x2), down)
    s2[...] = s
    w2[...], c2[...] = factors(s, k, 2)
    sk3[...] = jnp.concatenate([level3_rows(s, e2, r2), level3_rows(k, e2, r2)], axis=0)


def k_down12(own, xl, xr, s1, c1, w1, s2, c2, w2, sk3, g, q, g2, q2, chunk, f, e, x2, e2, r2):
    ix, iy = lax.axis_index("gx"), lax.axis_index("gy")
    for ref in (g, q):
        ref[0] = jnp.zeros((40, 128), F32)
        ref[33] = jnp.zeros((40, 128), F32)

    for z in range(0, 16, 4):
        for i, v in enumerate(opened(own, xl, xr, z, 16, ix, iy)):
            first = z + 8 * (z // 8) + 8 * i
            f[pl.ds(first, 4)] = v
            g[pl.ds(first + 1, 4)] = w1[pl.ds(first, 4)] * v

    def relax(z, at):
        q[at] = 0.4 * g[at] + c1[pl.ds(z - 1, A1)] * near(g, z, A1)

    blocks(1, 32, A1, relax, U1)
    wh, _ = weights(1)

    def residual(z, at):
        own = pl.ds(z - 1, A1)
        v = 0.04 * f[own] + (wh * s1[own]) * near(q, z, A1)
        e[pl.ds((z - 1) // 2, A1 // 2)] = pair_sum(v)

    blocks(1, 32, A1, residual, U1)
    fv = dot3(halve_x(e, 16, x2), down_matrix())
    gv = w2[...] * fv
    zero = jnp.zeros((1, 24, 128), F32)

    def spread(v):
        w = jnp.concatenate([zero, v, zero], axis=0)
        return around(w[:16], v, w[2:])

    qv = 0.4 * gv + c2[...] * spread(gv)
    wh, _ = weights(2)
    ev = 0.04 * fv + (wh * s2[...]) * spread(qv)
    g2[...] = gv
    q2[...] = qv
    parts = [level3_rows(ev, e2, r2), sk3[:4], sk3[4:]]
    parts = [pltpu.roll(part, 16 * iy, 1) for part in parts]

    tiles = [jnp.concatenate([parts[i], parts[(i + 1) % 3]], axis=0) for i in (0, 2, 1)]

    def copy(n, _):
        for i in range(3):
            chunk[3 * n + i] = tiles[i]
        return 0

    lax.fori_loop(0, 32, copy, 0, unroll=8)


def spread_in(shape, last):
    n, r, _ = shape
    row, col = iota(shape, 1), iota(shape, 2)
    zero = jnp.zeros((1,) + shape[1:], F32)

    def apply(v):
        w = jnp.concatenate([zero, v, zero], axis=0)
        x = jnp.where(row > 0, rows(v, 1), 0.0) + jnp.where(row < r - 1, rows(v, -1), 0.0)
        y = jnp.where(col > 0, lanes(v, 1), 0.0) + jnp.where(col < last, lanes(v, -1), 0.0)
        return 0.25 * (w[:n] + w[2:]) + x + y

    return apply


def k_whole(gathered, u, t3, x4, p3):
    ix, iy = lax.axis_index("gx"), lax.axis_index("gy")
    lane = iota((4, 128), 1) // 16
    for j in range(8):
        for n in range(3):
            for x in range(8):
                v = gathered[x * 24 + n]
                for y in range(1, 8):
                    v = jnp.where(lane == (j + y) % 8, gathered[x * 24 + 3 * y + n], v)
                t3[n, j, 4 * x : 4 * x + 4, :] = lanes(v, -16 * j) if j else v
    f3, s3, k3 = t3[0], t3[1], t3[2]
    near3 = spread_in((8, 32, 128), 127)
    w3, c3 = factors(s3, k3, 3)
    g3 = w3 * f3
    q3 = 0.4 * g3 + c3 * near3(g3)
    e3 = 0.04 * f3 + (weights(3)[0] * s3) * near3(q3)
    half = select_matrix((128, 128), lambda i, o: i // 2 == o, 0.125)
    fields = []
    for v in (e3, s3, k3):
        w = v.reshape(4, 2, 32, 128)
        x4[...] = w[:, 0] + w[:, 1]
        fields.append(dot3(x4[:, pl.ds(0, 16, 2), :] + x4[:, pl.ds(1, 16, 2), :], half))
    f4, s4, k4 = fields
    zero4, row4 = jnp.zeros((1, 16, 128), F32), iota((4, 16, 128), 1)

    def near4(v, before, after):
        w = jnp.concatenate([zero4, v, zero4], axis=0)
        x = jnp.where(row4 > 0, rows(v, 1), 0.0) + jnp.where(row4 < 15, rows(v, -1), 0.0)
        return (0.25 * (w[:4] + w[2:]) + x) + (before + after)

    w4, c4 = factors(s4, k4, 4)
    g4 = w4 * f4
    v4 = (0.2 * g4 + g4) + c4 * near4(g4, lanes(g4, 1), lanes(g4, -1))
    g4m, g4p, c4m, c4p = lanes(g4, 1), lanes(g4, -1), lanes(c4, 1), lanes(c4, -1)
    for _ in range(COARSE_SWEEPS // 2):
        vm, vp = lanes(v4, 1), lanes(v4, -1)
        am = (0.2 * vm + g4m) + c4m * near4(vm, lanes(v4, 2), v4)
        ap = (0.2 * vp + g4p) + c4p * near4(vp, v4, lanes(v4, -2))
        a = (0.2 * v4 + g4) + c4 * near4(v4, vm, vp)
        v4 = (0.2 * a + g4) + c4 * near4(a, am, ap)
    u4 = dot3(unscale(v4, s4), select_matrix((128, 128), lambda i, o: i == o // 2))
    p3[:, pl.ds(0, 16, 2), :] = u4
    p3[:, pl.ds(1, 16, 2), :] = u4
    w = p3[...]
    w = jnp.broadcast_to(w[:, None], (4, 2, 32, 128)).reshape(8, 32, 128)
    v3 = (q3 + 0.8 * g3) + s3 * w
    for _ in range(2):
        v3 = (0.2 * v3 + g3) + c3 * near3(v3)
    pick = select_matrix(
        (128, 128),
        lambda i, o: i == (jnp.where(o < 64, o // 2, 127 - (127 - o) // 2) + 16 * iy) % 128,
    )
    u[...] = pltpu.roll(dot3(v3 / s3, pick), (32 - 4 * ix) % 32, 1)


def k_up2(u3, g2, c2, s2, q2, u, p2):
    p2[:, 14:18, :] = jnp.zeros((8, 4, 128), F32)
    for n in range(2):
        p2[:, pl.ds(n, 7, 2), :] = u3[:, 0:7, :]
        p2[:, pl.ds(18 + n, 3, 2), :] = u3[:, 29:32, :]
    w = p2[...]
    w = jnp.broadcast_to(w[:, None], (8, 2, 24, 128)).reshape(16, 24, 128)
    gv, cv, sv = g2[...], c2[...], s2[...]
    zero = jnp.zeros((1, 24, 128), F32)
    v = (q2[...] + 0.8 * gv) + sv * w
    for _ in range(2):
        w = jnp.concatenate([zero, v, zero], axis=0)
        v = (0.2 * v + gv) + cv * around(w[:16], v, w[2:])
    pick = select_matrix(
        (128, 128),
        lambda i, o: i == jnp.where(o < 96, o // 2, 127 - (127 - o) // 2),
    )
    u[...] = dot3(unscale(v, sv), pick)


def k_up1(u2, g1, c1, s1, q1, u, p1, va, vb):
    for n in range(2):
        p1[:, pl.ds(n, 14, 2), :] = u2[:, 0:14, :]
        p1[:, pl.ds(28 + n, 6, 2), :] = u2[:, 18:24, :]
    for ref in (va, vb, u):
        ref[0] = jnp.zeros((40, 128), F32)
        ref[33] = jnp.zeros((40, 128), F32)

    def start(z, at):
        t = p1[pl.ds((z - 1) // 2, A1 // 2)]
        t = jnp.broadcast_to(t[:, None], (A1 // 2, 2, 40, 128)).reshape(A1, 40, 128)
        va[at] = (q1[at] + 0.8 * g1[at]) + s1[pl.ds(z - 1, A1)] * t

    blocks(1, 32, A1, start, U1)

    def sweep(z, at):
        vb[at] = (0.2 * va[at] + g1[at]) + c1[pl.ds(z - 1, A1)] * near(va, z, A1)

    blocks(1, 32, A1, sweep, U1)

    def last(z, at):
        own = pl.ds(z - 1, A1)
        v = (0.2 * vb[at] + g1[at]) + c1[own] * near(vb, z, A1)
        u[at] = unscale(v, s1[own])

    blocks(1, 32, A1, last, U1)


def k_up0(
    u1, gm, cm, sm, q, gw, cw, sw, qw, out, pm, pw, pv, wa, wb, ea, eb, done, sem
):
    iz = lax.axis_index("gz")

    def source(i, o):
        y = jnp.where(o % 16 < 8, 125 + o % 16, o % 16 - 11)
        return i == jnp.where(o < 128, o // 2, ((y + 256) // 2) % 128)

    u = u1[pl.ds(16 * iz, 18)]
    sub = iota((18, 8, 128), 1)
    u = jnp.concatenate([u[:, :16], jnp.where(sub < 4, u[:, 16:24], u[:, 32:40])], axis=1)
    u = dot3(u, select_matrix((128, 256), source))
    for h, ref in enumerate((pm, pw)):
        w = u[:, :, 128 * h : 128 * h + 128]
        for n in range(2):
            ref[:, pl.ds(n, 18, 2), :] = w[:, 0:18]
            ref[:, pl.ds(36 + n, 2, 2), :] = w[:, 22:24]
    pv[...] = lanes(pw[...], 8)
    slot = iota((40, 128), 1) // 8
    parts = []
    for side in range(2):
        for group in range(3):
            total = None
            for j in range(16):
                ref = pw if j % 2 == side else pv
                part = ref[min(max((16 * group + j - 1) // 2, 0), 17)]
                total = part if total is None else jnp.where(slot >= j, part, total)
            parts.append(total[None])
    g, c = gw[...], cw[...]
    v = (qw[...] + 0.8 * g) + sw[...] * jnp.concatenate(parts, axis=0)
    ea[...] = joint(v)
    eb[...] = joint((0.2 * v + g) + c * near_edges(v))

    def start(z, at):
        t = jnp.stack([pm[(z + i - 1) // 2] for i in range(A0)])
        wa[at] = (q[at] + 0.8 * gm[at]) + sm[at] * t

    blocks(1, 36, A0, start, U0)
    wa[0] = jnp.zeros((40, 128), F32)
    wa[37] = jnp.zeros((40, 128), F32)

    def sweep(z, at):
        wb[at] = (0.2 * wa[at] + gm[at]) + cm[at] * near_main(wa, ea, z, A0, True)

    blocks(1, 36, A0, sweep, U0)

    copies = []
    for b in range(32 // B0):
        z = 3 + b * B0
        at = pl.ds(z, B0)
        n = near_main(wb, eb, z, B0)[:, :32]
        v = (0.2 * wb[at, :32, :] + gm[at, :32, :]) + cm[at, :32, :] * n
        part = pl.ds(z - 3, B0)
        done[part] = v / sm[at, :32, :]
        copies.append(pltpu.make_async_copy(done.at[part], out.at[part], sem.at[b]))
        copies[-1].start()
    for copy in copies:
        copy.wait()


def k_up(
    gathered, g2, c2, s2, q2, g1, c1, s1, q1, gm, cm, sm, q0, gw, cw, sw, qw, out,
    u3, t3, x4, p3, u2, p2, u1, p1, va, vb, *rest,
):
    k_whole(gathered, u3, t3, x4, p3)
    k_up2(u3, g2, c2, s2, q2, u2, p2)
    k_up1(u2, g1, c1, s1, q1, u1, p1, va, vb)
    k_up0(u1, gm, cm, sm, q0, gw, cw, sw, qw, out, *rest)


def ring(v, axis, step):
    n = lax.axis_size(axis)
    return lax.ppermute(v, axis, [(i, (i + step) % n) for i in range(n)])


def pair(to_right, to_left, axis):
    return ring(to_right, axis, 1), ring(to_left, axis, -1)


def pack_level1(own):
    n = own.shape[0]
    full, *msg = run(k_pack, (own,), [(n, 16, 128)] + [(-(-n // SLOTS), 16, 128)] * 2)
    return jnp.concatenate([full, *pair(*msg, "gy")], axis=0)


def after(values, *others):
    return lax.optimization_barrier((values, others))[0]


def shards(f, s, k):
    first = jnp.where(lax.axis_index("gz") == 0, 29, 0)
    fz, sz, kz = [lax.dynamic_slice_in_dim(v, first, 3, 0) for v in (f, s, k)]
    sw, c = factors(sz, kz, 0)
    near = (sw * fz, c, jnp.where(kz > 0.0, sz, 0.0))
    zr = ring(run(k_face_z, near, [(7, 32, 128)])[0], "gz", 1)
    g, c, sk1 = run(
        k_load, (f, s, k), [(32, 32, 128)] * 2 + [(16, 16, 128)], [(16, 32, 128)] * 2
    )
    sk1 = after(sk1, zr)
    sk_z = ring(sk1, "gz", 1)
    xs = pair(*run(k_face_x, (g, c, s, zr), [(38, 8, 128)] * 2), "gx")
    small, both = [(3, 40, 128)], [(6, 40, 128)]
    edges = run(k_pack_own, (g, c, s, zr), [(3, 32, 128)] * 3)
    *edges, to_right, to_left = run(k_face_y, (*edges, *xs), small * 5)
    ys = pair(to_right, to_left, "gy")
    gm, cm, sm = run(k_assemble, (g, c, s, zr, *xs), [(38, 40, 128)] * 3)
    sk1, sk_z = after((sk1, sk_z), gm)
    sk_y = pack_level1(jnp.concatenate([sk1, sk_z], axis=0))
    gw, cw, sw, q0, qw, f1 = run(
        k_down0,
        (f, gm, cm, sm, *edges, *ys),
        both * 3 + [(38, 40, 128)] + both + [(8, 16, 128)],
        [(16, 32, 128)] + small * 2,
    )
    sk = after(sk_y, f1)
    f1 = jnp.concatenate([f1, ring(f1, "gz", 1)], axis=0)
    s1, c1, w1, s2, c2, w2, sk3 = run(
        k_coeff,
        (sk, *pair(sk, sk, "gx")),
        [(32, 40, 128)] * 3 + [(16, 24, 128)] * 3 + [(8, 128)],
        [(16, 40, 128)] * 2 + [(16, 24, 128), (8, 8, 128), (32, 128)],
    )
    f1 = pack_level1(f1)
    g1, q1, g2, q2, chunk = run(
        k_down12,
        (f1, *pair(f1, f1, "gx"), s1, c1, w1, s2, c2, w2, sk3),
        [(34, 40, 128)] * 2 + [(16, 24, 128)] * 2 + [(96, 8, 128)],
        [(32, 40, 128), (16, 40, 128), (16, 24, 128), (8, 8, 128), (32, 128)],
    )
    gathered = lax.all_to_all(chunk.reshape(64, 1, 1536), ("gx", "gy"), 0, 0, tiled=True)
    gathered = gathered.reshape(192, 4, 128)
    (out,) = run(
        k_up,
        (gathered, g2, c2, s2, q2, g1, c1, s1, q1, gm, cm, sm, q0, gw, cw, sw, qw),
        [(32, 32, 128)],
        [(8, 32, 128), (3, 8, 32, 128), (4, 32, 128), (4, 32, 128)]
        + [(16, 24, 128), (8, 24, 128)]
        + [(34, 40, 128), (16, 40, 128), (34, 40, 128), (34, 40, 128)]
        + [(18, 40, 128)] * 3 + [(38, 40, 128)] * 2 + small * 2 + [(32, 32, 128)],
        HBM,
        [(32 // B0,)],
    )
    return out


def solution(mesh):
    return jax.shard_map(
        shards,
        mesh=mesh,
        in_specs=(P("gz", "gx", "gy"),) * 3,
        out_specs=P("gz", "gx", "gy"),
        check_vma=False,
    )
```

```python
import math

import jax
import jax.numpy as jnp
from jax import lax
from jax.experimental import pallas as pl
from jax.experimental.pallas import tpu as pltpu
from jax.sharding import PartitionSpec as P

F32 = jnp.float32
VM = pl.BlockSpec(memory_space=pltpu.VMEM)
HBM = pl.BlockSpec(memory_space=pltpu.HBM)
BF16 = jnp.bfloat16
COARSE_SWEEPS = 11
MICROSECONDS = dict(
    k_face_z=0.2,
    k_load=4.0,
    k_face_x=0.2,
    k_pack_own=1.0,
    k_face_y=0.6,
    k_assemble=1.0,
    k_pack=0.3,
    k_down0=2.0,
    k_coeff=2.0,
    k_down12=3.0,
    k_whole=2.0,
    k_up2=0.5,
    k_up1=1.5,
    k_up0=2.5,
)
A0, B0, U0 = 12, 8, 3
A1, U1 = 4, 8
PARTS = ((0, 8), (8, 8), (16, 8), (24, 4), (28, 4))


def run(body, args, outs, scratch=(), out_spec=VM, sems=()):
    words = sum(math.prod(s) for s in (*outs, *scratch)) + sum(a.size for a in args)
    return pl.pallas_call(
        body,
        out_shape=[jax.ShapeDtypeStruct(o, F32) for o in outs],
        in_specs=[VM] * len(args),
        out_specs=[out_spec] * len(outs),
        scratch_shapes=[pltpu.VMEM(s, F32) for s in scratch]
        + [pltpu.SemaphoreType.DMA(n) for n in sems],
        compiler_params=pltpu.CompilerParams(vmem_limit_bytes=6 * words + (6 << 20)),
        cost_estimate=pl.CostEstimate(
            flops=0, transcendentals=0, bytes_accessed=int(3.5e6 * MICROSECONDS[body.__name__])
        ),
    )(*args)


def weights(level):
    wh = 0.25**level
    return wh, 2.0 * (0.25 * wh + 2.0 * wh)


def iota(shape, dim):
    return lax.broadcasted_iota(jnp.int32, shape, dim)


def lanes(v, shift):
    return pltpu.roll(v, shift % v.shape[-1], v.ndim - 1)


def rows(v, shift):
    return pltpu.roll(v, shift % v.shape[-2], v.ndim - 2)


def beside(v):
    return (rows(v, 1) + rows(v, -1)) + (lanes(v, 1) + lanes(v, -1))


def around(above, v, below):
    return 0.25 * (above + below) + beside(v)


def factors(s, k, level):
    wh, full = weights(level)
    diagonal = k + full * (s * s)
    sw = s * (0.8 / jnp.where(diagonal > 0.0, diagonal, 1.0))
    return sw, (wh * s) * sw


def unscale(v, s):
    inside = s > 0.0
    return jnp.where(inside, v / jnp.where(inside, s, 1.0), 0.0)


def dot(a, b):
    b = b.astype(BF16)
    high = a.astype(BF16)
    rest = a - high.astype(F32)
    middle = rest.astype(BF16)
    low = (rest - middle.astype(F32)).astype(BF16)
    terms = [jnp.dot(t, b, preferred_element_type=F32) for t in (high, middle, low)]
    return terms[0] + (terms[1] + terms[2])


def dot3(a, b):
    n, r, c = a.shape
    return dot(a.reshape(n * r, c), b).reshape(n, r, b.shape[1])


def blocks(first, count, size, body, unroll=1):
    def one(b, _):
        z = first + size * b
        body(z, pl.ds(z, size))
        return 0

    lax.fori_loop(0, count // size, one, 0, unroll=unroll)


def pair_sum(v):
    v = v.reshape(v.shape[0] // 2, 2, *v.shape[1:])
    return v[:, 0] + v[:, 1]


def select_matrix(shape, source_of, scale=1.0):
    i, o = iota(shape, 0), iota(shape, 1)
    return jnp.where(source_of(i, o), scale, 0.0).astype(F32)


def k_face_z(g, c, s, zmsg):
    upper = lax.axis_index("gz") == 0
    zmsg[0:3] = g[...]
    zmsg[3:5] = jnp.where(upper, c[1:], c[:2])
    zmsg[5:7] = jnp.where(upper, s[1:], s[:2])


def k_load(f, s, k, g, c, sk1, ps, pk):
    def one(z, at):
        sv, kv = s[at], k[at]
        sw, cv = factors(sv, kv, 0)
        g[at] = sw * f[at]
        c[at] = cv
        ps[pl.ds(z // 2, 2)] = pair_sum(sv)
        pk[pl.ds(z // 2, 2)] = pair_sum(kv)

    blocks(0, 32, 4, one, 2)
    a = ps[:, pl.ds(0, 16, 2), :] + ps[:, pl.ds(1, 16, 2), :]
    b = pk[:, pl.ds(0, 16, 2), :] + pk[:, pl.ds(1, 16, 2), :]
    left = select_matrix((128, 128), lambda i, o: i // 2 == o, 0.125)
    right = select_matrix((128, 128), lambda i, o: i // 2 == o - 64, 0.125)
    sk1[...] = dot3(a, left) + dot3(b, right)


def halo_rows(zr, iz, field, z):
    first, depth = ((0, 3), (3, 2), (5, 2))[field]
    d = z - 35 if z > 34 else 2 - z
    if d >= depth:
        return jnp.zeros(zr.shape[1:], F32)
    row = first + (d if z > 34 else depth - 1 - d)
    return jnp.where(iz == (0 if z > 34 else 1), zr[row], 0.0)


def k_face_x(g, c, s, zr, to_right, to_left):
    iz = lax.axis_index("gz")
    sub = iota((8, 128), 0)

    def put(z, gz, cz, sz):
        a, b, d = gz[24:32], cz[24:32], sz[24:32]
        to_right[z] = jnp.where(sub >= 5, a, jnp.where(sub >= 3, rows(b, -3), rows(d, -5)))
        a, b, d = gz[0:8], cz[0:8], sz[0:8]
        to_left[z] = jnp.where(sub < 3, a, jnp.where(sub < 5, rows(b, 3), rows(d, 5)))

    def one(z, _):
        put(z + 3, g[z], c[z], s[z])
        return 0

    lax.fori_loop(0, 32, one, 0, unroll=4)
    for z in (0, 1, 2, 35, 36, 37):
        put(z, *[halo_rows(zr, iz, n, z) for n in range(3)])


def k_pack_own(g, c, s, zr, *own):
    iz = lax.axis_index("gz")
    slot = iota((32, 128), 1)
    for n, (ref, out) in enumerate(zip((g, c, s), own)):
        for group in range(3):
            total = jnp.zeros((32, 128), F32)
            for j in range(16 if group < 2 else 6):
                z = 16 * group + j
                here = ref[z - 3] if 3 <= z < 35 else halo_rows(zr, iz, n, z)
                total = jnp.where(slot >= 8 * j, lanes(here, 8 * j + 3), total)
            out[group] = total


def side_rows(from_left, from_right, ix, z):
    sub = iota((8, 128), 0)
    lf = jnp.where(ix > 0, from_left[z], 0.0)
    rt = jnp.where(ix < 7, from_right[z], 0.0)
    return (
        jnp.where(sub >= 4, lf, rt),
        jnp.where(sub >= 4, rows(lf, 3), rows(rt, -3)),
        jnp.where(sub >= 4, rows(lf, 5), rows(rt, -5)),
    )


def k_face_y(og, oc, os, from_left, from_right, ag, ac, a_s, to_right, to_left):
    ix = lax.axis_index("gx")
    slot = iota((8, 128), 1)
    lane = iota((40, 128), 1) % 8
    for group in range(3):
        side = [jnp.zeros((8, 128), F32)] * 3
        mid = [ref[group] for ref in (og, oc, os)]
        for j in range(16 if group < 2 else 6):
            here = side_rows(from_left, from_right, ix, 16 * group + j)
            for n in range(3):
                side[n] = jnp.where(slot >= 8 * j, lanes(here[n], 8 * j + 3), side[n])
        g, c, s = [jnp.concatenate(parts, axis=0) for parts in zip(mid, side)]
        ag[group] = g
        ac[group] = c
        a_s[group] = s
        to_right[group] = jnp.where(
            lane < 3, g, jnp.where(lane < 5, lanes(c, 2), lanes(s, 4))
        )
        to_left[group] = jnp.where(
            lane >= 6, lanes(c, 3), jnp.where(lane >= 3, g, lanes(s, -2))
        )


def k_assemble(g, c, s, zr, from_left, from_right, gm, cm, sm):
    ix, iz = lax.axis_index("gx"), lax.axis_index("gz")

    def put(z, values):
        for ref, mid, side in zip(
            (gm, cm, sm), values, side_rows(from_left, from_right, ix, z)
        ):
            ref[z] = jnp.concatenate([mid, side], axis=0)

    def one(z, _):
        put(z + 3, (g[z], c[z], s[z]))
        return 0

    lax.fori_loop(0, 32, one, 0, unroll=4)
    for z in (0, 1, 2, 35, 36, 37):
        put(z, [halo_rows(zr, iz, n, z) for n in range(3)])


def near_edges(v):
    lane = iota(v.shape, 2)
    zero = jnp.zeros((1,) + v.shape[1:], F32)
    up, down = lanes(v, 8), lanes(v, -8)
    above = jnp.where(lane < 8, jnp.concatenate([zero, up[:-1]], axis=0), up)
    below = jnp.where(lane >= 120, jnp.concatenate([down[1:], zero], axis=0), down)
    return around(above, v, below)


def joint(v):
    lane = iota((3,) + v.shape[1:], 2)
    return jnp.where(lane % 8 == 4, lanes(v[3:], 2), v[:3])


def near_main(ref, edge, z, n, product=False):
    v = ref[pl.ds(z, n)]
    lane = iota(v.shape, 2)
    e = jnp.stack(
        [
            pltpu.roll(edge[(z + i) // 16], (124 - 8 * ((z + i) % 16)) % 128, 1)
            for i in range(n)
        ]
    )
    if product:
        across = dot3(v, select_matrix((128, 128), lambda i, o: (i == o + 1) | (i == o - 1)))
        across = jnp.where((lane == 0) | (lane == 127), e + across, across)
    else:
        across = jnp.where(lane == 0, e, lanes(v, 1)) + jnp.where(lane == 127, e, lanes(v, -1))
    above, below = ref[pl.ds(z - 1, n)], ref[pl.ds(z + 1, n)]
    return 0.25 * (above + below) + ((rows(v, 1) + rows(v, -1)) + across)


def near(ref, z, n):
    return around(ref[pl.ds(z - 1, n)], ref[pl.ds(z, n)], ref[pl.ds(z + 1, n)])


def k_down0(
    f, gm, cm, sm, og, oc, os, from_left, from_right, gw, cw, sw, q, qw, f1, e, eg, eq
):
    iy = lax.axis_index("gy")
    own = iota((3, 40, 128), 2) % 8 < 3
    lf = jnp.where(iy > 0, from_left[...], 0.0)
    rt = jnp.where(iy < 7, from_right[...], 0.0)

    def windows(ref, right, left):
        mid = ref[...]
        return jnp.concatenate(
            [jnp.where(own, mid, right), jnp.where(own, left, mid)], axis=0
        )

    g = windows(og, rt, lf)
    c = windows(oc, lanes(rt, -3), lanes(lf, -2))
    gw[...] = g
    cw[...] = c
    sw[...] = windows(os, lanes(rt, 2), lanes(lf, -4))
    w = 0.4 * g + c * near_edges(g)
    qw[...] = w
    eg[...] = joint(g)
    eq[...] = joint(w)
    q[0] = jnp.zeros((40, 128), F32)
    q[37] = jnp.zeros((40, 128), F32)

    def relax(z, at):
        q[at] = 0.4 * gm[at] + cm[at] * near_main(gm, eg, z, A0, True)

    blocks(1, 36, A0, relax, U0)

    def residual(z, at):
        v = 0.04 * f[pl.ds(z - 3, B0)] + sm[at, :32, :] * near_main(q, eq, z, B0, True)[:, :32]
        e[pl.ds((z - 3) // 2, B0 // 2)] = pair_sum(v)

    blocks(3, 32, B0, residual, U0)
    a = e[:, pl.ds(0, 16, 2), :] + e[:, pl.ds(1, 16, 2), :]
    lo = select_matrix((128, 128), lambda i, o: i // 2 == o, 0.125)
    hi = select_matrix((128, 128), lambda i, o: i // 2 == o - 64, 0.125)
    f1[...] = dot3(a[:8], lo) + dot3(a[8:], hi)


SLOTS = 5


def k_pack(own, full, to_right, to_left):
    iz = lax.axis_index("gz")
    lane = iota((16, 128), 1) % 64
    n = own.shape[0]
    for group in range(to_right.shape[0]):
        count = min(SLOTS, n - SLOTS * group)
        a, b, kept = None, None, []
        for j in range(count):
            z = SLOTS * group + j
            own_half = iz == (0 if z < n // 2 else 1)
            v = own[z % (n // 2) + jnp.where(own_half, 0, n // 2)]
            kept.append(v)
            last, first = lanes(v, 12 * j - 52), lanes(v, 12 * j) if j else v
            a = last if a is None else jnp.where(lane >= 12 * j, last, a)
            b = first if b is None else jnp.where(lane >= 12 * j, first, b)
        full[SLOTS * group : SLOTS * group + count] = jnp.stack(kept)
        to_right[group] = a
        to_left[group] = b


def joined(own, xl, xr, at, ix):
    lf = jnp.where(ix > 0, xl[at], 0.0)
    rt = jnp.where(ix < 7, xr[at], 0.0)
    sub = iota((rt.shape[0], 8, 128), 1)
    edge = jnp.where(sub < 4, rt[:, 8:16], lf[:, 0:8])
    return jnp.concatenate([own[at], rt[:, 0:8], edge, lf[:, 8:16]], axis=1)


def opened(own, xl, xr, z, n, ix, iy):
    groups = -(-n // SLOTS)
    mid = joined(own, xl, xr, pl.ds(z, 4), ix)
    need = range(z // SLOTS, (z + 3) // SLOTS + 1)
    lf = [joined(own, xl, xr, pl.ds(n + i, 1), ix)[0] for i in need]
    rt = [joined(own, xl, xr, pl.ds(n + groups + i, 1), ix)[0] for i in need]
    lf = [jnp.where(iy > 0, v, 0.0) for v in lf]
    rt = [jnp.where(iy < 7, v, 0.0) for v in rt]
    at = [((z + i) // SLOTS - need[0], (z + i) % SLOTS) for i in range(4)]
    lf = jnp.stack([lanes(lf[i], 116 - 12 * j) for i, j in at])
    rt = jnp.stack([lanes(rt[i], 64 - 12 * j) for i, j in at])
    lane = iota(mid.shape, 2)
    first = jnp.where(lane < 64, mid, jnp.where(lane < 96, rt, lf))
    second = jnp.where(lane >= 64, mid, jnp.where(lane < 32, rt, lf))
    return first, lanes(second, 64)


def halve_x(ref, n, x2):
    x2[:, 14:18, :] = jnp.zeros((n, 4, 128), F32)
    x2[:, 0:14, :] = ref[:, pl.ds(0, 14, 2), :] + ref[:, pl.ds(1, 14, 2), :]
    x2[:, 18:24, :] = ref[:, pl.ds(28, 6, 2), :] + ref[:, pl.ds(29, 6, 2), :]
    return x2[...]


def down_matrix():
    return select_matrix(
        (128, 128),
        lambda i, o: ((i // 2 == o) & (o < 38)) | ((i // 2 == o - 64) & (o >= 122)),
        0.125,
    )


def level3_rows(v, e2, rows2):
    half = select_matrix((128, 128), lambda i, o: (i // 2 == o) & (o < 16), 0.125)
    e2[...] = pair_sum(v)[:, :8, :]
    for j in range(8):
        rows2[4 * j : 4 * j + 4] = e2[j, pl.ds(0, 4, 2), :] + e2[j, pl.ds(1, 4, 2), :]
    pieces = dot(rows2[...], half)
    total = pieces[0:4]
    for j in range(1, 8):
        total = total + lanes(pieces[4 * j : 4 * j + 4], 16 * j)
    return total


def k_coeff(own, xl, xr, s1, c1, w1, s2, c2, w2, sk3, ps, pk, x2, e2, r2):
    ix, iy = lax.axis_index("gx"), lax.axis_index("gy")

    for z in range(0, 32, 4):
        at = pl.ds(z, 4)
        s, k = opened(own, xl, xr, z, 32, ix, iy)
        s1[at] = s
        w1[at], c1[at] = factors(s, k, 1)
        ps[pl.ds(z // 2, 2)] = pair_sum(s)
        pk[pl.ds(z // 2, 2)] = pair_sum(k)
    down = down_matrix()
    s = dot3(halve_x(ps, 16, x2), down)
    k = dot3(halve_x(pk, 16, x2), down)
    s2[...] = s
    w2[...], c2[...] = factors(s, k, 2)
    sk3[...] = jnp.concatenate([level3_rows(s, e2, r2), level3_rows(k, e2, r2)], axis=0)


def k_down12(own, xl, xr, s1, c1, w1, s2, c2, w2, sk3, g, q, g2, q2, chunk, f, e, x2, e2, r2):
    ix, iy = lax.axis_index("gx"), lax.axis_index("gy")
    for ref in (g, q):
        ref[0] = jnp.zeros((40, 128), F32)
        ref[33] = jnp.zeros((40, 128), F32)

    for z in range(0, 16, 4):
        for i, v in enumerate(opened(own, xl, xr, z, 16, ix, iy)):
            first = z + 8 * (z // 8) + 8 * i
            f[pl.ds(first, 4)] = v
            g[pl.ds(first + 1, 4)] = w1[pl.ds(first, 4)] * v

    def relax(z, at):
        q[at] = 0.4 * g[at] + c1[pl.ds(z - 1, A1)] * near(g, z, A1)

    blocks(1, 32, A1, relax, U1)
    wh, _ = weights(1)

    def residual(z, at):
        own = pl.ds(z - 1, A1)
        v = 0.04 * f[own] + (wh * s1[own]) * near(q, z, A1)
        e[pl.ds((z - 1) // 2, A1 // 2)] = pair_sum(v)

    blocks(1, 32, A1, residual, U1)
    fv = dot3(halve_x(e, 16, x2), down_matrix())
    gv = w2[...] * fv
    zero = jnp.zeros((1, 24, 128), F32)

    def spread(v):
        w = jnp.concatenate([zero, v, zero], axis=0)
        return around(w[:16], v, w[2:])

    qv = 0.4 * gv + c2[...] * spread(gv)
    wh, _ = weights(2)
    ev = 0.04 * fv + (wh * s2[...]) * spread(qv)
    g2[...] = gv
    q2[...] = qv
    parts = [level3_rows(ev, e2, r2), sk3[:4], sk3[4:]]
    parts = [pltpu.roll(part, 16 * iy, 1) for part in parts]

    tiles = [jnp.concatenate([parts[i], parts[(i + 1) % 3]], axis=0) for i in (0, 2, 1)]

    def copy(n, _):
        for i in range(3):
            chunk[3 * n + i] = tiles[i]
        return 0

    lax.fori_loop(0, 32, copy, 0, unroll=8)


def spread_in(shape, last):
    n, r, _ = shape
    row, col = iota(shape, 1), iota(shape, 2)
    zero = jnp.zeros((1,) + shape[1:], F32)

    def apply(v):
        w = jnp.concatenate([zero, v, zero], axis=0)
        x = jnp.where(row > 0, rows(v, 1), 0.0) + jnp.where(row < r - 1, rows(v, -1), 0.0)
        y = jnp.where(col > 0, lanes(v, 1), 0.0) + jnp.where(col < last, lanes(v, -1), 0.0)
        return 0.25 * (w[:n] + w[2:]) + x + y

    return apply


def k_whole(gathered, u, t3, x4, p3):
    ix, iy = lax.axis_index("gx"), lax.axis_index("gy")
    lane = iota((4, 128), 1) // 16
    for j in range(8):
        for n in range(3):
            for x in range(8):
                v = gathered[x * 24 + n]
                for y in range(1, 8):
                    v = jnp.where(lane == (j + y) % 8, gathered[x * 24 + 3 * y + n], v)
                t3[n, j, 4 * x : 4 * x + 4, :] = lanes(v, -16 * j) if j else v
    f3, s3, k3 = t3[0], t3[1], t3[2]
    near3 = spread_in((8, 32, 128), 127)
    w3, c3 = factors(s3, k3, 3)
    g3 = w3 * f3
    q3 = 0.4 * g3 + c3 * near3(g3)
    e3 = 0.04 * f3 + (weights(3)[0] * s3) * near3(q3)
    half = select_matrix((128, 128), lambda i, o: i // 2 == o, 0.125)
    fields = []
    for v in (e3, s3, k3):
        w = v.reshape(4, 2, 32, 128)
        x4[...] = w[:, 0] + w[:, 1]
        fields.append(dot3(x4[:, pl.ds(0, 16, 2), :] + x4[:, pl.ds(1, 16, 2), :], half))
    f4, s4, k4 = fields
    zero4, row4 = jnp.zeros((1, 16, 128), F32), iota((4, 16, 128), 1)

    def near4(v, before, after):
        w = jnp.concatenate([zero4, v, zero4], axis=0)
        x = jnp.where(row4 > 0, rows(v, 1), 0.0) + jnp.where(row4 < 15, rows(v, -1), 0.0)
        return (0.25 * (w[:4] + w[2:]) + x) + (before + after)

    w4, c4 = factors(s4, k4, 4)
    g4 = w4 * f4
    v4 = (0.2 * g4 + g4) + c4 * near4(g4, lanes(g4, 1), lanes(g4, -1))
    g4m, g4p, c4m, c4p = lanes(g4, 1), lanes(g4, -1), lanes(c4, 1), lanes(c4, -1)
    for _ in range(COARSE_SWEEPS // 2):
        vm, vp = lanes(v4, 1), lanes(v4, -1)
        am = (0.2 * vm + g4m) + c4m * near4(vm, lanes(v4, 2), v4)
        ap = (0.2 * vp + g4p) + c4p * near4(vp, v4, lanes(v4, -2))
        a = (0.2 * v4 + g4) + c4 * near4(v4, vm, vp)
        v4 = (0.2 * a + g4) + c4 * near4(a, am, ap)
    u4 = dot3(unscale(v4, s4), select_matrix((128, 128), lambda i, o: i == o // 2))
    p3[:, pl.ds(0, 16, 2), :] = u4
    p3[:, pl.ds(1, 16, 2), :] = u4
    w = p3[...]
    w = jnp.broadcast_to(w[:, None], (4, 2, 32, 128)).reshape(8, 32, 128)
    v3 = (q3 + 0.8 * g3) + s3 * w
    for _ in range(2):
        v3 = (0.2 * v3 + g3) + c3 * near3(v3)
    pick = select_matrix(
        (128, 128),
        lambda i, o: i == (jnp.where(o < 64, o // 2, 127 - (127 - o) // 2) + 16 * iy) % 128,
    )
    u[...] = pltpu.roll(dot3(v3 / s3, pick), (32 - 4 * ix) % 32, 1)


def k_up2(u3, g2, c2, s2, q2, u, p2):
    p2[:, 14:18, :] = jnp.zeros((8, 4, 128), F32)
    for n in range(2):
        p2[:, pl.ds(n, 7, 2), :] = u3[:, 0:7, :]
        p2[:, pl.ds(18 + n, 3, 2), :] = u3[:, 29:32, :]
    w = p2[...]
    w = jnp.broadcast_to(w[:, None], (8, 2, 24, 128)).reshape(16, 24, 128)
    gv, cv, sv = g2[...], c2[...], s2[...]
    zero = jnp.zeros((1, 24, 128), F32)
    v = (q2[...] + 0.8 * gv) + sv * w
    for _ in range(2):
        w = jnp.concatenate([zero, v, zero], axis=0)
        v = (0.2 * v + gv) + cv * around(w[:16], v, w[2:])
    pick = select_matrix(
        (128, 128),
        lambda i, o: i == jnp.where(o < 96, o // 2, 127 - (127 - o) // 2),
    )
    u[...] = dot3(unscale(v, sv), pick)


def k_up1(u2, g1, c1, s1, q1, u, p1, va, vb):
    for n in range(2):
        p1[:, pl.ds(n, 14, 2), :] = u2[:, 0:14, :]
        p1[:, pl.ds(28 + n, 6, 2), :] = u2[:, 18:24, :]
    for ref in (va, vb, u):
        ref[0] = jnp.zeros((40, 128), F32)
        ref[33] = jnp.zeros((40, 128), F32)

    def start(z, at):
        t = p1[pl.ds((z - 1) // 2, A1 // 2)]
        t = jnp.broadcast_to(t[:, None], (A1 // 2, 2, 40, 128)).reshape(A1, 40, 128)
        va[at] = (q1[at] + 0.8 * g1[at]) + s1[pl.ds(z - 1, A1)] * t

    blocks(1, 32, A1, start, U1)

    def sweep(z, at):
        vb[at] = (0.2 * va[at] + g1[at]) + c1[pl.ds(z - 1, A1)] * near(va, z, A1)

    blocks(1, 32, A1, sweep, U1)

    def last(z, at):
        own = pl.ds(z - 1, A1)
        v = (0.2 * vb[at] + g1[at]) + c1[own] * near(vb, z, A1)
        u[at] = unscale(v, s1[own])

    blocks(1, 32, A1, last, U1)


def k_up0(
    u1, gm, cm, sm, q, gw, cw, sw, qw, out, pm, pw, pv, wa, wb, ea, eb, done, sem
):
    iz = lax.axis_index("gz")

    def source(i, o):
        y = jnp.where(o % 16 < 8, 125 + o % 16, o % 16 - 11)
        return i == jnp.where(o < 128, o // 2, ((y + 256) // 2) % 128)

    u = u1[pl.ds(16 * iz, 18)]
    sub = iota((18, 8, 128), 1)
    u = jnp.concatenate([u[:, :16], jnp.where(sub < 4, u[:, 16:24], u[:, 32:40])], axis=1)
    u = dot3(u, select_matrix((128, 256), source))
    for h, ref in enumerate((pm, pw)):
        w = u[:, :, 128 * h : 128 * h + 128]
        for n in range(2):
            ref[:, pl.ds(n, 18, 2), :] = w[:, 0:18]
            ref[:, pl.ds(36 + n, 2, 2), :] = w[:, 22:24]
    pv[...] = lanes(pw[...], 8)
    slot = iota((40, 128), 1) // 8
    parts = []
    for side in range(2):
        for group in range(3):
            total = None
            for j in range(16):
                ref = pw if j % 2 == side else pv
                part = ref[min(max((16 * group + j - 1) // 2, 0), 17)]
                total = part if total is None else jnp.where(slot >= j, part, total)
            parts.append(total[None])
    g, c = gw[...], cw[...]
    v = (qw[...] + 0.8 * g) + sw[...] * jnp.concatenate(parts, axis=0)
    ea[...] = joint(v)
    eb[...] = joint((0.2 * v + g) + c * near_edges(v))

    def start(z, at):
        t = jnp.stack([pm[(z + i - 1) // 2] for i in range(A0)])
        wa[at] = (q[at] + 0.8 * gm[at]) + sm[at] * t

    blocks(1, 36, A0, start, U0)
    wa[0] = jnp.zeros((40, 128), F32)
    wa[37] = jnp.zeros((40, 128), F32)

    def sweep(z, at):
        wb[at] = (0.2 * wa[at] + gm[at]) + cm[at] * near_main(wa, ea, z, A0, True)

    blocks(1, 36, A0, sweep, U0)

    copies = []
    for b, (first, size) in enumerate(PARTS):
        z = 3 + first
        at = pl.ds(z, size)
        n = near_main(wb, eb, z, size)[:, :32]
        v = (0.2 * wb[at, :32, :] + gm[at, :32, :]) + cm[at, :32, :] * n
        part = pl.ds(first, size)
        done[part] = v / sm[at, :32, :]
        copies.append(pltpu.make_async_copy(done.at[part], out.at[part], sem.at[b]))
        copies[-1].start()
    for copy in copies:
        copy.wait()


def ring(v, axis, step):
    n = lax.axis_size(axis)
    return lax.ppermute(v, axis, [(i, (i + step) % n) for i in range(n)])


def pair(to_right, to_left, axis):
    return ring(to_right, axis, 1), ring(to_left, axis, -1)


def pack_level1(own):
    n = own.shape[0]
    full, *msg = run(k_pack, (own,), [(n, 16, 128)] + [(-(-n // SLOTS), 16, 128)] * 2)
    return jnp.concatenate([full, *pair(*msg, "gy")], axis=0)


def after(values, *others):
    return lax.optimization_barrier((values, others))[0]


def shards(f, s, k):
    first = jnp.where(lax.axis_index("gz") == 0, 29, 0)
    fz, sz, kz = [lax.dynamic_slice_in_dim(v, first, 3, 0) for v in (f, s, k)]
    sw, c = factors(sz, kz, 0)
    near = (sw * fz, c, jnp.where(kz > 0.0, sz, 0.0))
    zr = ring(run(k_face_z, near, [(7, 32, 128)])[0], "gz", 1)
    g, c, sk1 = run(
        k_load, (f, s, k), [(32, 32, 128)] * 2 + [(16, 16, 128)], [(16, 32, 128)] * 2
    )
    sk1 = after(sk1, zr)
    sk_z = ring(sk1, "gz", 1)
    xs = pair(*run(k_face_x, (g, c, s, zr), [(38, 8, 128)] * 2), "gx")
    small, both = [(3, 40, 128)], [(6, 40, 128)]
    edges = run(k_pack_own, (g, c, s, zr), [(3, 32, 128)] * 3)
    *edges, to_right, to_left = run(k_face_y, (*edges, *xs), small * 5)
    ys = pair(to_right, to_left, "gy")
    gm, cm, sm = run(k_assemble, (g, c, s, zr, *xs), [(38, 40, 128)] * 3)
    sk1, sk_z = after((sk1, sk_z), gm)
    sk_y = pack_level1(jnp.concatenate([sk1, sk_z], axis=0))
    gw, cw, sw, q0, qw, f1 = run(
        k_down0,
        (f, gm, cm, sm, *edges, *ys),
        both * 3 + [(38, 40, 128)] + both + [(8, 16, 128)],
        [(16, 32, 128)] + small * 2,
    )
    sk = after(sk_y, f1)
    f1 = jnp.concatenate([f1, ring(f1, "gz", 1)], axis=0)
    s1, c1, w1, s2, c2, w2, sk3 = run(
        k_coeff,
        (sk, *pair(sk, sk, "gx")),
        [(32, 40, 128)] * 3 + [(16, 24, 128)] * 3 + [(8, 128)],
        [(16, 40, 128)] * 2 + [(16, 24, 128), (8, 8, 128), (32, 128)],
    )
    f1 = pack_level1(f1)
    g1, q1, g2, q2, chunk = run(
        k_down12,
        (f1, *pair(f1, f1, "gx"), s1, c1, w1, s2, c2, w2, sk3),
        [(34, 40, 128)] * 2 + [(16, 24, 128)] * 2 + [(96, 8, 128)],
        [(32, 40, 128), (16, 40, 128), (16, 24, 128), (8, 8, 128), (32, 128)],
    )
    gathered = lax.all_to_all(chunk.reshape(64, 1, 1536), ("gx", "gy"), 0, 0, tiled=True)
    gathered = gathered.reshape(192, 4, 128)
    (u3,) = run(
        k_whole, (gathered,), [(8, 32, 128)], [(3, 8, 32, 128), (4, 32, 128), (4, 32, 128)]
    )
    (u2,) = run(k_up2, (u3, g2, c2, s2, q2), [(16, 24, 128)], [(8, 24, 128)])
    (u1,) = run(
        k_up1, (u2, g1, c1, s1, q1), [(34, 40, 128)], [(16, 40, 128)] + [(34, 40, 128)] * 2
    )
    (out,) = run(
        k_up0,
        (u1, gm, cm, sm, q0, gw, cw, sw, qw),
        [(32, 32, 128)],
        [(18, 40, 128)] * 3 + [(38, 40, 128)] * 2 + small * 2 + [(32, 32, 128)],
        HBM,
        [(len(PARTS),)],
    )
    return out


def solution(mesh):
    return jax.shard_map(
        shards,
        mesh=mesh,
        in_specs=(P("gz", "gx", "gy"),) * 3,
        out_specs=P("gz", "gx", "gy"),
        check_vma=False,
    )
```
